256 devices in a mesh: gx: 4 (over y), gy: 4 (over z_lo), gz: 16 (over z_hi, x, core).
Axes of the slice: x: 4, y: 4, z: 8 (z_hi: 2, z_lo: 4; z = z_hi * 4 + z_lo), core: 2. Of those that a mesh axis runs over, the one named last changes fastest.
Arguments:
- offsets: float32 [8, 8, 32, 3, 1024], P('gx', 'gy', 'gz'), may hold values from 0 to 1
- probes: bfloat16 [8, 8, 32, 32, 1024], P('gx', 'gy', 'gz'), may hold values from -6 to 6
- counts: int32 [8, 8, 32], P('gx', 'gy', 'gz'), may hold values from 1 to 1024, as said below
- req_box: int32 [4, 4, 16, 64, 2], P('gx', 'gy', 'gz'), may hold values from -1 to 7, as said below
- req_tgt: int32 [4, 4, 16, 64, 2], P('gx', 'gy', 'gz'), may hold values from 0 to 7, as said below
Outputs:
- kv: bfloat16 [8, 8, 32, 32, 1024], P('gx', 'gy', 'gz')
- quad: float32 [32], replicated
The draws below stay inside these ranges and needn't reach their ends.
Inputs may be any that keep to these rules, and one draw needn't show every extreme that they name: `counts`: every device has a box with 1024 points. `req_box`: A local box index of the peer, or -1 for an unused slot; the live slots of a pair come first; a pair whose gy indices and gz indices both differ by less than 2 has no live slot; some pair has all 2 slots live. `req_tgt`: A local box index of the requesting device.
All inputs are finite; a program needn't handle non-finite values.
Results may differ from the reference program's by a relative error of at most 0.0012.
The reference program's roundings to bfloat16 on the way count: a program that leaves them out, or rounds other values in their place, can miss the bound.
Values may be sent and summed in bfloat16 or wider, within the bound.
No kernel may reach another device: no remote copies, remote signals or barrier semaphores. Data moves between devices by JAX's collectives and lax.ppermute only.
A program may use at most 64 MiB of HBM per device.

```python
import math
import jax
import jax.numpy as jnp
from jax import lax

BX = 2
BY = 2
BZ = 2
NB = 1024
R = 32
ORDER = 4
CAP = 2
P_SIZE = 64
BOXES = 8
PEERS = 64
NXB = 8
NYB = 8
NZB = 32
N_GX = 4
N_GY = 4
N_GZ = 16


def draw_counts(key, part):
    key = jax.random.fold_in(key, 11)
    low_key, count_key = jax.random.split(key)
    dev_x = NXB // BX
    dev_y = NYB // BY
    dev_z = NZB // BZ
    lowest = jax.random.randint(low_key, (dev_x, dev_y, dev_z), 1, NB // 2 + 1)
    lowest = jnp.repeat(jnp.repeat(jnp.repeat(lowest, BX, 0), BY, 1), BZ, 2)
    drawn = jax.random.randint(count_key, (NXB, NYB, NZB), lowest, NB + 1)
    corner = (jnp.arange(NXB) % BX == 0)[:, None, None] & (jnp.arange(NYB) % BY == 0)[None, :, None] & (jnp.arange(NZB) % BZ == 0)[None, None, :]
    return jnp.where(corner, NB, drawn).astype(jnp.int32)


def draw_req_box(key, part):
    key = jax.random.fold_in(key, 23)
    load_key, box_key = jax.random.split(key)
    dev_x = NXB // BX
    dev_y = NYB // BY
    dev_z = NZB // BZ
    loads = jax.random.randint(load_key, (dev_x, dev_y, dev_z, PEERS), 0, CAP + 1)
    my_y = jnp.arange(dev_y)[None, :, None, None]
    my_z = jnp.arange(dev_z)[None, None, :, None]
    peer_all = jnp.arange(PEERS)[None, None, None, :]
    peer_y = peer_all // dev_z
    peer_z = peer_all % dev_z
    apart = (jnp.abs(peer_y - my_y) >= 2) | (jnp.abs(peer_z - my_z) >= 2)
    partner = (peer_y == (my_y + 2) % dev_y) & (peer_z == my_z)
    loads = jnp.where(partner, CAP, jnp.where(apart, loads, 0))
    chosen = jax.random.randint(box_key, (dev_x, dev_y, dev_z, PEERS, CAP), 0, BOXES)
    slot_ids = jnp.arange(CAP)
    return jnp.where(slot_ids < loads[..., None], chosen, -1).astype(jnp.int32)


def draw_req_tgt(key, part):
    key = jax.random.fold_in(key, 37)
    shape = (NXB // BX, NYB // BY, NZB // BZ, PEERS, CAP)
    return jax.random.randint(key, shape, 0, BOXES).astype(jnp.int32)


def level_of(stream_key, dims, cuts, smallest, top_value):
    level, own = 1.0, jax.random.fold_in(stream_key, 6)
    for axis_at, parts in cuts:
        steps = jnp.exp(jax.random.uniform(jax.random.fold_in(own, axis_at), (parts,), jnp.float32, smallest / len(cuts), top_value / len(cuts)))
        level = level * jnp.repeat(steps, dims[axis_at] // parts).reshape([-1 if axis == axis_at else 1 for axis in range(len(dims))])
    return level


def centred(own_key, dims, spread, most, cuts=(), held_as=jnp.bfloat16):
    gain = level_of(own_key, dims, cuts, -0.22, 0.18) if cuts else 1.0
    values = jax.random.normal(own_key, dims, jnp.float32) * spread * gain
    return jnp.minimum(jnp.maximum(values, -most), most).astype(held_as)


def setup_inputs(seed: int = 0) -> dict:
    arg_keys = jax.random.split(jax.random.key(seed), 6)
    offsets = jnp.clip(1.0 * jax.random.uniform(arg_keys[0], (NXB, NYB, NZB, 3, NB), jnp.float32) ** level_of(arg_keys[0], (NXB, NYB, NZB, 3, NB), ((0, 4), (1, 4), (2, 16)), -0.2, 0.2), 0.0, 1.0)
    probes = centred(arg_keys[1], (NXB, NYB, NZB, R, NB), 1.0, 6.0, ((0, 4), (1, 4), (2, 16)))
    counts = draw_counts(jax.random.fold_in(arg_keys[5], 71), 0)
    req_box = draw_req_box(jax.random.fold_in(arg_keys[5], 71), 0)
    req_tgt = draw_req_tgt(jax.random.fold_in(arg_keys[5], 71), 0)
    return {"offsets": offsets, "probes": probes, "counts": counts, "req_box": req_box, "req_tgt": req_tgt}


neighbour_shifts = ((0, 0, 0), (1, 0, 0), (-1, 0, 0), (0, 1, 0), (0, -1, 0), (0, 0, 1), (0, 0, -1))

def cheb_nodes():
    counter = jnp.arange(ORDER, dtype=jnp.float32)
    return 0.5 + 0.5 * jnp.cos((2.0 * counter + 1.0) * math.pi / (2.0 * ORDER))

def cheb_terms(unit_pos):
    series = [unit_pos, 2.0 * unit_pos * unit_pos - 1.0]
    for level_num in range(ORDER - 3):
        series.append(2.0 * unit_pos * series[-1] - series[-2])
    return jnp.stack(series[:ORDER - 1])

def axis_weights(coord_row):
    at_points = cheb_terms(2.0 * coord_row - 1.0)
    at_nodes = cheb_terms(2.0 * cheb_nodes() - 1.0)
    return 1.0 / ORDER + 2.0 / ORDER * jnp.dot(at_nodes.T, at_points, precision=lax.Precision.HIGHEST)

def interp_table(point_offsets):
    first_w = axis_weights(point_offsets[0])
    second_w = axis_weights(point_offsets[1])
    third_w = axis_weights(point_offsets[2])
    product = first_w[:, None, None, :] * second_w[None, :, None, :] * third_w[None, None, :, :]
    return product.reshape(ORDER * ORDER * ORDER, point_offsets.shape[-1])

def node_grid():
    node_pos = cheb_nodes()
    full_shape = (ORDER, ORDER, ORDER)
    first_c = jnp.broadcast_to(node_pos[:, None, None], full_shape).reshape(-1)
    second_c = jnp.broadcast_to(node_pos[None, :, None], full_shape).reshape(-1)
    third_c = jnp.broadcast_to(node_pos[None, None, :], full_shape).reshape(-1)
    return jnp.stack([first_c, second_c, third_c])

def translate(delta, picked, target_hot):
    grid_pos = node_grid()
    terms = grid_pos.shape[1]
    squares = jnp.zeros((delta.shape[0], terms, terms), jnp.float32)
    for axis_num in range(3):
        separation = delta[:, axis_num][:, None, None] + grid_pos[axis_num][None, None, :] - grid_pos[axis_num][None, :, None]
        squares = squares + separation * separation
    coupling = lax.rsqrt(1.0 + squares).astype(jnp.bfloat16)
    stacked = picked.reshape(picked.shape[0], terms, -1)
    local_terms = jnp.einsum('sqp,spr->sqr', coupling.astype(jnp.float32), stacked.astype(jnp.float32))
    flat_terms = local_terms.reshape(picked.shape[0], -1)
    return jnp.dot(target_hot, flat_terms, precision=lax.Precision.HIGHEST)

def near_field(ext_offsets, ext_vectors, first_i, second_i, third_i):
    points = ext_offsets.shape[-1]
    probe_count = ext_vectors.shape[-2]
    zero_i = jnp.zeros((), jnp.int32)
    first_i = jnp.asarray(first_i).astype(jnp.int32)
    second_i = jnp.asarray(second_i).astype(jnp.int32)
    third_i = jnp.asarray(third_i).astype(jnp.int32)
    one_i = jnp.ones((), jnp.int32)
    target = lax.dynamic_slice(ext_offsets, (first_i + one_i, second_i + one_i, third_i + one_i, zero_i, zero_i), (1, 1, 1, 3, points))[0, 0, 0]
    accumulated = jnp.zeros((probe_count, points), jnp.float32)
    for neighbour in neighbour_shifts:
        begin = ((first_i + 1 + neighbour[0]).astype(jnp.int32), (second_i + 1 + neighbour[1]).astype(jnp.int32), (third_i + 1 + neighbour[2]).astype(jnp.int32), zero_i, zero_i)
        source = lax.dynamic_slice(ext_offsets, begin, (1, 1, 1, 3, points))[0, 0, 0]
        source_vec = lax.dynamic_slice(ext_vectors, begin, (1, 1, 1, probe_count, points))[0, 0, 0]
        squares = jnp.zeros((points, points), jnp.float32)
        for axis_num in range(3):
            separation = neighbour[axis_num] + source[axis_num][:, None] - target[axis_num][None, :]
            squares = squares + separation * separation
        kernel_tile = lax.rsqrt(1.0 + squares).astype(jnp.bfloat16)
        accumulated = accumulated + jnp.dot(source_vec, kernel_tile, preferred_element_type=jnp.float32)
    return accumulated

def to_blocks(array):
    rest = array.shape[3:]
    split = array.reshape((N_GX, BX, N_GY, BY, N_GZ, BZ) + rest)
    order_list = (0, 2, 4, 1, 3, 5) + tuple(range(6, 6 + len(rest)))
    return jnp.transpose(split, order_list).reshape((N_GX, N_GY, N_GZ, BOXES) + rest)

def from_blocks(array):
    rest = array.shape[4:]
    split = array.reshape((N_GX, N_GY, N_GZ, BX, BY, BZ) + rest)
    order_list = (0, 3, 1, 4, 2, 5) + tuple(range(6, 6 + len(rest)))
    return jnp.transpose(split, order_list).reshape((NXB, NYB, NZB) + rest)

def reference(offsets, probes, counts, req_box, req_tgt):
    points = offsets.shape[-1]
    slot_ids = jnp.arange(points, dtype=jnp.int32)
    live_mask = slot_ids[None, None, None, :] < counts[..., None]
    vectors = jnp.where(live_mask[:, :, :, None, :], probes, jnp.zeros_like(probes))
    widths = ((1, 1), (1, 1), (1, 1), (0, 0), (0, 0))
    ext_offsets = jnp.pad(offsets, widths)
    ext_vectors = jnp.pad(vectors, widths)
    flat_ids = jnp.arange(NXB * NYB * NZB, dtype=jnp.int32)

    def near_one(box_id):
        return near_field(ext_offsets, ext_vectors, box_id // (NYB * NZB), box_id // NZB % NYB, box_id % NZB)
    near = lax.map(near_one, flat_ids).reshape(NXB, NYB, NZB, R, points)
    tables = jax.vmap(interp_table)(offsets.reshape(-1, 3, points)).astype(jnp.bfloat16)
    moments = jnp.einsum('bpn,brn->bpr', tables.astype(jnp.float32), vectors.reshape(-1, R, points).astype(jnp.float32))
    moments = moments.astype(jnp.bfloat16).reshape(NXB, NYB, NZB, P_SIZE * R)
    moment_blocks = to_blocks(moments)
    box_range = jnp.arange(BOXES, dtype=jnp.int32)
    peer_ids = jnp.broadcast_to(jnp.arange(PEERS, dtype=jnp.int32)[:, None], (PEERS, CAP))

    def far_device(device_id):
        first_d = device_id // (N_GY * N_GZ)
        second_d = device_id // N_GZ % N_GY
        third_d = device_id % N_GZ
        asked = req_box[first_d, second_d, third_d]
        wanted = req_tgt[first_d, second_d, third_d]
        slab = moment_blocks[first_d].reshape(PEERS, BOXES, P_SIZE * R)
        picked = slab[peer_ids, jnp.maximum(asked, 0)]
        picked = jnp.where(asked[..., None] >= 0, picked, jnp.zeros_like(picked))
        delta_x = asked // (BY * BZ) - wanted // (BY * BZ)
        delta_y = (peer_ids // N_GZ - second_d) * BY + asked // BZ % BY - wanted // BZ % BY
        delta_z = (peer_ids % N_GZ - third_d) * BZ + asked % BZ - wanted % BZ
        delta = jnp.stack([delta_x, delta_y, delta_z], axis=-1).reshape(-1, 3).astype(jnp.float32)
        target_hot = (wanted.reshape(-1)[None, :] == box_range[:, None]).astype(jnp.float32)
        return translate(delta, picked.reshape(-1, P_SIZE * R), target_hot)
    locals_all = lax.map(far_device, jnp.arange(N_GX * N_GY * N_GZ, dtype=jnp.int32))
    locals_all = locals_all.astype(jnp.bfloat16).reshape(N_GX, N_GY, N_GZ, BOXES, P_SIZE, R)
    table_blocks = to_blocks(tables.reshape(NXB, NYB, NZB, P_SIZE, points))
    far = jnp.einsum('uvwbqr,uvwbqn->uvwbrn', locals_all.astype(jnp.float32), table_blocks.astype(jnp.float32))
    far = from_blocks(far)
    total = (near + far) * (1.0 / math.sqrt(7.0 * points))
    kv = jnp.where(live_mask[:, :, :, None, :], total, 0.0).astype(jnp.bfloat16)
    sums = lax.optimization_barrier(jnp.sum(vectors.astype(jnp.float32) * total, axis=(0, 1, 2, 4)))
    quad = sums / jnp.sum(live_mask.astype(jnp.float32))
    return (kv, quad)
```

```python
import functools
import math

import jax
import jax.numpy as jnp
from jax import lax
from jax.experimental import pallas as pl
from jax.experimental.pallas import tpu as pltpu
from jax.sharding import PartitionSpec as P

ORDER = 4
CHUNK = 128
BOXES = 8
FEATS = 48
ROWS = 48
F32 = jnp.float32
BF16 = jnp.bfloat16
NODES = [math.cos((2.0 * a + 1.0) * math.pi / (2.0 * ORDER)) for a in range(ORDER)]
FACES = ((0, -1), (0, 1), (1, -1), (1, 1), (2, -1), (2, 1))


def box_id(axis, at, first, second):
    place = [0, 0, 0]
    rest = [d for d in range(3) if d != axis]
    place[axis] = at
    place[rest[0]] = first
    place[rest[1]] = second
    return (place[0] * 2 + place[1]) * 2 + place[2]


def face_boxes(axis, at):
    return [box_id(axis, at, i, j) for i in range(2) for j in range(2)]


def split3(value):
    high = value.astype(BF16).astype(F32)
    rest = value - high
    mid = rest.astype(BF16).astype(F32)
    return high, mid, rest - mid


def row_ids(points):
    return lax.broadcasted_iota(jnp.int32, (8, points), 0)


def source_rows(pos, row):
    p1, p2, p3 = split3(pos)
    n1, n2, n3 = split3(1.0 + jnp.sum(pos * pos, axis=0, keepdims=True))
    s1 = jnp.where(row < 3, p1, jnp.where(row == 3, n1, jnp.where(row == 4, n2, jnp.where(row == 5, n3, 1.0))))
    s2 = p2 + pltpu.roll(p3, 3, 0)
    return jnp.concatenate([s1, s1, s2, s2, s1, jnp.zeros_like(s1)], axis=0).astype(BF16)


def target_rows(pos, row):
    p1, p2, p3 = split3(-2.0 * pos)
    m1, m2, m3 = split3(jnp.sum(pos * pos, axis=0, keepdims=True))
    qa = jnp.where(row < 3, p1, jnp.where(row < 6, 1.0, jnp.where(row == 6, m1, m2)))
    qb = jnp.where(row < 3, p2, jnp.where(row == 6, m3, 0.0))
    qc = p1 + pltpu.roll(p1, 3, 0)
    return jnp.concatenate([qa, qb, qc, p2, p3, jnp.zeros_like(qa)], axis=0).astype(BF16)


def prep_kernel(counts, offs, probes, pay, fa, fb, tab, mom, momf, f0, f1, f2, f3, f4, f5, pad):
    points = offs.shape[-1]
    row = row_ids(points)
    lane = lax.broadcasted_iota(jnp.int32, (1, points), 1)
    faces = (f0, f1, f2, f3, f4, f5)
    for k in range(BOXES):
        place = (k // 4, k // 2 % 2, k % 2)
        pad[...] = jnp.zeros_like(pad)
        pad[0:3, :] = offs[k]
        off = pad[...]
        shift = jnp.where(row == 0, place[0] - 1.0, jnp.where(row == 1, place[1] - 1.0, jnp.where(row == 2, place[2] - 1.0, 0.0)))
        pos = off + shift
        src = source_rows(pos, row)
        fa[k] = src
        fb[k] = target_rows(pos, row)
        if k == 0:
            fa[BOXES] = src
        count = counts[k]
        vec = jnp.where(lane < count, probes[k].astype(F32), 0.0).astype(BF16)
        chunks = ((count + CHUNK - 1) // CHUNK).astype(F32)
        p1, p2, p3 = split3(pos)
        rows_a = jnp.where(row == 6, chunks, p1 + pltpu.roll(p2, 3, 0))
        tail = jnp.concatenate([rows_a, p3], axis=0).astype(BF16)
        pay[k, 0:32, :] = vec
        pay[k, 32:48, :] = tail
        for at in range(2):
            for axis in range(3):
                if place[axis] == at:
                    other = [d for d in range(3) if d != axis]
                    out = faces[2 * axis + at]
                    slot = place[other[0]] * 2 + place[other[1]]
                    out[slot, 0:32, :] = vec
                    out[slot, 32:48, :] = tail
        unit = 2.0 * off - 1.0
        t2 = 2.0 * unit * unit - 1.0
        t3 = 2.0 * unit * t2 - unit
        weights = []
        for c in NODES:
            e2 = 2.0 * c * c - 1.0
            e3 = 2.0 * c * e2 - c
            weights.append(0.25 + 0.5 * (c * unit + e2 * t2 + e3 * t3))
        third = jnp.zeros_like(off)
        for d in range(ORDER):
            third = jnp.where(row % 4 == d, weights[d][2:3, :], third)
        seconds = []
        for half in range(2):
            seconds.append(jnp.where(row < 4, weights[2 * half][1:2, :], weights[2 * half + 1][1:2, :]))
        parts = []
        for a in range(ORDER):
            for half in range(2):
                parts.append(weights[a][0:1, :] * seconds[half] * third)
        table = jnp.concatenate(parts, axis=0).astype(BF16)
        tab[k] = table
        moment = lax.dot_general(table, vec, (((1,), (1,)), ((), ())), preferred_element_type=F32)
        momf[:, k * 32:(k + 1) * 32] = moment
    mom[...] = momf[...].astype(BF16)
    pay[BOXES] = jnp.zeros_like(pay[BOXES])


def run_steps(targets, sources_of, chunks_of, dummy, two_way, fa, vec, fb, own, out, tiles, steps, owner):
    at = jnp.int32(0)
    for b in targets:
        for s in sources_of(b):
            count = chunks_of(s)

            def put(c, carry, s=s, b=b, at=at):
                steps[at + c] = s * 8 + c
                owner[(at + c) >> 1] = b
                return carry

            lax.fori_loop(0, count, put, 0)
            at = at + count
        steps[at] = dummy * 8
        at = at + (at & 1)
    for extra in range(6):
        steps[at + extra] = dummy * 8
        owner[(at >> 1) + (extra >> 1)] = targets[0]
    total = at >> 1

    def columns(index):
        return pl.ds(pl.multiple_of((index & 7) * CHUNK, CHUNK), CHUNK)

    def make(t, slot):
        target = fb[owner[t]]
        for h in range(2):
            index = steps[2 * t + h]
            source = fa[index >> 3, :, columns(index)]
            squares = lax.dot_general(source, target, (((0,), (0,)), ((), ())), preferred_element_type=F32)
            tiles[slot, h * CHUNK:(h + 1) * CHUNK, :] = lax.rsqrt(squares).astype(BF16)

    def use(t, slot):
        b = owner[t]
        first = steps[2 * t]
        second = steps[2 * t + 1]
        tile = tiles[slot]
        both = jnp.concatenate([vec[first >> 3, 0:32, columns(first)], vec[second >> 3, 0:32, columns(second)]], axis=1)
        out[b] += jnp.dot(both, tile, preferred_element_type=F32)
        if two_way:
            back = lax.dot_general(own[b, 0:32, :], tile, (((1,), (1,)), ((), ())), preferred_element_type=F32)
            out[first >> 3, :, columns(first)] += back[:, 0:CHUNK]
            out[second >> 3, :, columns(second)] += back[:, CHUNK:]

    make(0, 0)

    def body(k, carry):
        t = 2 * k
        make(t + 1, 1)
        use(t, 0)
        make(t + 2, 0)
        use(t + 1, 1)
        return carry

    lax.fori_loop(0, (total + 1) >> 1, body, 0)


INNER = {4: (0,), 2: (0,), 1: (0,), 6: (2, 4), 5: (1, 4), 3: (1, 2), 7: (3, 5, 6)}


def inner_kernel(targets, sources_of, two_way, counts, fa, pay, fb, acc_in, token, acc, token_out, out, tiles, steps, owner):
    if acc_in is None:
        out[...] = jnp.zeros_like(out)
    else:
        out[0:BOXES] = acc_in[...]
        out[BOXES] = jnp.zeros_like(out[BOXES])
    run_steps(
        targets, sources_of, lambda s: (counts[s] + CHUNK - 1) >> 7, BOXES, two_way,
        fa, pay, fb, pay, out, tiles, steps, owner,
    )
    acc[...] = out[0:BOXES]


def outer_kernel(faces, fb, acc_in, *refs):
    halos = refs[:len(faces)]
    acc, fa, vec, tiles, steps, owner, chunk_no = refs[len(faces):]
    points = fb.shape[-1]
    row = row_ids(points)
    acc[...] = acc_in[...]
    sources = {b: [] for b in range(BOXES)}
    spare = 4 * len(faces)
    for d, (axis, sign) in enumerate(faces):
        halo = halos[d]
        targets = face_boxes(axis, 0 if sign < 0 else 1)
        for i in range(4):
            s = d * 4 + i
            sources[targets[i]].append(s)
            tail = halo[i, 32:48, :].astype(F32)
            rows_a = tail[0:8]
            pos = rows_a + pltpu.roll(rows_a, 5, 0) + tail[8:16]
            pos = jnp.where(row < 3, pos + jnp.where(row == axis, 2.0 * sign, 0.0), 0.0)
            feats = source_rows(pos, row)
            fa[s] = feats
            if s == 0:
                fa[spare] = feats
            vec[s] = halo[i, 0:32, :]
            chunk_no[s] = jnp.max(rows_a[6:7, 0:128]).astype(jnp.int32)
    vec[spare] = jnp.zeros_like(vec[spare])
    order = [b for b in range(BOXES) if sources[b]]
    run_steps(
        order, lambda b: sources[b], lambda s: chunk_no[s], spare, False,
        fa, vec, fb, None, acc, tiles, steps, owner,
    )


def far_kernel(counts, req_box, req_tgt, here, there, near, tab, pay, kv, sums, slab, far_acc, live, sems):
    points = tab.shape[-1]
    first_copy = pltpu.make_async_copy(here, slab.at[pl.ds(0, 32)], sems.at[0])
    second_copy = pltpu.make_async_copy(there, slab.at[pl.ds(32, 32)], sems.at[1])
    first_copy.start()
    second_copy.start()
    my_y = lax.axis_index("gy")
    my_z = lax.axis_index("gz")
    far_acc[...] = jnp.zeros_like(far_acc)

    def keep(i, n):
        live[n] = i
        return n + (req_box[i] >= 0).astype(jnp.int32)

    used = lax.fori_loop(0, 128, keep, jnp.int32(0))
    shape = (64, 64)
    source_q = lax.broadcasted_iota(jnp.int32, shape, 1)
    target_q = lax.broadcasted_iota(jnp.int32, shape, 0)

    def node(index):
        value = jnp.full(shape, 0.5 + 0.5 * NODES[0], F32)
        for a in range(1, ORDER):
            value = jnp.where(index == a, 0.5 + 0.5 * NODES[a], value)
        return value

    gaps = [node((source_q >> s) & 3) - node((target_q >> s) & 3) for s in (4, 2, 0)]
    group = lax.broadcasted_iota(jnp.int32, (64, 256), 1) >> 5
    first_copy.wait()
    second_copy.wait()

    def step(g, carry):
        for u in range(4):
            k = g * 4 + u
            i = live[jnp.minimum(k, used - 1)]
            box = req_box[i]
            tgt = req_tgt[i]
            peer = i >> 1
            peer_y = peer >> 4
            peer_z = peer & 15
            dx = (box >> 2) - (tgt >> 2)
            dy = (peer_y - my_y) * 2 + ((box >> 1) & 1) - ((tgt >> 1) & 1)
            dz = (peer_z - my_z) * 2 + (box & 1) - (tgt & 1)
            ex = gaps[0] + dx.astype(F32)
            ey = gaps[1] + dy.astype(F32)
            ez = gaps[2] + dz.astype(F32)
            coupling = lax.rsqrt(1.0 + ex * ex + ey * ey + ez * ez).astype(BF16)
            rel_y = peer_y ^ my_y
            rel_z = peer_z ^ my_z
            at = (rel_z & 1) * 32 + ((rel_z >> 1) & 3) * 8 + rel_y * 2 + (rel_z >> 3)
            term = jnp.dot(coupling, slab[at], preferred_element_type=F32)
            wanted = jnp.where(k < used, box, -1)
            far_acc[tgt] += jnp.where(group == wanted, term, 0.0)
        return carry

    lax.fori_loop(0, (used + 3) >> 2, step, 0)
    lane = lax.broadcasted_iota(jnp.int32, (1, points), 1)
    total_sum = jnp.zeros((32, 128), F32)
    live_points = jnp.int32(0)
    for b in range(BOXES):
        wide = far_acc[b]
        half = wide[:, 0:128] + wide[:, 128:256]
        half = half + pltpu.roll(half, 64, 1)
        half = half + pltpu.roll(half, 32, 1)
        local_exp = half[:, 0:32].astype(BF16)
        far = lax.dot_general(local_exp, tab[b], (((0,), (0,)), ((), ())), preferred_element_type=F32)
        total = (near[b] + far) * (1.0 / math.sqrt(7.0 * points))
        kv[b] = jnp.where(lane < counts[b], total, 0.0).astype(BF16)
        weighted = pay[b, 0:32, :].astype(F32) * total
        for j in range(points // 128):
            total_sum = total_sum + weighted[:, j * 128:(j + 1) * 128]
        live_points = live_points + counts[b]
    lane128 = lax.broadcasted_iota(jnp.int32, (32, 128), 1)
    sums[...] = jnp.where(lane128 == 0, jnp.sum(total_sum, axis=1, keepdims=True), live_points.astype(F32))


VMEM = pl.BlockSpec(memory_space=pltpu.VMEM)
SMEM = pl.BlockSpec(memory_space=pltpu.SMEM)
ANY = pl.BlockSpec(memory_space=pl.ANY)
PARAMS = pltpu.CompilerParams(vmem_limit_bytes=48 * 2**20)


def xor_permute(value, axis, bits):
    count = lax.axis_size(axis)
    return lax.ppermute(value, axis, [(i, i ^ bits) for i in range(count)])


def shards(offsets, probes, counts, req_box, req_tgt):
    points = offsets.shape[-1]
    offs = offsets.reshape(BOXES, 3, points)
    probe = probes.reshape(BOXES, 32, points)
    count = counts.reshape(BOXES)
    shape = jax.ShapeDtypeStruct
    face = shape((4, ROWS, points), BF16)
    pay, fa, fb, tab, mom, momf, *faces = pl.pallas_call(
        prep_kernel,
        out_shape=[
            shape((BOXES + 1, ROWS, points), BF16),
            shape((BOXES + 1, FEATS, points), BF16),
            shape((BOXES, FEATS, points), BF16),
            shape((BOXES, 64, points), BF16),
            shape((64, 256), BF16),
            shape((64, 256), F32),
        ] + [face] * 6,
        in_specs=[SMEM, VMEM, VMEM],
        out_specs=[VMEM] * 12,
        scratch_shapes=[pltpu.VMEM((8, points), F32)],
        compiler_params=PARAMS,
        name="prep",
    )(count, offs, probe)

    acc_shape = shape((BOXES, 32, points), F32)

    def inner(name, targets, sources_of, two_way, acc, token):
        has_acc = acc is not None
        tokens = [token]

        def kernel(*refs):
            refs = list(refs)
            head = refs[:4]
            rest = refs[4:]
            acc_ref = rest.pop(0) if has_acc else None
            inner_kernel(targets, sources_of, two_way, *head, acc_ref, *rest)

        args = [count, fa, pay, fb] + ([acc] if has_acc else []) + tokens
        return pl.pallas_call(
            kernel,
            out_shape=[acc_shape, shape(token.shape, token.dtype)],
            in_specs=[SMEM, VMEM, VMEM, VMEM] + [VMEM] * has_acc + [ANY],
            out_specs=[VMEM, ANY],
            input_output_aliases={len(args) - 1: 1},
            scratch_shapes=[
                pltpu.VMEM((BOXES + 1, 32, points), F32),
                pltpu.VMEM((2, 2 * CHUNK, points), BF16),
                pltpu.SMEM((256,), jnp.int32),
                pltpu.SMEM((128,), jnp.int32),
            ],
            compiler_params=PARAMS,
            name=name,
        )(*args)

    got = []
    for (axis, sign) in FACES:
        name = ("gx", "gy", "gz")[axis]
        size = lax.axis_size(name)
        if sign < 0:
            pairs = [(i, i + 1) for i in range(size - 1)]
            got.append(lax.ppermute(faces[2 * axis + 1], name, pairs))
        else:
            pairs = [(i + 1, i) for i in range(size - 1)]
            got.append(lax.ppermute(faces[2 * axis], name, pairs))

    block = mom.reshape(1, 64, 256)
    block = jnp.concatenate([block, xor_permute(block, "gz", 8)], axis=0)
    acc, block = inner("self_tiles", list(range(BOXES)), lambda b: [b], False, None, block)
    block = jnp.concatenate([block] + [xor_permute(block, "gy", k) for k in (1, 2, 3)], axis=0)
    acc, block = inner("pairs_low", [1, 2, 4, 3], lambda b: INNER[b], True, acc, block)
    block = jnp.concatenate([block] + [xor_permute(block, "gz", 2 * k) for k in (1, 2, 3)], axis=0)
    acc, block = inner("pairs_high", [5, 6, 7], lambda b: INNER[b], True, acc, block)
    other = xor_permute(block, "gz", 1)

    def outer(name, which, acc):
        nsrc = 4 * len(which) + 1
        return pl.pallas_call(
            functools.partial(outer_kernel, [FACES[d] for d in which]),
            out_shape=acc_shape,
            in_specs=[VMEM] * (2 + len(which)),
            out_specs=VMEM,
            scratch_shapes=[
                pltpu.VMEM((nsrc, FEATS, points), BF16),
                pltpu.VMEM((nsrc, 32, points), BF16),
                pltpu.VMEM((2, 2 * CHUNK, points), BF16),
                pltpu.SMEM((256,), jnp.int32),
                pltpu.SMEM((128,), jnp.int32),
                pltpu.SMEM((32,), jnp.int32),
            ],
            compiler_params=PARAMS,
            name=name,
        )(fb, acc, *[got[d] for d in which])

    acc = outer("face_tiles", [0, 1, 2, 3, 4, 5], acc)
    kv, sums = pl.pallas_call(
        far_kernel,
        out_shape=[shape((BOXES, 32, points), BF16), shape((32, 128), F32)],
        in_specs=[SMEM, SMEM, SMEM, ANY, ANY, VMEM, VMEM, VMEM],
        out_specs=[VMEM, VMEM],
        scratch_shapes=[
            pltpu.VMEM((64, 64, 256), BF16),
            pltpu.VMEM((BOXES, 64, 256), F32),
            pltpu.SMEM((136,), jnp.int32),
            pltpu.SemaphoreType.DMA((2,)),
        ],
        compiler_params=PARAMS,
        name="far_total",
    )(count, req_box.reshape(128), req_tgt.reshape(128), block, other, acc, tab, pay)
    for axis, bits in (("gx", (1, 2)), ("gy", (1, 2)), ("gz", (1, 2, 4, 8))):
        for bit in bits:
            sums = sums + xor_permute(sums, axis, bit)
    quad = sums[:, 0] / sums[:, 1]
    return kv.reshape(probes.shape), quad


def solution(mesh):
    placed = (
        P("gx", "gy", "gz", None, None),
        P("gx", "gy", "gz", None, None),
        P("gx", "gy", "gz"),
        P("gx", "gy", "gz", None, None),
        P("gx", "gy", "gz", None, None),
    )
    return jax.shard_map(
        shards,
        mesh=mesh,
        in_specs=placed,
        out_specs=(P("gx", "gy", "gz", None, None), P()),
        check_vma=False,
    )
```

```python
import functools
import math

import jax
import jax.numpy as jnp
from jax import lax
from jax.experimental import pallas as pl
from jax.experimental.pallas import tpu as pltpu
from jax.sharding import PartitionSpec as P

ORDER = 4
CHUNK = 128
BOXES = 8
FEATS = 48
ROWS = 48
F32 = jnp.float32
BF16 = jnp.bfloat16
NODES = [math.cos((2.0 * a + 1.0) * math.pi / (2.0 * ORDER)) for a in range(ORDER)]
FACES = ((0, -1), (0, 1), (1, -1), (1, 1), (2, -1), (2, 1))


def box_id(axis, at, first, second):
    place = [0, 0, 0]
    rest = [d for d in range(3) if d != axis]
    place[axis] = at
    place[rest[0]] = first
    place[rest[1]] = second
    return (place[0] * 2 + place[1]) * 2 + place[2]


def face_boxes(axis, at):
    return [box_id(axis, at, i, j) for i in range(2) for j in range(2)]


def split3(value):
    high = value.astype(BF16).astype(F32)
    rest = value - high
    mid = rest.astype(BF16).astype(F32)
    return high, mid, rest - mid


def row_ids(points):
    return lax.broadcasted_iota(jnp.int32, (8, points), 0)


def source_rows(pos, row):
    p1, p2, p3 = split3(pos)
    n1, n2, n3 = split3(1.0 + jnp.sum(pos * pos, axis=0, keepdims=True))
    s1 = jnp.where(row < 3, p1, jnp.where(row == 3, n1, jnp.where(row == 4, n2, jnp.where(row == 5, n3, 1.0))))
    s2 = p2 + pltpu.roll(p3, 3, 0)
    return jnp.concatenate([s1, s1, s2, s2, s1, jnp.zeros_like(s1)], axis=0).astype(BF16)


def target_rows(pos, row):
    p1, p2, p3 = split3(-2.0 * pos)
    m1, m2, m3 = split3(jnp.sum(pos * pos, axis=0, keepdims=True))
    qa = jnp.where(row < 3, p1, jnp.where(row < 6, 1.0, jnp.where(row == 6, m1, m2)))
    qb = jnp.where(row < 3, p2, jnp.where(row == 6, m3, 0.0))
    qc = p1 + pltpu.roll(p1, 3, 0)
    return jnp.concatenate([qa, qb, qc, p2, p3, jnp.zeros_like(qa)], axis=0).astype(BF16)


def prep_kernel(counts, offs, probes, pay, fa, fb, tab, mom, momf, f0, f1, f2, f3, f4, f5, pad):
    points = offs.shape[-1]
    row = row_ids(points)
    lane = lax.broadcasted_iota(jnp.int32, (1, points), 1)
    faces = (f0, f1, f2, f3, f4, f5)
    for k in range(BOXES):
        place = (k // 4, k // 2 % 2, k % 2)
        pad[...] = jnp.zeros_like(pad)
        pad[0:3, :] = offs[k]
        off = pad[...]
        shift = jnp.where(row == 0, place[0] - 1.0, jnp.where(row == 1, place[1] - 1.0, jnp.where(row == 2, place[2] - 1.0, 0.0)))
        pos = off + shift
        src = source_rows(pos, row)
        fa[k] = src
        fb[k] = target_rows(pos, row)
        if k == 0:
            fa[BOXES] = src
        count = counts[k]
        vec = jnp.where(lane < count, probes[k].astype(F32), 0.0).astype(BF16)
        chunks = ((count + CHUNK - 1) // CHUNK).astype(F32)
        p1, p2, p3 = split3(pos)
        rows_a = jnp.where(row == 6, chunks, p1 + pltpu.roll(p2, 3, 0))
        tail = jnp.concatenate([rows_a, p3], axis=0).astype(BF16)
        pay[k, 0:32, :] = vec
        pay[k, 32:48, :] = tail
        for at in range(2):
            for axis in range(3):
                if place[axis] == at:
                    other = [d for d in range(3) if d != axis]
                    out = faces[2 * axis + at]
                    slot = place[other[0]] * 2 + place[other[1]]
                    out[slot, 0:32, :] = vec
                    out[slot, 32:48, :] = tail
        unit = 2.0 * off - 1.0
        t2 = 2.0 * unit * unit - 1.0
        t3 = 2.0 * unit * t2 - unit
        weights = []
        for c in NODES:
            e2 = 2.0 * c * c - 1.0
            e3 = 2.0 * c * e2 - c
            weights.append(0.25 + 0.5 * (c * unit + e2 * t2 + e3 * t3))
        third = jnp.zeros_like(off)
        for d in range(ORDER):
            third = jnp.where(row % 4 == d, weights[d][2:3, :], third)
        seconds = []
        for half in range(2):
            seconds.append(jnp.where(row < 4, weights[2 * half][1:2, :], weights[2 * half + 1][1:2, :]))
        parts = []
        for a in range(ORDER):
            for half in range(2):
                parts.append(weights[a][0:1, :] * seconds[half] * third)
        table = jnp.concatenate(parts, axis=0).astype(BF16)
        tab[k] = table
        moment = lax.dot_general(table, vec, (((1,), (1,)), ((), ())), preferred_element_type=F32)
        momf[:, k * 32:(k + 1) * 32] = moment
    mom[...] = momf[...].astype(BF16)
    pay[BOXES] = jnp.zeros_like(pay[BOXES])


def run_steps(targets, sources_of, chunks_of, dummy, two_way, fa, vec, fb, own, out, tiles, steps, owner):
    at = jnp.int32(0)
    for b in targets:
        for s in sources_of(b):
            count = chunks_of(s)

            def put(c, carry, s=s, b=b, at=at):
                steps[at + c] = s * 8 + c
                owner[(at + c) >> 1] = b
                return carry

            lax.fori_loop(0, count, put, 0)
            at = at + count
        steps[at] = dummy * 8
        at = at + (at & 1)
    for extra in range(6):
        steps[at + extra] = dummy * 8
        owner[(at >> 1) + (extra >> 1)] = targets[0]
    total = at >> 1

    def columns(index):
        return pl.ds(pl.multiple_of((index & 7) * CHUNK, CHUNK), CHUNK)

    def make(t, slot):
        target = fb[owner[t]]
        for h in range(2):
            index = steps[2 * t + h]
            source = fa[index >> 3, :, columns(index)]
            squares = lax.dot_general(source, target, (((0,), (0,)), ((), ())), preferred_element_type=F32)
            tiles[slot, h * CHUNK:(h + 1) * CHUNK, :] = lax.rsqrt(squares).astype(BF16)

    def use(t, slot):
        b = owner[t]
        first = steps[2 * t]
        second = steps[2 * t + 1]
        tile = tiles[slot]
        both = jnp.concatenate([vec[first >> 3, 0:32, columns(first)], vec[second >> 3, 0:32, columns(second)]], axis=1)
        out[b] += jnp.dot(both, tile, preferred_element_type=F32)
        if two_way:
            back = lax.dot_general(own[b, 0:32, :], tile, (((1,), (1,)), ((), ())), preferred_element_type=F32)
            out[first >> 3, :, columns(first)] += back[:, 0:CHUNK]
            out[second >> 3, :, columns(second)] += back[:, CHUNK:]

    make(0, 0)

    def body(k, carry):
        t = 2 * k
        make(t + 1, 1)
        use(t, 0)
        make(t + 2, 0)
        use(t + 1, 1)
        return carry

    lax.fori_loop(0, (total + 1) >> 1, body, 0)


INNER = {4: (0,), 2: (0,), 1: (0,), 6: (2, 4), 5: (1, 4), 3: (1, 2), 7: (3, 5, 6)}


def inner_kernel(targets, sources_of, two_way, counts, fa, pay, fb, acc_in, after, acc, done, out, tiles, steps, owner):
    if acc_in is None:
        out[...] = jnp.zeros_like(out)
    else:
        out[0:BOXES] = acc_in[...]
        out[BOXES] = jnp.zeros_like(out[BOXES])
    run_steps(
        targets, sources_of, lambda s: (counts[s] + CHUNK - 1) >> 7, BOXES, two_way,
        fa, pay, fb, pay, out, tiles, steps, owner,
    )
    acc[...] = out[0:BOXES]
    done[...] = jnp.zeros_like(done)


def outer_kernel(faces, fb, acc_in, after, *refs):
    halos = refs[:len(faces)]
    acc, fa, vec, tiles, steps, owner, chunk_no = refs[len(faces):]
    points = fb.shape[-1]
    row = row_ids(points)
    acc[...] = acc_in[...]
    sources = {b: [] for b in range(BOXES)}
    spare = 4 * len(faces)
    for d, (axis, sign) in enumerate(faces):
        halo = halos[d]
        targets = face_boxes(axis, 0 if sign < 0 else 1)
        for i in range(4):
            s = d * 4 + i
            sources[targets[i]].append(s)
            tail = halo[i, 32:48, :].astype(F32)
            rows_a = tail[0:8]
            pos = rows_a + pltpu.roll(rows_a, 5, 0) + tail[8:16]
            pos = jnp.where(row < 3, pos + jnp.where(row == axis, 2.0 * sign, 0.0), 0.0)
            feats = source_rows(pos, row)
            fa[s] = feats
            if s == 0:
                fa[spare] = feats
            vec[s] = halo[i, 0:32, :]
            chunk_no[s] = jnp.max(rows_a[6:7, 0:128]).astype(jnp.int32)
    vec[spare] = jnp.zeros_like(vec[spare])
    order = [b for b in range(BOXES) if sources[b]]
    run_steps(
        order, lambda b: sources[b], lambda s: chunk_no[s], spare, False,
        fa, vec, fb, None, acc, tiles, steps, owner,
    )


def far_kernel(counts, req_box, req_tgt, here, there, near, tab, pay, kv, sums, slab, far_acc, live, sems):
    points = tab.shape[-1]
    first_copy = pltpu.make_async_copy(here, slab.at[pl.ds(0, 32)], sems.at[0])
    second_copy = pltpu.make_async_copy(there, slab.at[pl.ds(32, 32)], sems.at[1])
    first_copy.start()
    second_copy.start()
    my_y = lax.axis_index("gy")
    my_z = lax.axis_index("gz")
    far_acc[...] = jnp.zeros_like(far_acc)

    def keep(i, n):
        live[n] = i
        return n + (req_box[i] >= 0).astype(jnp.int32)

    used = lax.fori_loop(0, 128, keep, jnp.int32(0))
    shape = (64, 64)
    source_q = lax.broadcasted_iota(jnp.int32, shape, 1)
    target_q = lax.broadcasted_iota(jnp.int32, shape, 0)

    def node(index):
        value = jnp.full(shape, 0.5 + 0.5 * NODES[0], F32)
        for a in range(1, ORDER):
            value = jnp.where(index == a, 0.5 + 0.5 * NODES[a], value)
        return value

    gaps = [node((source_q >> s) & 3) - node((target_q >> s) & 3) for s in (4, 2, 0)]
    group = lax.broadcasted_iota(jnp.int32, (64, 256), 1) >> 5
    first_copy.wait()
    second_copy.wait()

    def step(g, carry):
        for u in range(4):
            k = g * 4 + u
            i = live[jnp.minimum(k, used - 1)]
            box = req_box[i]
            tgt = req_tgt[i]
            peer = i >> 1
            peer_y = peer >> 4
            peer_z = peer & 15
            dx = (box >> 2) - (tgt >> 2)
            dy = (peer_y - my_y) * 2 + ((box >> 1) & 1) - ((tgt >> 1) & 1)
            dz = (peer_z - my_z) * 2 + (box & 1) - (tgt & 1)
            ex = gaps[0] + dx.astype(F32)
            ey = gaps[1] + dy.astype(F32)
            ez = gaps[2] + dz.astype(F32)
            coupling = lax.rsqrt(1.0 + ex * ex + ey * ey + ez * ez).astype(BF16)
            rel_y = peer_y ^ my_y
            rel_z = peer_z ^ my_z
            at = (rel_z & 1) * 32 + ((rel_z >> 1) & 3) * 8 + rel_y * 2 + (rel_z >> 3)
            term = jnp.dot(coupling, slab[at], preferred_element_type=F32)
            wanted = jnp.where(k < used, box, -1)
            far_acc[tgt] += jnp.where(group == wanted, term, 0.0)
        return carry

    lax.fori_loop(0, (used + 3) >> 2, step, 0)
    lane = lax.broadcasted_iota(jnp.int32, (1, points), 1)
    total_sum = jnp.zeros((32, 128), F32)
    live_points = jnp.int32(0)
    for b in range(BOXES):
        wide = far_acc[b]
        half = wide[:, 0:128] + wide[:, 128:256]
        half = half + pltpu.roll(half, 64, 1)
        half = half + pltpu.roll(half, 32, 1)
        local_exp = half[:, 0:32].astype(BF16)
        far = lax.dot_general(local_exp, tab[b], (((0,), (0,)), ((), ())), preferred_element_type=F32)
        total = (near[b] + far) * (1.0 / math.sqrt(7.0 * points))
        kv[b] = jnp.where(lane < counts[b], total, 0.0).astype(BF16)
        weighted = pay[b, 0:32, :].astype(F32) * total
        for j in range(points // 128):
            total_sum = total_sum + weighted[:, j * 128:(j + 1) * 128]
        live_points = live_points + counts[b]
    lane128 = lax.broadcasted_iota(jnp.int32, (32, 128), 1)
    row128 = lax.broadcasted_iota(jnp.int32, (32, 128), 0)
    spread = jnp.where(lane128 == row128, jnp.sum(total_sum, axis=1, keepdims=True), 0.0)
    flat = jnp.sum(spread, axis=0, keepdims=True)
    sums[...] = jnp.where(lane128[0:1] == 32, live_points.astype(F32), flat)


VMEM = pl.BlockSpec(memory_space=pltpu.VMEM)
SMEM = pl.BlockSpec(memory_space=pltpu.SMEM)
ANY = pl.BlockSpec(memory_space=pl.ANY)
PARAMS = pltpu.CompilerParams(vmem_limit_bytes=20 * 2**20)


COST = pl.CostEstimate(flops=12 * 10**9, bytes_accessed=4 * 2**20, transcendentals=10**7)


def join(name, *arrays):
    return pl.pallas_call(
        lambda *refs: None,
        out_shape=[jax.ShapeDtypeStruct(a.shape, a.dtype) for a in arrays],
        in_specs=[ANY] * len(arrays),
        out_specs=[ANY] * len(arrays),
        input_output_aliases={i: i for i in range(len(arrays))},
        compiler_params=pltpu.CompilerParams(vmem_limit_bytes=2**20),
        name=name,
    )(*arrays)


def xor_permute(value, axis, bits):
    count = lax.axis_size(axis)
    return lax.ppermute(value, axis, [(i, i ^ bits) for i in range(count)])


def shards(offsets, probes, counts, req_box, req_tgt):
    points = offsets.shape[-1]
    offs = offsets.reshape(BOXES, 3, points)
    probe = probes.reshape(BOXES, 32, points)
    count = counts.reshape(BOXES)
    shape = jax.ShapeDtypeStruct
    face = shape((4, ROWS, points), BF16)
    pay, fa, fb, tab, mom, momf, *faces = pl.pallas_call(
        prep_kernel,
        out_shape=[
            shape((BOXES + 1, ROWS, points), BF16),
            shape((BOXES + 1, FEATS, points), BF16),
            shape((BOXES, FEATS, points), BF16),
            shape((BOXES, 64, points), BF16),
            shape((64, 256), BF16),
            shape((64, 256), F32),
        ] + [face] * 6,
        in_specs=[SMEM, VMEM, VMEM],
        out_specs=[VMEM] * 12,
        scratch_shapes=[pltpu.VMEM((8, points), F32)],
        compiler_params=PARAMS,
        name="prep",
    )(count, offs, probe)

    acc_shape = shape((BOXES, 32, points), F32)

    def inner(name, targets, sources_of, two_way, acc, after):
        has_acc = acc is not None

        def kernel(*refs):
            refs = list(refs)
            head = refs[:4]
            rest = refs[4:]
            acc_ref = rest.pop(0) if has_acc else None
            inner_kernel(targets, sources_of, two_way, *head, acc_ref, *rest)

        args = [count, fa, pay, fb] + ([acc] if has_acc else []) + [after]
        return pl.pallas_call(
            kernel,
            out_shape=[acc_shape, shape((8, 128), F32)],
            in_specs=[SMEM, VMEM, VMEM, VMEM] + [VMEM] * has_acc + [ANY],
            out_specs=[VMEM, VMEM],
            scratch_shapes=[
                pltpu.VMEM((BOXES + 1, 32, points), F32),
                pltpu.VMEM((2, 2 * CHUNK, points), BF16),
                pltpu.SMEM((256,), jnp.int32),
                pltpu.SMEM((128,), jnp.int32),
            ],
            compiler_params=PARAMS,
            cost_estimate=COST,
            name=name,
        )(*args)

    def halo(d):
        axis, sign = FACES[d]
        name = ("gx", "gy", "gz")[axis]
        size = lax.axis_size(name)
        if sign < 0:
            return lax.ppermute(faces[2 * axis + 1], name, [(i, i + 1) for i in range(size - 1)])
        return lax.ppermute(faces[2 * axis], name, [(i + 1, i) for i in range(size - 1)])

    got = [None] * 6
    block = mom.reshape(1, 64, 256)
    twin = xor_permute(block, "gz", 8)
    got[0], got[1] = halo(0), halo(1)
    acc, tick = inner("self_tiles", list(range(BOXES)), lambda b: [b], False, None, mom)
    tick, twin, got[0], got[1] = join("join_first", tick, twin, got[0], got[1])
    block = jnp.concatenate([block, twin], axis=0)
    more = [xor_permute(block, "gy", k) for k in (1, 2, 3)]
    got[4], got[5] = halo(4), halo(5)
    acc, tick = inner("pairs_low", [1, 2, 4, 3], lambda b: INNER[b], True, acc, tick)
    tick, got[4], got[5], *more = join("join_second", tick, got[4], got[5], *more)
    block = jnp.concatenate([block] + more, axis=0)
    more = [xor_permute(block, "gz", 2 * k) for k in (1, 2, 3)]
    got[2], got[3] = halo(2), halo(3)
    acc, tick = inner("pairs_high", [5, 6, 7], lambda b: INNER[b], True, acc, tick)
    tick, got[2], got[3], *more = join("join_third", tick, got[2], got[3], *more)
    block = jnp.concatenate([block] + more, axis=0)
    other = xor_permute(block, "gz", 1)

    def outer(name, which, acc, after):
        nsrc = 4 * len(which) + 1
        return pl.pallas_call(
            functools.partial(outer_kernel, [FACES[d] for d in which]),
            out_shape=acc_shape,
            in_specs=[VMEM, VMEM, ANY] + [VMEM] * len(which),
            out_specs=VMEM,
            scratch_shapes=[
                pltpu.VMEM((nsrc, FEATS, points), BF16),
                pltpu.VMEM((nsrc, 32, points), BF16),
                pltpu.VMEM((2, 2 * CHUNK, points), BF16),
                pltpu.SMEM((256,), jnp.int32),
                pltpu.SMEM((128,), jnp.int32),
                pltpu.SMEM((32,), jnp.int32),
            ],
            compiler_params=PARAMS,
            cost_estimate=COST,
            name=name,
        )(fb, acc, after, *[got[d] for d in which])

    acc = outer("face_tiles", [0, 1, 2, 3, 4, 5], acc, tick)
    kv, sums = pl.pallas_call(
        far_kernel,
        out_shape=[shape((BOXES, 32, points), BF16), shape((1, 128), F32)],
        in_specs=[SMEM, SMEM, SMEM, ANY, ANY, VMEM, VMEM, VMEM],
        out_specs=[VMEM, VMEM],
        scratch_shapes=[
            pltpu.VMEM((64, 64, 256), BF16),
            pltpu.VMEM((BOXES, 64, 256), F32),
            pltpu.SMEM((136,), jnp.int32),
            pltpu.SemaphoreType.DMA((2,)),
        ],
        compiler_params=PARAMS,
        name="far_total",
    )(count, req_box.reshape(128), req_tgt.reshape(128), block, other, acc, tab, pay)
    devices = lax.axis_size("gx") * lax.axis_size("gy") * lax.axis_size("gz")
    spread = jnp.broadcast_to(sums, (devices, 128))
    gathered = lax.all_to_all(spread, ("gx", "gy", "gz"), 0, 0, tiled=True)
    whole = jnp.sum(gathered, axis=0)
    quad = whole[0:32] / whole[32]
    return kv.reshape(probes.shape), quad


def solution(mesh):
    placed = (
        P("gx", "gy", "gz", None, None),
        P("gx", "gy", "gz", None, None),
        P("gx", "gy", "gz"),
        P("gx", "gy", "gz", None, None),
        P("gx", "gy", "gz", None, None),
    )
    return jax.shard_map(
        shards,
        mesh=mesh,
        in_specs=placed,
        out_specs=(P("gx", "gy", "gz", None, None), P()),
        check_vma=False,
    )
```

```python
import functools
import math

import jax
import jax.numpy as jnp
from jax import lax
from jax.experimental import pallas as pl
from jax.experimental.pallas import tpu as pltpu
from jax.sharding import PartitionSpec as P

ORDER = 4
CHUNK = 128
BOXES = 8
FEATS = 48
ROWS = 48
F32 = jnp.float32
BF16 = jnp.bfloat16
NODES = [math.cos((2.0 * a + 1.0) * math.pi / (2.0 * ORDER)) for a in range(ORDER)]


def box_id(axis, at, first, second):
    place = [0, 0, 0]
    rest = [d for d in range(3) if d != axis]
    place[axis] = at
    place[rest[0]] = first
    place[rest[1]] = second
    return (place[0] * 2 + place[1]) * 2 + place[2]


def face_boxes(axis, at):
    return [box_id(axis, at, i, j) for i in range(2) for j in range(2)]


def split3(value):
    high = value.astype(BF16).astype(F32)
    rest = value - high
    mid = rest.astype(BF16).astype(F32)
    return high, mid, rest - mid


def row_ids(points):
    return lax.broadcasted_iota(jnp.int32, (8, points), 0)


def source_rows(pos, row):
    p1, p2, p3 = split3(pos)
    n1, n2, n3 = split3(1.0 + jnp.sum(pos * pos, axis=0, keepdims=True))
    s1 = jnp.where(row < 3, p1, jnp.where(row == 3, n1, jnp.where(row == 4, n2, jnp.where(row == 5, n3, 1.0))))
    s2 = p2 + pltpu.roll(p3, 3, 0)
    return jnp.concatenate([s1, s1, s2, s2, s1, jnp.zeros_like(s1)], axis=0).astype(BF16)


def target_rows(pos, row):
    p1, p2, p3 = split3(-2.0 * pos)
    m1, m2, m3 = split3(jnp.sum(pos * pos, axis=0, keepdims=True))
    qa = jnp.where(row < 3, p1, jnp.where(row < 6, 1.0, jnp.where(row == 6, m1, m2)))
    qb = jnp.where(row < 3, p2, jnp.where(row == 6, m3, 0.0))
    qc = p1 + pltpu.roll(p1, 3, 0)
    return jnp.concatenate([qa, qb, qc, p2, p3, jnp.zeros_like(qa)], axis=0).astype(BF16)


def prep_kernel(counts, offs_hbm, probes_hbm, pay, fa, fb, tab, mom, momf, f0, f1, f2, pad, offs, probes, sems):
    points = offs.shape[-1]
    row = row_ids(points)
    lane = lax.broadcasted_iota(jnp.int32, (1, points), 1)
    faces = (f0, f1, f2)
    all_offs = pltpu.make_async_copy(offs_hbm, offs, sems.at[BOXES])
    all_offs.start()
    loads = []
    for k in range(BOXES):
        load = pltpu.make_async_copy(probes_hbm.at[k // 4, k // 2 % 2, k % 2], probes.at[k], sems.at[k])
        load.start()
        loads.append(load)
    pay[BOXES] = jnp.zeros_like(pay[BOXES])
    all_offs.wait()
    for k in range(BOXES):
        place = (k // 4, k // 2 % 2, k % 2)
        pad[...] = jnp.zeros_like(pad)
        pad[0:3, :] = offs[place[0], place[1], place[2]]
        off = pad[...]
        shift = jnp.where(row == 0, place[0] - 1.0, jnp.where(row == 1, place[1] - 1.0, jnp.where(row == 2, place[2] - 1.0, 0.0)))
        pos = off + shift
        src = source_rows(pos, row)
        fa[k] = src
        fb[k] = target_rows(pos, row)
        if k == 0:
            fa[BOXES] = src
        count = counts[place]
        chunks = ((count + CHUNK - 1) // CHUNK).astype(F32)
        p1, p2, p3 = split3(pos)
        rows_a = jnp.where(row == 6, chunks, p1 + pltpu.roll(p2, 3, 0))
        tail = jnp.concatenate([rows_a, p3], axis=0).astype(BF16)
        loads[k].wait()
        vec = jnp.where(lane < count, probes[k].astype(F32), 0.0).astype(BF16)
        pay[k, 0:32, :] = vec
        pay[k, 32:48, :] = tail
        for axis in range(3):
            if place[axis] == 0:
                other = [d for d in range(3) if d != axis]
                slot = place[other[0]] * 2 + place[other[1]]
                faces[axis][slot, 0:32, :] = vec
                faces[axis][slot, 32:48, :] = tail
        unit = 2.0 * off - 1.0
        t2 = 2.0 * unit * unit - 1.0
        t3 = 2.0 * unit * t2 - unit
        weights = []
        for c in NODES:
            e2 = 2.0 * c * c - 1.0
            e3 = 2.0 * c * e2 - c
            weights.append(0.25 + 0.5 * (c * unit + e2 * t2 + e3 * t3))
        third = jnp.zeros_like(off)
        for d in range(ORDER):
            third = jnp.where(row % 4 == d, weights[d][2:3, :], third)
        seconds = []
        for half in range(2):
            seconds.append(jnp.where(row < 4, weights[2 * half][1:2, :], weights[2 * half + 1][1:2, :]))
        parts = []
        for a in range(ORDER):
            for half in range(2):
                parts.append(weights[a][0:1, :] * seconds[half] * third)
        table = jnp.concatenate(parts, axis=0).astype(BF16)
        tab[k] = table
        moment = lax.dot_general(table, vec, (((1,), (1,)), ((), ())), preferred_element_type=F32)
        momf[:, k * 32:(k + 1) * 32] = moment
    mom[...] = momf[...].astype(BF16)


WIDTHS = (512, 768, 1024)
REGION = 160


def run_steps(targets, sources_of, chunks_of, width_of, dummy, fa, vec, fb, own, out, back, tiles, steps, owner, filled):
    for c in range(len(WIDTHS)):
        filled[c] = 0
    for b in targets:
        count_b = width_of(b)
        kind = jnp.int32(0)
        for width in WIDTHS[:-1]:
            kind = kind + (count_b > width).astype(jnp.int32)
        base = kind * REGION
        at = base + filled[kind]
        for s in sources_of(b):
            count = chunks_of(s)

            def put(c, carry, s=s, b=b, at=at):
                steps[at + c] = s * 8 + c
                owner[(at + c) >> 1] = b
                return carry

            lax.fori_loop(0, count, put, 0)
            at = at + count
        steps[at] = dummy * 8
        at = at + (at & 1)
        filled[kind] = at - base
    for c in range(len(WIDTHS)):
        end = c * REGION + filled[c]
        for extra in range(6):
            steps[end + extra] = dummy * 8
            owner[(end + extra) >> 1] = targets[0]

    def columns(index):
        return pl.ds(pl.multiple_of((index & 7) * CHUNK, CHUNK), CHUNK)

    for c, width in enumerate(WIDTHS):
        first_step = c * (REGION // 2)
        total = filled[c] >> 1

        def make(t, slot, width=width):
            target = fb[owner[t], :, 0:width]
            for h in range(2):
                index = steps[2 * t + h]
                source = fa[index >> 3, :, columns(index)]
                squares = lax.dot_general(source, target, (((0,), (0,)), ((), ())), preferred_element_type=F32)
                tiles[slot, h * CHUNK:(h + 1) * CHUNK, 0:width] = lax.rsqrt(squares).astype(BF16)

        def use(t, slot, width=width):
            b = owner[t]
            first = steps[2 * t]
            second = steps[2 * t + 1]
            tile = tiles[slot, :, 0:width]
            both = jnp.concatenate([vec[first >> 3, 0:32, columns(first)], vec[second >> 3, 0:32, columns(second)]], axis=1)
            out[b, :, 0:width] += jnp.dot(both, tile, preferred_element_type=F32)
            if back is not None:
                sent = lax.dot_general(own[b, 0:32, 0:width], tile, (((1,), (1,)), ((), ())), preferred_element_type=F32)
                back[first >> 3, :, columns(first)] += sent[:, 0:CHUNK]
                back[second >> 3, :, columns(second)] += sent[:, CHUNK:]

        @pl.when(total > 0)
        def _(make=make, use=use, first_step=first_step, total=total):
            make(first_step, 0)

            def body(k, carry):
                t = first_step + 2 * k
                make(t + 1, 1)
                use(t, 0)
                make(t + 2, 0)
                use(t + 1, 1)
                return carry

            lax.fori_loop(0, (total + 1) >> 1, body, 0)


INNER = {4: (0,), 2: (0,), 1: (0,), 6: (2, 4), 5: (1, 4), 3: (1, 2), 7: (3, 5, 6)}


def count_of(counts, k):
    return counts[k // 4, k // 2 % 2, k % 2]


def inner_kernel(targets, sources_of, two_way, counts, fa, pay, fb, acc_in, after, acc, done, out, tiles, steps, owner, filled):
    if acc_in is None:
        out[...] = jnp.zeros_like(out)
    else:
        out[0:BOXES] = acc_in[...]
        out[BOXES] = jnp.zeros_like(out[BOXES])
    run_steps(
        targets, sources_of, lambda s: (count_of(counts, s) + CHUNK - 1) >> 7, lambda b: count_of(counts, b), BOXES,
        fa, pay, fb, pay, out, out if two_way else None, tiles, steps, owner, filled,
    )
    acc[...] = out[0:BOXES]
    done[...] = jnp.zeros_like(done)


def outer_kernel(counts, fb, pay, acc_self, acc_in, after, halo0, halo1, halo2, near, b0, b1, b2, probe_sums,
                 fa, vec, plus, back, tiles, steps, owner, filled, chunk_no):
    halos = (halo0, halo1, halo2)
    points = fb.shape[-1]
    row = row_ids(points)
    plus[...] = jnp.zeros_like(plus)
    back[...] = jnp.zeros_like(back)
    sources = {b: [] for b in range(BOXES)}
    spare = 12
    for axis in range(3):
        halo = halos[axis]
        targets = face_boxes(axis, 1)
        for i in range(4):
            s = axis * 4 + i
            sources[targets[i]].append(s)
            tail = halo[i, 32:48, :].astype(F32)
            rows_a = tail[0:8]
            pos = rows_a + pltpu.roll(rows_a, 5, 0) + tail[8:16]
            pos = jnp.where(row < 3, pos + jnp.where(row == axis, 2.0, 0.0), 0.0)
            feats = source_rows(pos, row)
            fa[s] = feats
            if s == 0:
                fa[spare] = feats
            vec[s] = halo[i, 0:32, :]
            chunk_no[s] = jnp.max(rows_a[6:7, 0:128]).astype(jnp.int32)
    vec[spare] = jnp.zeros_like(vec[spare])
    order = [b for b in range(BOXES) if sources[b]]
    run_steps(
        order, lambda b: sources[b], lambda s: chunk_no[s], lambda b: count_of(counts, b), spare,
        fa, vec, fb, pay, plus, back, tiles, steps, owner, filled,
    )
    total = jnp.zeros((32, 128), F32)
    for b in range(BOXES):
        extra = plus[b]
        base = acc_self[b] + acc_in[b]
        near[b] = base + extra
        weighted = pay[b, 0:32, :].astype(F32) * (base + 2.0 * extra)
        for j in range(points // 128):
            total = total + weighted[:, j * 128:(j + 1) * 128]
    probe_sums[...] = total
    for axis, ref in enumerate((b0, b1, b2)):
        ref[...] = back[4 * axis:4 * axis + 4]


def local_kernel(counts, req_box, req_tgt, here, there, momf, probe_sums, loc, sums, slab, far_acc, live, sems):
    first_copy = pltpu.make_async_copy(here, slab.at[pl.ds(0, 32)], sems.at[0])
    second_copy = pltpu.make_async_copy(there, slab.at[pl.ds(32, 32)], sems.at[1])
    first_copy.start()
    second_copy.start()
    my_y = lax.axis_index("gy")
    my_z = lax.axis_index("gz")
    far_acc[...] = jnp.zeros_like(far_acc)

    def keep(i, n):
        live[n] = i
        return n + (req_box[i >> 6, i & 63] >= 0).astype(jnp.int32)

    used = lax.fori_loop(0, 128, keep, jnp.int32(0))
    shape = (64, 64)
    source_q = lax.broadcasted_iota(jnp.int32, shape, 1)
    target_q = lax.broadcasted_iota(jnp.int32, shape, 0)

    def node(index):
        value = jnp.full(shape, 0.5 + 0.5 * NODES[0], F32)
        for a in range(1, ORDER):
            value = jnp.where(index == a, 0.5 + 0.5 * NODES[a], value)
        return value

    gaps = [node((source_q >> s) & 3) - node((target_q >> s) & 3) for s in (4, 2, 0)]
    group = lax.broadcasted_iota(jnp.int32, (64, 256), 1) >> 5
    first_copy.wait()
    second_copy.wait()

    def step(g, carry):
        for u in range(4):
            k = g * 4 + u
            i = live[jnp.minimum(k, used - 1)]
            peer = i & 63
            box = req_box[i >> 6, peer]
            tgt = req_tgt[i >> 6, peer]
            peer_y = peer >> 4
            peer_z = peer & 15
            dx = (box >> 2) - (tgt >> 2)
            dy = (peer_y - my_y) * 2 + ((box >> 1) & 1) - ((tgt >> 1) & 1)
            dz = (peer_z - my_z) * 2 + (box & 1) - (tgt & 1)
            ex = gaps[0] + dx.astype(F32)
            ey = gaps[1] + dy.astype(F32)
            ez = gaps[2] + dz.astype(F32)
            coupling = lax.rsqrt(1.0 + ex * ex + ey * ey + ez * ez).astype(BF16)
            rel_y = peer_y ^ my_y
            rel_z = peer_z ^ my_z
            at = (rel_z & 1) * 32 + ((rel_z >> 1) & 3) * 8 + rel_y * 2 + (rel_z >> 3)
            term = jnp.dot(coupling, slab[at], preferred_element_type=F32)
            wanted = jnp.where(k < used, box, -1)
            far_acc[tgt] += jnp.where(group == wanted, term, 0.0)
        return carry

    lax.fori_loop(0, (used + 3) >> 2, step, 0)
    lane = lax.broadcasted_iota(jnp.int32, (64, 128), 1)
    far_sums = jnp.zeros((64, 128), F32)
    live_points = jnp.int32(0)
    for b in range(BOXES):
        wide = far_acc[b]
        half = wide[:, 0:128] + wide[:, 128:256]
        half = half + pltpu.roll(half, 64, 1)
        half = half + pltpu.roll(half, 32, 1)
        rounded = half.astype(BF16)
        loc[b] = rounded
        moment = momf[:, (b // 4) * 128:(b // 4 + 1) * 128]
        far_sums = far_sums + jnp.where((lane >> 5) == b % 4, rounded.astype(F32) * moment, 0.0)
        live_points = live_points + count_of(counts, b)
    folded = jnp.sum(far_sums, axis=0, keepdims=True)
    folded = folded + pltpu.roll(folded, 64, 1)
    folded = folded + pltpu.roll(folded, 32, 1)
    lane32 = lax.broadcasted_iota(jnp.int32, (32, 128), 1)
    row32 = lax.broadcasted_iota(jnp.int32, (32, 128), 0)
    per_probe = jnp.sum(probe_sums[...], axis=1, keepdims=True)
    flat = jnp.sum(jnp.where(lane32 == row32, per_probe, 0.0), axis=0, keepdims=True)
    sums[...] = jnp.where(lane32[0:1] < 32, flat + folded, jnp.where(lane32[0:1] == 32, live_points.astype(F32), 0.0))


def total_kernel(counts, near, r0, r1, r2, loc, tab, kv):
    points = tab.shape[-1]
    lane = lax.broadcasted_iota(jnp.int32, (1, points), 1)
    for b in range(BOXES):
        place = (b // 4, b // 2 % 2, b % 2)
        far = lax.dot_general(loc[b][:, 0:32], tab[b], (((0,), (0,)), ((), ())), preferred_element_type=F32)
        total = near[b] + far
        for axis, ref in enumerate((r0, r1, r2)):
            if place[axis] == 0:
                other = [d for d in range(3) if d != axis]
                total = total + ref[place[other[0]] * 2 + place[other[1]]]
        kv[b] = jnp.where(lane < count_of(counts, b), total * (1.0 / math.sqrt(7.0 * points)), 0.0).astype(BF16)


VMEM = pl.BlockSpec(memory_space=pltpu.VMEM)
SMEM = pl.BlockSpec(memory_space=pltpu.SMEM)
ANY = pl.BlockSpec(memory_space=pl.ANY)
PARAMS = pltpu.CompilerParams(vmem_limit_bytes=20 * 2**20)


COST = pl.CostEstimate(flops=12 * 10**9, bytes_accessed=4 * 2**20, transcendentals=10**7)


def join(name, *arrays):
    return pl.pallas_call(
        lambda *refs: None,
        out_shape=[jax.ShapeDtypeStruct(a.shape, a.dtype) for a in arrays],
        in_specs=[ANY] * len(arrays),
        out_specs=[ANY] * len(arrays),
        input_output_aliases={i: i for i in range(len(arrays))},
        compiler_params=pltpu.CompilerParams(vmem_limit_bytes=2**20),
        name=name,
    )(*arrays)


def xor_permute(value, axis, bits):
    count = lax.axis_size(axis)
    return lax.ppermute(value, axis, [(i, i ^ bits) for i in range(count)])


def shards(offsets, probes, counts, req_box, req_tgt):
    points = offsets.shape[-1]
    shape = jax.ShapeDtypeStruct
    face = shape((4, ROWS, points), BF16)
    pay, fa, fb, tab, mom, momf, *faces = pl.pallas_call(
        prep_kernel,
        out_shape=[
            shape((BOXES + 1, ROWS, points), BF16),
            shape((BOXES + 1, FEATS, points), BF16),
            shape((BOXES, FEATS, points), BF16),
            shape((BOXES, 64, points), BF16),
            shape((64, 256), BF16),
            shape((64, 256), F32),
        ] + [face] * 3,
        in_specs=[SMEM, ANY, ANY],
        out_specs=[VMEM] * 9,
        scratch_shapes=[
            pltpu.VMEM((8, points), F32),
            pltpu.VMEM(offsets.shape, F32),
            pltpu.VMEM((BOXES, 32, points), BF16),
            pltpu.SemaphoreType.DMA((BOXES + 1,)),
        ],
        compiler_params=PARAMS,
        name="prep",
    )(counts, offsets, probes)

    acc_shape = shape((BOXES, 32, points), F32)
    lists = [
        pltpu.VMEM((2, 2 * CHUNK, points), BF16),
        pltpu.SMEM((len(WIDTHS) * REGION,), jnp.int32),
        pltpu.SMEM((len(WIDTHS) * REGION // 2,), jnp.int32),
        pltpu.SMEM((8,), jnp.int32),
    ]

    def inner(name, targets, sources_of, two_way, acc, after):
        has_acc = acc is not None

        def kernel(*refs):
            refs = list(refs)
            head = refs[:4]
            rest = refs[4:]
            acc_ref = rest.pop(0) if has_acc else None
            inner_kernel(targets, sources_of, two_way, *head, acc_ref, *rest)

        args = [counts, fa, pay, fb] + ([acc] if has_acc else []) + [after]
        return pl.pallas_call(
            kernel,
            out_shape=[acc_shape, shape((8, 128), F32)],
            in_specs=[SMEM, VMEM, VMEM, VMEM] + [VMEM] * has_acc + [ANY],
            out_specs=[VMEM, VMEM],
            scratch_shapes=[pltpu.VMEM((BOXES + 1, 32, points), F32)] + lists,
            compiler_params=PARAMS,
            cost_estimate=COST,
            name=name,
        )(*args)

    def along(axis, value, step):
        name = ("gx", "gy", "gz")[axis]
        size = lax.axis_size(name)
        return lax.ppermute(value, name, [(i, i + step) for i in range(size) if 0 <= i + step < size])

    block = mom.reshape(1, 64, 256)
    twin = xor_permute(block, "gz", 8)
    got = [along(axis, faces[axis], -1) for axis in range(3)]
    acc_self, tick = inner("self_tiles", list(range(BOXES)), lambda b: [b], False, None, mom)
    tick, twin = join("join_first", tick, twin)
    block = jnp.concatenate([block, twin], axis=0)
    more = [xor_permute(block, "gy", k) for k in (1, 2, 3)]
    acc, tick = inner("pairs_low", [1, 2, 4, 3], lambda b: INNER[b], True, None, tick)
    tick, got[0], got[1], got[2], *more = join("join_second", tick, *got, *more)
    block = jnp.concatenate([block] + more, axis=0)
    more = [xor_permute(block, "gz", 2 * k) for k in (1, 2, 3)]
    acc, tick = inner("pairs_high", [5, 6, 7], lambda b: INNER[b], True, acc, tick)
    tick, *more = join("join_third", tick, *more)
    block = jnp.concatenate([block] + more, axis=0)
    other = xor_permute(block, "gz", 1)
    near, *backs, probe_sums = pl.pallas_call(
        outer_kernel,
        out_shape=[acc_shape] + [shape((4, 32, points), F32)] * 3 + [shape((32, 128), F32)],
        in_specs=[SMEM, VMEM, VMEM, VMEM, VMEM, ANY, VMEM, VMEM, VMEM],
        out_specs=[VMEM] * 5,
        scratch_shapes=[
            pltpu.VMEM((13, FEATS, points), BF16),
            pltpu.VMEM((13, 32, points), BF16),
            pltpu.VMEM((BOXES, 32, points), F32),
            pltpu.VMEM((13, 32, points), F32),
        ] + lists + [pltpu.SMEM((16,), jnp.int32)],
        compiler_params=PARAMS,
        cost_estimate=COST,
        name="face_tiles",
    )(counts, fb, pay, acc_self, acc, tick, *got)
    returned = [along(axis, backs[axis], 1) for axis in range(3)]
    loc, sums = pl.pallas_call(
        local_kernel,
        out_shape=[shape((BOXES, 64, 128), BF16), shape((1, 128), F32)],
        in_specs=[SMEM, SMEM, SMEM, ANY, ANY, VMEM, VMEM],
        out_specs=[VMEM, VMEM],
        scratch_shapes=[
            pltpu.VMEM((64, 64, 256), BF16),
            pltpu.VMEM((BOXES, 64, 256), F32),
            pltpu.SMEM((136,), jnp.int32),
            pltpu.SemaphoreType.DMA((2,)),
        ],
        compiler_params=PARAMS,
        name="locals",
    )(counts, *[jnp.swapaxes(r, 3, 4).reshape(2, 64) for r in (req_box, req_tgt)], block, other, momf, probe_sums)
    devices = lax.axis_size("gx") * lax.axis_size("gy") * lax.axis_size("gz")
    spread = jnp.broadcast_to(sums, (devices, 128))
    gathered = lax.all_to_all(spread, ("gx", "gy", "gz"), 0, 0, tiled=True)
    kv = pl.pallas_call(
        total_kernel,
        out_shape=shape((BOXES, 32, points), BF16),
        in_specs=[SMEM] + [VMEM] * 6,
        out_specs=VMEM,
        compiler_params=PARAMS,
        cost_estimate=COST,
        name="total",
    )(counts, near, *returned, loc, tab)
    whole = jnp.sum(gathered, axis=0)
    quad = whole[0:32] * (1.0 / math.sqrt(7.0 * points)) / whole[32]
    return kv.reshape(probes.shape), quad


def solution(mesh):
    placed = (
        P("gx", "gy", "gz", None, None),
        P("gx", "gy", "gz", None, None),
        P("gx", "gy", "gz"),
        P("gx", "gy", "gz", None, None),
        P("gx", "gy", "gz", None, None),
    )
    return jax.shard_map(
        shards,
        mesh=mesh,
        in_specs=placed,
        out_specs=(P("gx", "gy", "gz", None, None), P()),
        check_vma=False,
    )
```

```python
import functools
import math

import jax
import jax.numpy as jnp
from jax import lax
from jax.experimental import pallas as pl
from jax.experimental.pallas import tpu as pltpu
from jax.sharding import PartitionSpec as P

ORDER = 4
CHUNK = 128
BOXES = 8
FEATS = 48
ROWS = 48
F32 = jnp.float32
BF16 = jnp.bfloat16
NODES = [math.cos((2.0 * a + 1.0) * math.pi / (2.0 * ORDER)) for a in range(ORDER)]


def box_id(axis, at, first, second):
    place = [0, 0, 0]
    rest = [d for d in range(3) if d != axis]
    place[axis] = at
    place[rest[0]] = first
    place[rest[1]] = second
    return (place[0] * 2 + place[1]) * 2 + place[2]


def face_boxes(axis, at):
    return [box_id(axis, at, i, j) for i in range(2) for j in range(2)]


def split3(value):
    high = value.astype(BF16).astype(F32)
    rest = value - high
    mid = rest.astype(BF16).astype(F32)
    return high, mid, rest - mid


def row_ids(points):
    return lax.broadcasted_iota(jnp.int32, (8, points), 0)


def source_rows(pos, row):
    p1, p2, p3 = split3(pos)
    n1, n2, n3 = split3(1.0 + jnp.sum(pos * pos, axis=0, keepdims=True))
    s1 = jnp.where(row < 3, p1, jnp.where(row == 3, n1, jnp.where(row == 4, n2, jnp.where(row == 5, n3, 1.0))))
    s2 = p2 + pltpu.roll(p3, 3, 0)
    return jnp.concatenate([s1, s1, s2, s2, s1, jnp.zeros_like(s1)], axis=0).astype(BF16)


def target_rows(pos, row):
    p1, p2, p3 = split3(-2.0 * pos)
    m1, m2, m3 = split3(jnp.sum(pos * pos, axis=0, keepdims=True))
    qa = jnp.where(row < 3, p1, jnp.where(row < 6, 1.0, jnp.where(row == 6, m1, m2)))
    qb = jnp.where(row < 3, p2, jnp.where(row == 6, m3, 0.0))
    qc = p1 + pltpu.roll(p1, 3, 0)
    return jnp.concatenate([qa, qb, qc, p2, p3, jnp.zeros_like(qa)], axis=0).astype(BF16)


def prep_kernel(counts, offs, probes, pay, fa, fb, tab, mom, momf, f0, f1, f2, pad):
    points = offs.shape[-1]
    row = row_ids(points)
    lane = lax.broadcasted_iota(jnp.int32, (1, points), 1)
    faces = (f0, f1, f2)
    pay[BOXES] = jnp.zeros_like(pay[BOXES])
    for k in range(BOXES):
        place = (k // 4, k // 2 % 2, k % 2)
        pad[...] = jnp.zeros_like(pad)
        pad[0:3, :] = offs[place[0], place[1], place[2]]
        off = pad[...]
        shift = jnp.where(row == 0, place[0] - 1.0, jnp.where(row == 1, place[1] - 1.0, jnp.where(row == 2, place[2] - 1.0, 0.0)))
        pos = off + shift
        src = source_rows(pos, row)
        fa[k] = src
        fb[k] = target_rows(pos, row)
        if k == 0:
            fa[BOXES] = src
        count = counts[place]
        chunks = ((count + CHUNK - 1) // CHUNK).astype(F32)
        p1, p2, p3 = split3(pos)
        rows_a = jnp.where(row == 6, chunks, p1 + pltpu.roll(p2, 3, 0))
        tail = jnp.concatenate([rows_a, p3], axis=0).astype(BF16)
        vec = jnp.where(lane < count, probes[place].astype(F32), 0.0).astype(BF16)
        pay[k, 0:32, :] = vec
        pay[k, 32:48, :] = tail
        for axis in range(3):
            if place[axis] == 0:
                other = [d for d in range(3) if d != axis]
                slot = place[other[0]] * 2 + place[other[1]]
                faces[axis][slot, 0:32, :] = vec
                faces[axis][slot, 32:48, :] = tail
        unit = 2.0 * off - 1.0
        t2 = 2.0 * unit * unit - 1.0
        t3 = 2.0 * unit * t2 - unit
        weights = []
        for c in NODES:
            e2 = 2.0 * c * c - 1.0
            e3 = 2.0 * c * e2 - c
            weights.append(0.25 + 0.5 * (c * unit + e2 * t2 + e3 * t3))
        third = jnp.zeros_like(off)
        for d in range(ORDER):
            third = jnp.where(row % 4 == d, weights[d][2:3, :], third)
        seconds = []
        for half in range(2):
            seconds.append(jnp.where(row < 4, weights[2 * half][1:2, :], weights[2 * half + 1][1:2, :]))
        parts = []
        for a in range(ORDER):
            for half in range(2):
                parts.append(weights[a][0:1, :] * seconds[half] * third)
        table = jnp.concatenate(parts, axis=0).astype(BF16)
        tab[k] = table
        moment = lax.dot_general(table, vec, (((1,), (1,)), ((), ())), preferred_element_type=F32)
        momf[:, k * 32:(k + 1) * 32] = moment
    mom[...] = momf[...].astype(BF16)


WIDTHS = (768, 1024)
REGION = 160


def run_steps(targets, sources_of, chunks_of, width_of, dummy, fa, vec, fb, own, out, back, tiles, flips, steps, owner, filled):
    for c in range(len(WIDTHS)):
        filled[c] = 0
    for b in targets:
        count_b = width_of(b)
        kind = jnp.int32(0)
        for width in WIDTHS[:-1]:
            kind = kind + (count_b > width).astype(jnp.int32)
        base = kind * REGION
        at = base + filled[kind]
        for s in sources_of(b):
            count = chunks_of(s)

            def put(c, carry, s=s, b=b, at=at):
                steps[at + c] = s * 8 + c
                owner[(at + c) >> 1] = b
                return carry

            lax.fori_loop(0, count, put, 0)
            at = at + count
        steps[at] = dummy * 8
        at = at + (at & 1)
        filled[kind] = at - base
    for c in range(len(WIDTHS)):
        end = c * REGION + filled[c]
        for extra in range(8):
            steps[end + extra] = dummy * 8
            owner[(end + extra) >> 1] = targets[0]

    def columns(index):
        return pl.ds(pl.multiple_of((index & 7) * CHUNK, CHUNK), CHUNK)

    for c, width in enumerate(WIDTHS):
        first_step = c * (REGION // 2)
        total = filled[c] >> 1

        def flip(t, slot):
            for h in range(2):
                index = steps[2 * t + h]
                flips[slot, h * CHUNK:(h + 1) * CHUNK, :] = fa[index >> 3, :, columns(index)].T

        def make(t, slot, width=width):
            target = fb[owner[t], :, 0:width]
            squares = jnp.dot(flips[slot], target, preferred_element_type=F32)
            tiles[slot, :, 0:width] = lax.rsqrt(squares).astype(BF16)

        def use(t, slot, width=width):
            b = owner[t]
            first = steps[2 * t]
            second = steps[2 * t + 1]
            tile = tiles[slot, :, 0:width]
            both = jnp.concatenate([vec[first >> 3, 0:32, columns(first)], vec[second >> 3, 0:32, columns(second)]], axis=1)
            out[b, :, 0:width] += jnp.dot(both, tile, preferred_element_type=F32)
            if back is not None:
                sent = lax.dot_general(own[b, 0:32, 0:width], tile, (((1,), (1,)), ((), ())), preferred_element_type=F32)
                back[first >> 3, :, columns(first)] += sent[:, 0:CHUNK]
                back[second >> 3, :, columns(second)] += sent[:, CHUNK:]

        @pl.when(total > 0)
        def _(flip=flip, make=make, use=use, first_step=first_step, total=total):
            flip(first_step, 0)
            flip(first_step + 1, 1)
            make(first_step, 0)

            def body(k, carry):
                t = first_step + 2 * k
                make(t + 1, 1)
                flip(t + 2, 0)
                use(t, 0)
                make(t + 2, 0)
                flip(t + 3, 1)
                use(t + 1, 1)
                return carry

            lax.fori_loop(0, (total + 1) >> 1, body, 0)


INNER = {4: (0,), 2: (0,), 1: (0,), 6: (2, 4), 5: (1, 4), 3: (1, 2), 7: (3, 5, 6)}


def count_of(counts, k):
    return counts[k // 4, k // 2 % 2, k % 2]


def inner_kernel(targets, sources_of, two_way, counts, fa, pay, fb, acc_in, after, acc, done, out, tiles, flips, steps, owner, filled):
    if acc_in is None:
        out[...] = jnp.zeros_like(out)
    else:
        out[0:BOXES] = acc_in[...]
        out[BOXES] = jnp.zeros_like(out[BOXES])
    run_steps(
        targets, sources_of, lambda s: (count_of(counts, s) + CHUNK - 1) >> 7, lambda b: count_of(counts, b), BOXES,
        fa, pay, fb, pay, out, out if two_way else None, tiles, flips, steps, owner, filled,
    )
    acc[...] = out[0:BOXES]
    done[...] = jnp.zeros_like(done)


def outer_kernel(counts, fb, pay, acc_self, acc_in, after, halo0, halo1, halo2, near, b0, b1, b2, probe_sums,
                 fa, vec, plus, back, tiles, flips, steps, owner, filled, chunk_no):
    halos = (halo0, halo1, halo2)
    points = fb.shape[-1]
    row = row_ids(points)
    plus[...] = jnp.zeros_like(plus)
    back[...] = jnp.zeros_like(back)
    sources = {b: [] for b in range(BOXES)}
    spare = 12
    for axis in range(3):
        halo = halos[axis]
        targets = face_boxes(axis, 1)
        for i in range(4):
            s = axis * 4 + i
            sources[targets[i]].append(s)
            tail = halo[i, 32:48, :].astype(F32)
            rows_a = tail[0:8]
            pos = rows_a + pltpu.roll(rows_a, 5, 0) + tail[8:16]
            pos = jnp.where(row < 3, pos + jnp.where(row == axis, 2.0, 0.0), 0.0)
            feats = source_rows(pos, row)
            fa[s] = feats
            if s == 0:
                fa[spare] = feats
            vec[s] = halo[i, 0:32, :]
            chunk_no[s] = jnp.max(rows_a[6:7, 0:128]).astype(jnp.int32)
    vec[spare] = jnp.zeros_like(vec[spare])
    order = [b for b in range(BOXES) if sources[b]]
    run_steps(
        order, lambda b: sources[b], lambda s: chunk_no[s], lambda b: count_of(counts, b), spare,
        fa, vec, fb, pay, plus, back, tiles, flips, steps, owner, filled,
    )
    total = jnp.zeros((32, 128), F32)
    for b in range(BOXES):
        extra = plus[b]
        base = acc_self[b] + acc_in[b]
        near[b] = base + extra
        weighted = pay[b, 0:32, :].astype(F32) * (base + 2.0 * extra)
        for j in range(points // 128):
            total = total + weighted[:, j * 128:(j + 1) * 128]
    probe_sums[...] = total
    for axis, ref in enumerate((b0, b1, b2)):
        ref[...] = back[4 * axis:4 * axis + 4]


def local_kernel(counts, req_box, req_tgt, here, there, momf, probe_sums, loc, sums, slab, far_acc, live, sems):
    first_copy = pltpu.make_async_copy(here, slab.at[pl.ds(0, 32)], sems.at[0])
    second_copy = pltpu.make_async_copy(there, slab.at[pl.ds(32, 32)], sems.at[1])
    first_copy.start()
    second_copy.start()
    my_y = lax.axis_index("gy")
    my_z = lax.axis_index("gz")
    far_acc[...] = jnp.zeros_like(far_acc)

    def keep(i, n):
        live[n] = i
        return n + (req_box[i >> 6, i & 63] >= 0).astype(jnp.int32)

    used = lax.fori_loop(0, 128, keep, jnp.int32(0))
    shape = (64, 64)
    source_q = lax.broadcasted_iota(jnp.int32, shape, 1)
    target_q = lax.broadcasted_iota(jnp.int32, shape, 0)

    def node(index):
        value = jnp.full(shape, 0.5 + 0.5 * NODES[0], F32)
        for a in range(1, ORDER):
            value = jnp.where(index == a, 0.5 + 0.5 * NODES[a], value)
        return value

    gaps = [node((source_q >> s) & 3) - node((target_q >> s) & 3) for s in (4, 2, 0)]
    group = lax.broadcasted_iota(jnp.int32, (64, 256), 1) >> 5
    first_copy.wait()
    second_copy.wait()

    def step(g, carry):
        for u in range(8):
            k = g * 8 + u
            i = live[jnp.minimum(k, used - 1)]
            peer = i & 63
            box = req_box[i >> 6, peer]
            tgt = req_tgt[i >> 6, peer]
            peer_y = peer >> 4
            peer_z = peer & 15
            dx = (box >> 2) - (tgt >> 2)
            dy = (peer_y - my_y) * 2 + ((box >> 1) & 1) - ((tgt >> 1) & 1)
            dz = (peer_z - my_z) * 2 + (box & 1) - (tgt & 1)
            ex = gaps[0] + dx.astype(F32)
            ey = gaps[1] + dy.astype(F32)
            ez = gaps[2] + dz.astype(F32)
            coupling = lax.rsqrt(1.0 + ex * ex + ey * ey + ez * ez).astype(BF16)
            rel_y = peer_y ^ my_y
            rel_z = peer_z ^ my_z
            at = (rel_z & 1) * 32 + ((rel_z >> 1) & 3) * 8 + rel_y * 2 + (rel_z >> 3)
            term = jnp.dot(coupling, slab[at], preferred_element_type=F32)
            wanted = jnp.where(k < used, box, -1)
            far_acc[tgt] += jnp.where(group == wanted, term, 0.0)
        return carry

    lax.fori_loop(0, (used + 7) >> 3, step, 0)
    lane = lax.broadcasted_iota(jnp.int32, (64, 128), 1)
    far_sums = jnp.zeros((64, 128), F32)
    live_points = jnp.int32(0)
    for b in range(BOXES):
        wide = far_acc[b]
        half = wide[:, 0:128] + wide[:, 128:256]
        half = half + pltpu.roll(half, 64, 1)
        half = half + pltpu.roll(half, 32, 1)
        rounded = half.astype(BF16)
        loc[b] = rounded
        moment = momf[:, (b // 4) * 128:(b // 4 + 1) * 128]
        far_sums = far_sums + jnp.where((lane >> 5) == b % 4, rounded.astype(F32) * moment, 0.0)
        live_points = live_points + count_of(counts, b)
    folded = jnp.sum(far_sums, axis=0, keepdims=True)
    folded = folded + pltpu.roll(folded, 64, 1)
    folded = folded + pltpu.roll(folded, 32, 1)
    lane32 = lax.broadcasted_iota(jnp.int32, (32, 128), 1)
    row32 = lax.broadcasted_iota(jnp.int32, (32, 128), 0)
    per_probe = jnp.sum(probe_sums[...], axis=1, keepdims=True)
    flat = jnp.sum(jnp.where(lane32 == row32, per_probe, 0.0), axis=0, keepdims=True)
    sums[...] = jnp.where(lane32[0:1] < 32, flat + folded, jnp.where(lane32[0:1] == 32, live_points.astype(F32), 0.0))


def total_kernel(counts, near, r0, r1, r2, loc, tab, kv):
    points = tab.shape[-1]
    lane = lax.broadcasted_iota(jnp.int32, (1, points), 1)
    for b in range(BOXES):
        place = (b // 4, b // 2 % 2, b % 2)
        far = lax.dot_general(loc[b][:, 0:32], tab[b], (((0,), (0,)), ((), ())), preferred_element_type=F32)
        total = near[b] + far
        for axis, ref in enumerate((r0, r1, r2)):
            if place[axis] == 0:
                other = [d for d in range(3) if d != axis]
                total = total + ref[place[other[0]] * 2 + place[other[1]]]
        kv[b] = jnp.where(lane < count_of(counts, b), total * (1.0 / math.sqrt(7.0 * points)), 0.0).astype(BF16)


VMEM = pl.BlockSpec(memory_space=pltpu.VMEM)
SMEM = pl.BlockSpec(memory_space=pltpu.SMEM)
ANY = pl.BlockSpec(memory_space=pl.ANY)
PARAMS = pltpu.CompilerParams(vmem_limit_bytes=20 * 2**20)


COST = pl.CostEstimate(flops=12 * 10**9, bytes_accessed=4 * 2**20, transcendentals=10**7)


def join(name, *arrays):
    return pl.pallas_call(
        lambda *refs: None,
        out_shape=[jax.ShapeDtypeStruct(a.shape, a.dtype) for a in arrays],
        in_specs=[ANY] * len(arrays),
        out_specs=[ANY] * len(arrays),
        input_output_aliases={i: i for i in range(len(arrays))},
        compiler_params=pltpu.CompilerParams(vmem_limit_bytes=2**20),
        name=name,
    )(*arrays)


def xor_permute(value, axis, bits):
    count = lax.axis_size(axis)
    return lax.ppermute(value, axis, [(i, i ^ bits) for i in range(count)])


def shards(offsets, probes, counts, req_box, req_tgt):
    points = offsets.shape[-1]
    shape = jax.ShapeDtypeStruct
    face = shape((4, ROWS, points), BF16)
    pay, fa, fb, tab, mom, momf, *faces = pl.pallas_call(
        prep_kernel,
        out_shape=[
            shape((BOXES + 1, ROWS, points), BF16),
            shape((BOXES + 1, FEATS, points), BF16),
            shape((BOXES, FEATS, points), BF16),
            shape((BOXES, 64, points), BF16),
            shape((64, 256), BF16),
            shape((64, 256), F32),
        ] + [face] * 3,
        in_specs=[SMEM, VMEM, VMEM],
        out_specs=[VMEM] * 9,
        scratch_shapes=[
            pltpu.VMEM((8, points), F32),
        ],
        compiler_params=PARAMS,
        name="prep",
    )(counts, offsets, probes)

    acc_shape = shape((BOXES, 32, points), F32)
    lists = [
        pltpu.VMEM((2, 2 * CHUNK, points), BF16),
        pltpu.VMEM((2, 2 * CHUNK, FEATS), BF16),
        pltpu.SMEM((len(WIDTHS) * REGION,), jnp.int32),
        pltpu.SMEM((len(WIDTHS) * REGION // 2,), jnp.int32),
        pltpu.SMEM((8,), jnp.int32),
    ]

    def inner(name, targets, sources_of, two_way, acc, after):
        has_acc = acc is not None

        def kernel(*refs):
            refs = list(refs)
            head = refs[:4]
            rest = refs[4:]
            acc_ref = rest.pop(0) if has_acc else None
            inner_kernel(targets, sources_of, two_way, *head, acc_ref, *rest)

        args = [counts, fa, pay, fb] + ([acc] if has_acc else []) + [after]
        return pl.pallas_call(
            kernel,
            out_shape=[acc_shape, shape((8, 128), F32)],
            in_specs=[SMEM, VMEM, VMEM, VMEM] + [VMEM] * has_acc + [ANY],
            out_specs=[VMEM, VMEM],
            scratch_shapes=[pltpu.VMEM((BOXES + 1, 32, points), F32)] + lists,
            compiler_params=PARAMS,
            cost_estimate=COST,
            name=name,
        )(*args)

    def along(axis, value, step):
        name = ("gx", "gy", "gz")[axis]
        size = lax.axis_size(name)
        return lax.ppermute(value, name, [(i, i + step) for i in range(size) if 0 <= i + step < size])

    block = mom.reshape(1, 64, 256)
    twin = xor_permute(block, "gz", 8)
    got = [along(axis, faces[axis], -1) for axis in range(3)]
    acc_self, tick = inner("self_tiles", list(range(BOXES)), lambda b: [b], False, None, mom)
    tick, twin, got[0], got[1], got[2] = join("join_first", tick, twin, *got)
    block = jnp.concatenate([block, twin], axis=0)
    more = [xor_permute(block, "gy", k) for k in (1, 2, 3)]
    acc, tick = inner("pairs_low", [1, 2, 4, 3], lambda b: INNER[b], True, None, tick)
    tick, *more = join("join_second", tick, *more)
    block = jnp.concatenate([block] + more, axis=0)
    more = [xor_permute(block, "gz", 2 * k) for k in (1, 2, 3)]
    acc, tick = inner("pairs_high", [5, 6, 7], lambda b: INNER[b], True, acc, tick)
    tick, *more = join("join_third", tick, *more)
    block = jnp.concatenate([block] + more, axis=0)
    other = xor_permute(block, "gz", 1)
    near, *backs, probe_sums = pl.pallas_call(
        outer_kernel,
        out_shape=[acc_shape] + [shape((4, 32, points), F32)] * 3 + [shape((32, 128), F32)],
        in_specs=[SMEM, VMEM, VMEM, VMEM, VMEM, ANY, VMEM, VMEM, VMEM],
        out_specs=[VMEM] * 5,
        scratch_shapes=[
            pltpu.VMEM((13, FEATS, points), BF16),
            pltpu.VMEM((13, 32, points), BF16),
            pltpu.VMEM((BOXES, 32, points), F32),
            pltpu.VMEM((13, 32, points), F32),
        ] + lists + [pltpu.SMEM((16,), jnp.int32)],
        compiler_params=PARAMS,
        cost_estimate=COST,
        name="face_tiles",
    )(counts, fb, pay, acc_self, acc, tick, *got)
    returned = [along(axis, backs[axis], 1) for axis in range(3)]
    loc, sums = pl.pallas_call(
        local_kernel,
        out_shape=[shape((BOXES, 64, 128), BF16), shape((1, 128), F32)],
        in_specs=[SMEM, SMEM, SMEM, ANY, ANY, VMEM, VMEM],
        out_specs=[VMEM, VMEM],
        scratch_shapes=[
            pltpu.VMEM((64, 64, 256), BF16),
            pltpu.VMEM((BOXES, 64, 256), F32),
            pltpu.SMEM((136,), jnp.int32),
            pltpu.SemaphoreType.DMA((2,)),
        ],
        compiler_params=PARAMS,
        name="locals",
    )(counts, *[jnp.swapaxes(r, 3, 4).reshape(2, 64) for r in (req_box, req_tgt)], block, other, momf, probe_sums)
    devices = lax.axis_size("gx") * lax.axis_size("gy") * lax.axis_size("gz")
    spread = jnp.broadcast_to(sums, (devices, 128))
    gathered = lax.all_to_all(spread, ("gx", "gy", "gz"), 0, 0, tiled=True)
    kv = pl.pallas_call(
        total_kernel,
        out_shape=shape((BOXES, 32, points), BF16),
        in_specs=[SMEM] + [VMEM] * 6,
        out_specs=VMEM,
        compiler_params=PARAMS,
        cost_estimate=COST,
        name="total",
    )(counts, near, *returned, loc, tab)
    whole = jnp.sum(gathered, axis=0)
    quad = whole[0:32] * (1.0 / math.sqrt(7.0 * points)) / whole[32]
    return kv.reshape(probes.shape), quad


def solution(mesh):
    placed = (
        P("gx", "gy", "gz", None, None),
        P("gx", "gy", "gz", None, None),
        P("gx", "gy", "gz"),
        P("gx", "gy", "gz", None, None),
        P("gx", "gy", "gz", None, None),
    )
    return jax.shard_map(
        shards,
        mesh=mesh,
        in_specs=placed,
        out_specs=(P("gx", "gy", "gz", None, None), P()),
        check_vma=False,
    )
```

```python
import functools
import math

import jax
import jax.numpy as jnp
from jax import lax
from jax.experimental import pallas as pl
from jax.experimental.pallas import tpu as pltpu
from jax.sharding import PartitionSpec as P

ORDER = 4
CHUNK = 128
BOXES = 8
FEATS = 48
ROWS = 48
F32 = jnp.float32
BF16 = jnp.bfloat16
NODES = [math.cos((2.0 * a + 1.0) * math.pi / (2.0 * ORDER)) for a in range(ORDER)]


def box_id(axis, at, first, second):
    place = [0, 0, 0]
    rest = [d for d in range(3) if d != axis]
    place[axis] = at
    place[rest[0]] = first
    place[rest[1]] = second
    return (place[0] * 2 + place[1]) * 2 + place[2]


def face_boxes(axis, at):
    return [box_id(axis, at, i, j) for i in range(2) for j in range(2)]


def split3(value):
    high = value.astype(BF16).astype(F32)
    rest = value - high
    mid = rest.astype(BF16).astype(F32)
    return high, mid, rest - mid


def row_ids(points):
    return lax.broadcasted_iota(jnp.int32, (8, points), 0)


def source_rows(pos, row):
    p1, p2, p3 = split3(pos)
    n1, n2, n3 = split3(1.0 + jnp.sum(pos * pos, axis=0, keepdims=True))
    s1 = jnp.where(row < 3, p1, jnp.where(row == 3, n1, jnp.where(row == 4, n2, jnp.where(row == 5, n3, 1.0))))
    s2 = p2 + pltpu.roll(p3, 3, 0)
    return jnp.concatenate([s1, s1, s2, s2, s1, jnp.zeros_like(s1)], axis=0).astype(BF16)


def target_rows(pos, row):
    p1, p2, p3 = split3(-2.0 * pos)
    m1, m2, m3 = split3(jnp.sum(pos * pos, axis=0, keepdims=True))
    qa = jnp.where(row < 3, p1, jnp.where(row < 6, 1.0, jnp.where(row == 6, m1, m2)))
    qb = jnp.where(row < 3, p2, jnp.where(row == 6, m3, 0.0))
    qc = p1 + pltpu.roll(p1, 3, 0)
    return jnp.concatenate([qa, qb, qc, p2, p3, jnp.zeros_like(qa)], axis=0).astype(BF16)


def prep_kernel(counts, offs, probes, pay, fa, fb, tab, mom, momf, f0, f1, f2, pad):
    points = offs.shape[-1]
    row = row_ids(points)
    lane = lax.broadcasted_iota(jnp.int32, (1, points), 1)
    faces = (f0, f1, f2)
    pay[BOXES] = jnp.zeros_like(pay[BOXES])
    for k in range(BOXES):
        place = (k // 4, k // 2 % 2, k % 2)
        pad[...] = jnp.zeros_like(pad)
        for d in range(3):
            pad[d:d + 1, :] = offs[place[0], place[1], d, place[2]:place[2] + 1, :]
        off = pad[...]
        shift = jnp.where(row == 0, place[0] - 1.0, jnp.where(row == 1, place[1] - 1.0, jnp.where(row == 2, place[2] - 1.0, 0.0)))
        pos = off + shift
        src = source_rows(pos, row)
        fa[k] = src
        fb[k] = target_rows(pos, row)
        if k == 0:
            fa[BOXES] = src
        count = counts[place]
        chunks = ((count + CHUNK - 1) // CHUNK).astype(F32)
        p1, p2, p3 = split3(pos)
        rows_a = jnp.where(row == 6, chunks, p1 + pltpu.roll(p2, 3, 0))
        tail = jnp.concatenate([rows_a, p3], axis=0).astype(BF16)
        vec = jnp.where(lane < count, probes[place].astype(F32), 0.0).astype(BF16)
        pay[k, 0:32, :] = vec
        pay[k, 32:48, :] = tail
        for axis in range(3):
            if place[axis] == 0:
                other = [d for d in range(3) if d != axis]
                slot = place[other[0]] * 2 + place[other[1]]
                faces[axis][slot, 0:32, :] = vec
                faces[axis][slot, 32:48, :] = tail
        unit = 2.0 * off - 1.0
        t2 = 2.0 * unit * unit - 1.0
        t3 = 2.0 * unit * t2 - unit
        weights = []
        for c in NODES:
            e2 = 2.0 * c * c - 1.0
            e3 = 2.0 * c * e2 - c
            weights.append(0.25 + 0.5 * (c * unit + e2 * t2 + e3 * t3))
        third = jnp.zeros_like(off)
        for d in range(ORDER):
            third = jnp.where(row % 4 == d, weights[d][2:3, :], third)
        seconds = []
        for half in range(2):
            seconds.append(jnp.where(row < 4, weights[2 * half][1:2, :], weights[2 * half + 1][1:2, :]))
        parts = []
        for a in range(ORDER):
            for half in range(2):
                parts.append(weights[a][0:1, :] * seconds[half] * third)
        table = jnp.concatenate(parts, axis=0).astype(BF16)
        tab[k] = table
        moment = lax.dot_general(table, vec, (((1,), (1,)), ((), ())), preferred_element_type=F32)
        momf[:, k * 32:(k + 1) * 32] = moment
    mom[...] = momf[...].astype(BF16)


WIDTHS = (768, 1024)
REGION = 160


def run_steps(targets, sources_of, chunks_of, width_of, dummy, fa, vec, fb, own, out, back, tiles, flips, steps, owner, filled):
    for c in range(len(WIDTHS)):
        filled[c] = 0
    for b in targets:
        count_b = width_of(b)
        kind = jnp.int32(0)
        for width in WIDTHS[:-1]:
            kind = kind + (count_b > width).astype(jnp.int32)
        base = kind * REGION
        at = base + filled[kind]
        for s in sources_of(b):
            count = chunks_of(s)

            def put(c, carry, s=s, b=b, at=at):
                steps[at + c] = s * 8 + c
                owner[(at + c) >> 1] = b
                return carry

            lax.fori_loop(0, count, put, 0)
            at = at + count
        steps[at] = dummy * 8
        at = at + (at & 1)
        filled[kind] = at - base
    for c in range(len(WIDTHS)):
        end = c * REGION + filled[c]
        for extra in range(8):
            steps[end + extra] = dummy * 8
            owner[(end + extra) >> 1] = targets[0]

    def columns(index):
        return pl.ds(pl.multiple_of((index & 7) * CHUNK, CHUNK), CHUNK)

    for c, width in enumerate(WIDTHS):
        first_step = c * (REGION // 2)
        total = filled[c] >> 1

        def flip(t, slot):
            for h in range(2):
                index = steps[2 * t + h]
                flips[slot, h * CHUNK:(h + 1) * CHUNK, :] = fa[index >> 3, :, columns(index)].T

        def make(t, slot, width=width):
            target = fb[owner[t], :, 0:width]
            squares = jnp.dot(flips[slot], target, preferred_element_type=F32)
            tiles[slot, :, 0:width] = lax.rsqrt(squares).astype(BF16)

        def use(t, slot, width=width):
            b = owner[t]
            first = steps[2 * t]
            second = steps[2 * t + 1]
            tile = tiles[slot, :, 0:width]
            both = jnp.concatenate([vec[first >> 3, 0:32, columns(first)], vec[second >> 3, 0:32, columns(second)]], axis=1)
            out[b, :, 0:width] += jnp.dot(both, tile, preferred_element_type=F32)
            if back is not None:
                sent = lax.dot_general(own[b, 0:32, 0:width], tile, (((1,), (1,)), ((), ())), preferred_element_type=F32)
                back[first >> 3, :, columns(first)] += sent[:, 0:CHUNK]
                back[second >> 3, :, columns(second)] += sent[:, CHUNK:]

        @pl.when(total > 0)
        def _(flip=flip, make=make, use=use, first_step=first_step, total=total):
            flip(first_step, 0)
            flip(first_step + 1, 1)
            make(first_step, 0)

            def body(k, carry):
                t = first_step + 2 * k
                make(t + 1, 1)
                flip(t + 2, 0)
                use(t, 0)
                make(t + 2, 0)
                flip(t + 3, 1)
                use(t + 1, 1)
                return carry

            lax.fori_loop(0, (total + 1) >> 1, body, 0)


INNER = {4: (0,), 2: (0,), 1: (0,), 6: (2, 4), 5: (1, 4), 3: (1, 2), 7: (3, 5, 6)}


def count_of(counts, k):
    return counts[k // 4, k // 2 % 2, k % 2]


def inner_kernel(targets, sources_of, two_way, counts, fa, pay, fb, acc_in, after, acc, done, out, tiles, flips, steps, owner, filled):
    if acc_in is None:
        out[...] = jnp.zeros_like(out)
    else:
        out[0:BOXES] = acc_in[...]
        out[BOXES] = jnp.zeros_like(out[BOXES])
    run_steps(
        targets, sources_of, lambda s: (count_of(counts, s) + CHUNK - 1) >> 7, lambda b: count_of(counts, b), BOXES,
        fa, pay, fb, pay, out, out if two_way else None, tiles, flips, steps, owner, filled,
    )
    acc[...] = out[0:BOXES]
    done[...] = jnp.zeros_like(done)


def outer_kernel(counts, fb, pay, acc_self, acc_in, after, halo0, halo1, halo2, near, b0, b1, b2, probe_sums,
                 fa, vec, plus, back, tiles, flips, steps, owner, filled, chunk_no):
    halos = (halo0, halo1, halo2)
    points = fb.shape[-1]
    row = row_ids(points)
    plus[...] = jnp.zeros_like(plus)
    back[...] = jnp.zeros_like(back)
    sources = {b: [] for b in range(BOXES)}
    spare = 12
    for axis in range(3):
        halo = halos[axis]
        name = ("gx", "gy", "gz")[axis]
        at_edge = lax.axis_index(name) == lax.axis_size(name) - 1
        targets = face_boxes(axis, 1)
        for i in range(4):
            s = axis * 4 + i
            sources[targets[i]].append(s)
            tail = halo[i, 32:48, :].astype(F32)
            rows_a = tail[0:8]
            pos = rows_a + pltpu.roll(rows_a, 5, 0) + tail[8:16]
            pos = jnp.where(row < 3, pos + jnp.where(row == axis, 2.0, 0.0), 0.0)
            feats = source_rows(pos, row)
            fa[s] = feats
            if s == 0:
                fa[spare] = feats
            vec[s] = halo[i, 0:32, :]
            chunk_no[s] = jnp.where(at_edge, 0, jnp.max(rows_a[6:7, 0:128]).astype(jnp.int32))
    vec[spare] = jnp.zeros_like(vec[spare])
    order = [b for b in range(BOXES) if sources[b]]
    run_steps(
        order, lambda b: sources[b], lambda s: chunk_no[s], lambda b: count_of(counts, b), spare,
        fa, vec, fb, pay, plus, back, tiles, flips, steps, owner, filled,
    )
    total = jnp.zeros((32, 128), F32)
    for b in range(BOXES):
        extra = plus[b]
        base = acc_self[b] + acc_in[b]
        near[b] = base + extra
        weighted = pay[b, 0:32, :].astype(F32) * (base + 2.0 * extra)
        for j in range(points // 128):
            total = total + weighted[:, j * 128:(j + 1) * 128]
    probe_sums[...] = total
    for axis, ref in enumerate((b0, b1, b2)):
        ref[...] = back[4 * axis:4 * axis + 4]


def local_kernel(counts, req_box, req_tgt, here, there, momf, probe_sums, loc, sums, slab, far_acc, live, sems):
    first_copy = pltpu.make_async_copy(here, slab.at[pl.ds(0, 32)], sems.at[0])
    second_copy = pltpu.make_async_copy(there, slab.at[pl.ds(32, 32)], sems.at[1])
    first_copy.start()
    second_copy.start()
    my_y = lax.axis_index("gy")
    my_z = lax.axis_index("gz")
    far_acc[...] = jnp.zeros_like(far_acc)

    def keep(i, n):
        live[n] = i
        return n + (req_box[i >> 6, i & 63] >= 0).astype(jnp.int32)

    used = lax.fori_loop(0, 128, keep, jnp.int32(0))
    shape = (64, 64)
    source_q = lax.broadcasted_iota(jnp.int32, shape, 1)
    target_q = lax.broadcasted_iota(jnp.int32, shape, 0)

    def node(index):
        value = jnp.full(shape, 0.5 + 0.5 * NODES[0], F32)
        for a in range(1, ORDER):
            value = jnp.where(index == a, 0.5 + 0.5 * NODES[a], value)
        return value

    gaps = [node((source_q >> s) & 3) - node((target_q >> s) & 3) for s in (4, 2, 0)]
    group = lax.broadcasted_iota(jnp.int32, (64, 256), 1) >> 5
    first_copy.wait()
    second_copy.wait()

    def step(g, carry):
        for u in range(8):
            k = g * 8 + u
            i = live[jnp.minimum(k, used - 1)]
            peer = i & 63
            box = req_box[i >> 6, peer]
            tgt = req_tgt[i >> 6, peer]
            peer_y = peer >> 4
            peer_z = peer & 15
            dx = (box >> 2) - (tgt >> 2)
            dy = (peer_y - my_y) * 2 + ((box >> 1) & 1) - ((tgt >> 1) & 1)
            dz = (peer_z - my_z) * 2 + (box & 1) - (tgt & 1)
            ex = gaps[0] + dx.astype(F32)
            ey = gaps[1] + dy.astype(F32)
            ez = gaps[2] + dz.astype(F32)
            coupling = lax.rsqrt(1.0 + ex * ex + ey * ey + ez * ez).astype(BF16)
            rel_y = peer_y ^ my_y
            rel_z = peer_z ^ my_z
            at = (rel_z & 1) * 32 + ((rel_z >> 1) & 3) * 8 + rel_y * 2 + (rel_z >> 3)
            term = jnp.dot(coupling, slab[at], preferred_element_type=F32)
            wanted = jnp.where(k < used, box, -1)
            far_acc[tgt] += jnp.where(group == wanted, term, 0.0)
        return carry

    lax.fori_loop(0, (used + 7) >> 3, step, 0)
    lane = lax.broadcasted_iota(jnp.int32, (64, 128), 1)
    far_sums = jnp.zeros((64, 128), F32)
    live_points = jnp.int32(0)
    for b in range(BOXES):
        wide = far_acc[b]
        half = wide[:, 0:128] + wide[:, 128:256]
        half = half + pltpu.roll(half, 64, 1)
        half = half + pltpu.roll(half, 32, 1)
        rounded = half.astype(BF16)
        loc[b] = rounded
        moment = momf[:, (b // 4) * 128:(b // 4 + 1) * 128]
        far_sums = far_sums + jnp.where((lane >> 5) == b % 4, rounded.astype(F32) * moment, 0.0)
        live_points = live_points + count_of(counts, b)
    folded = jnp.sum(far_sums, axis=0, keepdims=True)
    folded = folded + pltpu.roll(folded, 64, 1)
    folded = folded + pltpu.roll(folded, 32, 1)
    lane32 = lax.broadcasted_iota(jnp.int32, (32, 128), 1)
    row32 = lax.broadcasted_iota(jnp.int32, (32, 128), 0)
    per_probe = jnp.sum(probe_sums[...], axis=1, keepdims=True)
    flat = jnp.sum(jnp.where(lane32 == row32, per_probe, 0.0), axis=0, keepdims=True)
    sums[...] = jnp.where(lane32[0:1] < 32, flat + folded, jnp.where(lane32[0:1] == 32, live_points.astype(F32), 0.0))


def total_kernel(counts, near, r0, r1, r2, loc, tab, kv, done):
    points = tab.shape[-1]
    lane = lax.broadcasted_iota(jnp.int32, (1, points), 1)
    for b in range(BOXES):
        place = (b // 4, b // 2 % 2, b % 2)
        far = lax.dot_general(loc[b][:, 0:32], tab[b], (((0,), (0,)), ((), ())), preferred_element_type=F32)
        total = near[b] + far
        for axis, ref in enumerate((r0, r1, r2)):
            if place[axis] == 0:
                other = [d for d in range(3) if d != axis]
                total = total + ref[place[other[0]] * 2 + place[other[1]]]
        if b == 0:
            done[...] = jnp.zeros_like(done)
        kv[b] = jnp.where(lane < count_of(counts, b), total * (1.0 / math.sqrt(7.0 * points)), 0.0).astype(BF16)


def quad_kernel(gathered, after, quad):
    lane = lax.broadcasted_iota(jnp.int32, (1, 128), 1)
    whole = jnp.sum(gathered[...], axis=0, keepdims=True)
    live_points = jnp.sum(jnp.where(lane == 32, whole, 0.0), axis=1, keepdims=True)
    scaled = whole * (1.0 / math.sqrt(7.0 * 1024)) / live_points
    quad[...] = scaled[0, 0:32]


VMEM = pl.BlockSpec(memory_space=pltpu.VMEM)
SMEM = pl.BlockSpec(memory_space=pltpu.SMEM)
ANY = pl.BlockSpec(memory_space=pl.ANY)
PARAMS = pltpu.CompilerParams(vmem_limit_bytes=20 * 2**20)


COST = pl.CostEstimate(flops=12 * 10**9, bytes_accessed=4 * 2**20, transcendentals=10**7)


def join(name, *arrays):
    return pl.pallas_call(
        lambda *refs: None,
        out_shape=[jax.ShapeDtypeStruct(a.shape, a.dtype) for a in arrays],
        in_specs=[ANY] * len(arrays),
        out_specs=[ANY] * len(arrays),
        input_output_aliases={i: i for i in range(len(arrays))},
        compiler_params=pltpu.CompilerParams(vmem_limit_bytes=2**20),
        name=name,
    )(*arrays)


def xor_permute(value, axis, bits):
    count = lax.axis_size(axis)
    return lax.ppermute(value, axis, [(i, i ^ bits) for i in range(count)])


def shards(offsets, probes, counts, req_box, req_tgt):
    points = offsets.shape[-1]
    shape = jax.ShapeDtypeStruct
    face = shape((4, ROWS, points), BF16)
    pay, fa, fb, tab, mom, momf, *faces = pl.pallas_call(
        prep_kernel,
        out_shape=[
            shape((BOXES + 1, ROWS, points), BF16),
            shape((BOXES + 1, FEATS, points), BF16),
            shape((BOXES, FEATS, points), BF16),
            shape((BOXES, 64, points), BF16),
            shape((64, 256), BF16),
            shape((64, 256), F32),
        ] + [face] * 3,
        in_specs=[SMEM, VMEM, VMEM],
        out_specs=[VMEM] * 9,
        scratch_shapes=[
            pltpu.VMEM((8, points), F32),
        ],
        compiler_params=PARAMS,
        name="prep",
    )(counts, jnp.swapaxes(offsets, 2, 3), probes)

    acc_shape = shape((BOXES, 32, points), F32)
    lists = [
        pltpu.VMEM((2, 2 * CHUNK, points), BF16),
        pltpu.VMEM((2, 2 * CHUNK, FEATS), BF16),
        pltpu.SMEM((len(WIDTHS) * REGION,), jnp.int32),
        pltpu.SMEM((len(WIDTHS) * REGION // 2,), jnp.int32),
        pltpu.SMEM((8,), jnp.int32),
    ]

    def inner(name, targets, sources_of, two_way, acc, after):
        has_acc = acc is not None

        def kernel(*refs):
            refs = list(refs)
            head = refs[:4]
            rest = refs[4:]
            acc_ref = rest.pop(0) if has_acc else None
            inner_kernel(targets, sources_of, two_way, *head, acc_ref, *rest)

        args = [counts, fa, pay, fb] + ([acc] if has_acc else []) + [after]
        return pl.pallas_call(
            kernel,
            out_shape=[acc_shape, shape((8, 128), F32)],
            in_specs=[SMEM, VMEM, VMEM, VMEM] + [VMEM] * has_acc + [ANY],
            out_specs=[VMEM, VMEM],
            scratch_shapes=[pltpu.VMEM((BOXES + 1, 32, points), F32)] + lists,
            compiler_params=PARAMS,
            cost_estimate=COST,
            name=name,
        )(*args)

    def along(axis, value, step):
        name = ("gx", "gy", "gz")[axis]
        size = lax.axis_size(name)
        return lax.ppermute(value, name, [(i, (i + step) % size) for i in range(size)])

    block = mom.reshape(1, 64, 256)
    twin = xor_permute(block, "gz", 8)
    got = [along(axis, faces[axis], -1) for axis in range(3)]
    acc_self, tick = inner("self_tiles", list(range(BOXES)), lambda b: [b], False, None, mom)
    tick, twin, got[0], got[1] = join("join_first", tick, twin, got[0], got[1])
    block = jnp.concatenate([block, twin], axis=0)
    more = [xor_permute(block, "gy", k) for k in (1, 2, 3)]
    acc, tick = inner("pairs_low", [1, 2, 4, 3], lambda b: INNER[b], True, None, tick)
    tick, got[2], *more = join("join_second", tick, got[2], *more)
    block = jnp.concatenate([block] + more, axis=0)
    more = [xor_permute(block, "gz", 2 * k) for k in (1, 2, 3)]
    acc, tick = inner("pairs_high", [5, 6, 7], lambda b: INNER[b], True, acc, tick)
    tick, *more = join("join_third", tick, *more)
    block = jnp.concatenate([block] + more, axis=0)
    other = xor_permute(block, "gz", 1)
    near, *backs, probe_sums = pl.pallas_call(
        outer_kernel,
        out_shape=[acc_shape] + [shape((4, 32, points), F32)] * 3 + [shape((32, 128), F32)],
        in_specs=[SMEM, VMEM, VMEM, VMEM, VMEM, ANY, VMEM, VMEM, VMEM],
        out_specs=[VMEM] * 5,
        scratch_shapes=[
            pltpu.VMEM((13, FEATS, points), BF16),
            pltpu.VMEM((13, 32, points), BF16),
            pltpu.VMEM((BOXES, 32, points), F32),
            pltpu.VMEM((13, 32, points), F32),
        ] + lists + [pltpu.SMEM((16,), jnp.int32)],
        compiler_params=PARAMS,
        cost_estimate=COST,
        name="face_tiles",
    )(counts, fb, pay, acc_self, acc, tick, *got)
    returned = [along(axis, backs[axis], 1) for axis in range(3)]
    loc, sums = pl.pallas_call(
        local_kernel,
        out_shape=[shape((BOXES, 64, 128), BF16), shape((1, 128), F32)],
        in_specs=[SMEM, SMEM, SMEM, ANY, ANY, VMEM, VMEM],
        out_specs=[VMEM, VMEM],
        scratch_shapes=[
            pltpu.VMEM((64, 64, 256), BF16),
            pltpu.VMEM((BOXES, 64, 256), F32),
            pltpu.SMEM((136,), jnp.int32),
            pltpu.SemaphoreType.DMA((2,)),
        ],
        compiler_params=PARAMS,
        name="locals",
    )(counts, *[jnp.swapaxes(r, 3, 4).reshape(2, 64) for r in (req_box, req_tgt)], block, other, momf, probe_sums)
    devices = lax.axis_size("gx") * lax.axis_size("gy") * lax.axis_size("gz")
    spread = jnp.broadcast_to(sums, (devices, 128))
    gathered = lax.all_to_all(spread, ("gx", "gy", "gz"), 0, 0, tiled=True)
    kv, total_tick = pl.pallas_call(
        total_kernel,
        out_shape=[shape((BOXES, 32, points), BF16), shape((8, 128), F32)],
        in_specs=[SMEM] + [VMEM] * 6,
        out_specs=[VMEM, VMEM],
        compiler_params=PARAMS,
        cost_estimate=COST,
        name="total",
    )(counts, near, *returned, loc, tab)
    quad = pl.pallas_call(
        quad_kernel,
        out_shape=shape((32,), F32),
        in_specs=[VMEM, ANY],
        out_specs=VMEM,
        compiler_params=pltpu.CompilerParams(vmem_limit_bytes=2**21),
        name="quad",
    )(gathered, total_tick)
    return kv.reshape(probes.shape), quad


def solution(mesh):
    placed = (
        P("gx", "gy", "gz", None, None),
        P("gx", "gy", "gz", None, None),
        P("gx", "gy", "gz"),
        P("gx", "gy", "gz", None, None),
        P("gx", "gy", "gz", None, None),
    )
    return jax.shard_map(
        shards,
        mesh=mesh,
        in_specs=placed,
        out_specs=(P("gx", "gy", "gz", None, None), P()),
        check_vma=False,
    )
```

```python
import functools
import math

import jax
import jax.numpy as jnp
from jax import lax
from jax.experimental import pallas as pl
from jax.experimental.pallas import tpu as pltpu
from jax.sharding import PartitionSpec as P

ORDER = 4
CHUNK = 128
BOXES = 8
FEATS = 48
ROWS = 48
F32 = jnp.float32
BF16 = jnp.bfloat16
NODES = [math.cos((2.0 * a + 1.0) * math.pi / (2.0 * ORDER)) for a in range(ORDER)]


def box_id(axis, at, first, second):
    place = [0, 0, 0]
    rest = [d for d in range(3) if d != axis]
    place[axis] = at
    place[rest[0]] = first
    place[rest[1]] = second
    return (place[0] * 2 + place[1]) * 2 + place[2]


def face_boxes(axis, at):
    return [box_id(axis, at, i, j) for i in range(2) for j in range(2)]


def split3(value):
    high = value.astype(BF16).astype(F32)
    rest = value - high
    mid = rest.astype(BF16).astype(F32)
    return high, mid, rest - mid


def row_ids(points):
    return lax.broadcasted_iota(jnp.int32, (8, points), 0)


def source_rows(pos, row):
    p1, p2, p3 = split3(pos)
    n1, n2, n3 = split3(1.0 + jnp.sum(pos * pos, axis=0, keepdims=True))
    s1 = jnp.where(row < 3, p1, jnp.where(row == 3, n1, jnp.where(row == 4, n2, jnp.where(row == 5, n3, 1.0))))
    s2 = p2 + pltpu.roll(p3, 3, 0)
    return jnp.concatenate([s1, s1, s2, s2, s1, jnp.zeros_like(s1)], axis=0).astype(BF16)


def target_rows(pos, row):
    p1, p2, p3 = split3(-2.0 * pos)
    m1, m2, m3 = split3(jnp.sum(pos * pos, axis=0, keepdims=True))
    qa = jnp.where(row < 3, p1, jnp.where(row < 6, 1.0, jnp.where(row == 6, m1, m2)))
    qb = jnp.where(row < 3, p2, jnp.where(row == 6, m3, 0.0))
    qc = p1 + pltpu.roll(p1, 3, 0)
    return jnp.concatenate([qa, qb, qc, p2, p3, jnp.zeros_like(qa)], axis=0).astype(BF16)


def prep_kernel(counts, offs, probes, pay, fa, fb, tab, mom, momf, f0, f1, f2, pad):
    points = offs.shape[-1]
    row = row_ids(points)
    lane = lax.broadcasted_iota(jnp.int32, (1, points), 1)
    faces = (f0, f1, f2)
    pay[BOXES] = jnp.zeros_like(pay[BOXES])
    for k in range(BOXES):
        place = (k // 4, k // 2 % 2, k % 2)
        pad[...] = jnp.zeros_like(pad)
        for d in range(3):
            pad[d:d + 1, :] = offs[place[0], place[1], d, place[2]:place[2] + 1, :]
        off = pad[...]
        shift = jnp.where(row == 0, place[0] - 1.0, jnp.where(row == 1, place[1] - 1.0, jnp.where(row == 2, place[2] - 1.0, 0.0)))
        pos = off + shift
        src = source_rows(pos, row)
        fa[k] = src
        fb[k] = target_rows(pos, row)
        if k == 0:
            fa[BOXES] = src
        count = counts[place]
        chunks = ((count + CHUNK - 1) // CHUNK).astype(F32)
        p1, p2, p3 = split3(pos)
        rows_a = jnp.where(row == 6, chunks, p1 + pltpu.roll(p2, 3, 0))
        tail = jnp.concatenate([rows_a, p3], axis=0).astype(BF16)
        vec = jnp.where(lane < count, probes[place].astype(F32), 0.0).astype(BF16)
        pay[k, 0:32, :] = vec
        pay[k, 32:48, :] = tail
        for axis in range(3):
            if place[axis] == 0:
                other = [d for d in range(3) if d != axis]
                slot = place[other[0]] * 2 + place[other[1]]
                faces[axis][slot, 0:32, :] = vec
                faces[axis][slot, 32:48, :] = tail
        unit = 2.0 * off - 1.0
        t2 = 2.0 * unit * unit - 1.0
        t3 = 2.0 * unit * t2 - unit
        weights = []
        for c in NODES:
            e2 = 2.0 * c * c - 1.0
            e3 = 2.0 * c * e2 - c
            weights.append(0.25 + 0.5 * (c * unit + e2 * t2 + e3 * t3))
        third = jnp.zeros_like(off)
        for d in range(ORDER):
            third = jnp.where(row % 4 == d, weights[d][2:3, :], third)
        seconds = []
        for half in range(2):
            seconds.append(jnp.where(row < 4, weights[2 * half][1:2, :], weights[2 * half + 1][1:2, :]))
        parts = []
        for a in range(ORDER):
            for half in range(2):
                parts.append(weights[a][0:1, :] * seconds[half] * third)
        table = jnp.concatenate(parts, axis=0).astype(BF16)
        tab[k] = table
        moment = lax.dot_general(table, vec, (((1,), (1,)), ((), ())), preferred_element_type=F32)
        momf[:, k * 32:(k + 1) * 32] = moment
    mom[...] = momf[...].astype(BF16)


WIDTHS = (768, 1024)
REGION = 160


def run_steps(targets, sources_of, chunks_of, width_of, dummy, fa, vec, fb, own, out, back, tiles, flips, steps, owner, filled):
    for c in range(len(WIDTHS)):
        filled[c] = 0
    for b in targets:
        count_b = width_of(b)
        kind = jnp.int32(0)
        for width in WIDTHS[:-1]:
            kind = kind + (count_b > width).astype(jnp.int32)
        base = kind * REGION
        at = base + filled[kind]
        for s in sources_of(b):
            for c in range(8):
                steps[at + c] = s * 8 + c
            for c in range(5):
                owner[(at >> 1) + c] = b
            at = at + chunks_of(s)
        steps[at] = dummy * 8
        at = at + (at & 1)
        filled[kind] = at - base
    for c in range(len(WIDTHS)):
        end = c * REGION + filled[c]
        for extra in range(8):
            steps[end + extra] = dummy * 8
            owner[(end + extra) >> 1] = targets[0]

    def columns(index):
        return pl.ds(pl.multiple_of((index & 7) * CHUNK, CHUNK), CHUNK)

    for c, width in enumerate(WIDTHS):
        first_step = c * (REGION // 2)
        total = filled[c] >> 1

        def flip(t, slot):
            for h in range(2):
                index = steps[2 * t + h]
                flips[slot, h * CHUNK:(h + 1) * CHUNK, :] = fa[index >> 3, :, columns(index)].T

        def make(t, slot, width=width):
            target = fb[owner[t], :, 0:width]
            squares = jnp.dot(flips[slot], target, preferred_element_type=F32)
            tiles[slot, :, 0:width] = lax.rsqrt(squares).astype(BF16)

        def use(t, slot, width=width):
            b = owner[t]
            first = steps[2 * t]
            second = steps[2 * t + 1]
            tile = tiles[slot, :, 0:width]
            both = jnp.concatenate([vec[first >> 3, 0:32, columns(first)], vec[second >> 3, 0:32, columns(second)]], axis=1)
            out[b, :, 0:width] += jnp.dot(both, tile, preferred_element_type=F32)
            if back is not None:
                sent = lax.dot_general(own[b, 0:32, 0:width], tile, (((1,), (1,)), ((), ())), preferred_element_type=F32)
                back[first >> 3, :, columns(first)] += sent[:, 0:CHUNK]
                back[second >> 3, :, columns(second)] += sent[:, CHUNK:]

        @pl.when(total > 0)
        def _(flip=flip, make=make, use=use, first_step=first_step, total=total):
            flip(first_step, 0)
            flip(first_step + 1, 1)
            make(first_step, 0)

            def body(k, carry):
                t = first_step + 2 * k
                make(t + 1, 1)
                flip(t + 2, 0)
                use(t, 0)
                make(t + 2, 0)
                flip(t + 3, 1)
                use(t + 1, 1)
                return carry

            lax.fori_loop(0, (total + 1) >> 1, body, 0)


INNER = {4: (0,), 2: (0,), 1: (0,), 6: (2, 4), 5: (1, 4), 3: (1, 2), 7: (3, 5, 6)}


def count_of(counts, k):
    return counts[k // 4, k // 2 % 2, k % 2]


def inner_kernel(targets, sources_of, two_way, counts, fa, pay, fb, acc_in, after, out, done, tiles, flips, steps, owner, filled):
    if acc_in is None:
        out[...] = jnp.zeros_like(out)
    else:
        out[...] = acc_in[...]
    run_steps(
        targets, sources_of, lambda s: (count_of(counts, s) + CHUNK - 1) >> 7, lambda b: count_of(counts, b), BOXES,
        fa, pay, fb, pay, out, out if two_way else None, tiles, flips, steps, owner, filled,
    )
    done[...] = jnp.zeros_like(done)


def outer_kernel(counts, fb, pay, acc_self, acc_in, after, halo0, halo1, halo2, near, b0, b1, b2, probe_sums,
                 fa, vec, plus, back, tiles, flips, steps, owner, filled, chunk_no):
    halos = (halo0, halo1, halo2)
    points = fb.shape[-1]
    row = row_ids(points)
    plus[...] = jnp.zeros_like(plus)
    back[...] = jnp.zeros_like(back)
    sources = {b: [] for b in range(BOXES)}
    spare = 12
    for axis in range(3):
        halo = halos[axis]
        name = ("gx", "gy", "gz")[axis]
        at_edge = lax.axis_index(name) == lax.axis_size(name) - 1
        targets = face_boxes(axis, 1)
        for i in range(4):
            s = axis * 4 + i
            sources[targets[i]].append(s)
            tail = halo[i, 32:48, :].astype(F32)
            rows_a = tail[0:8]
            pos = rows_a + pltpu.roll(rows_a, 5, 0) + tail[8:16]
            pos = jnp.where(row < 3, pos + jnp.where(row == axis, 2.0, 0.0), 0.0)
            feats = source_rows(pos, row)
            fa[s] = feats
            if s == 0:
                fa[spare] = feats
            vec[s] = halo[i, 0:32, :]
            chunk_no[s] = jnp.where(at_edge, 0, jnp.max(rows_a[6:7, 0:128]).astype(jnp.int32))
    vec[spare] = jnp.zeros_like(vec[spare])
    order = [b for b in range(BOXES) if sources[b]]
    run_steps(
        order, lambda b: sources[b], lambda s: chunk_no[s], lambda b: count_of(counts, b), spare,
        fa, vec, fb, pay, plus, back, tiles, flips, steps, owner, filled,
    )
    total = jnp.zeros((32, 128), F32)
    for b in range(BOXES):
        extra = plus[b]
        base = acc_self[b] + acc_in[b]
        near[b] = base + extra
        weighted = pay[b, 0:32, :].astype(F32) * (base + 2.0 * extra)
        for j in range(points // 128):
            total = total + weighted[:, j * 128:(j + 1) * 128]
    probe_sums[...] = total
    for axis, ref in enumerate((b0, b1, b2)):
        ref[...] = back[4 * axis:4 * axis + 4]


def local_kernel(counts, req_box, req_tgt, here, there, momf, probe_sums, loc, sums, slab, far_acc, live, sems):
    first_copy = pltpu.make_async_copy(here, slab.at[pl.ds(0, 32)], sems.at[0])
    second_copy = pltpu.make_async_copy(there, slab.at[pl.ds(32, 32)], sems.at[1])
    first_copy.start()
    second_copy.start()
    my_y = lax.axis_index("gy")
    my_z = lax.axis_index("gz")
    far_acc[...] = jnp.zeros_like(far_acc)

    def keep(i, n):
        live[n] = i
        return n + (req_box[i >> 6, i & 63] >= 0).astype(jnp.int32)

    used = lax.fori_loop(0, 128, keep, jnp.int32(0))
    shape = (64, 64)
    source_q = lax.broadcasted_iota(jnp.int32, shape, 1)
    target_q = lax.broadcasted_iota(jnp.int32, shape, 0)

    def node(index):
        value = jnp.full(shape, 0.5 + 0.5 * NODES[0], F32)
        for a in range(1, ORDER):
            value = jnp.where(index == a, 0.5 + 0.5 * NODES[a], value)
        return value

    gaps = [node((source_q >> s) & 3) - node((target_q >> s) & 3) for s in (4, 2, 0)]
    group = lax.broadcasted_iota(jnp.int32, (64, 256), 1) >> 5
    first_copy.wait()
    second_copy.wait()

    def step(g, carry):
        for u in range(8):
            k = g * 8 + u
            i = live[jnp.minimum(k, used - 1)]
            peer = i & 63
            box = req_box[i >> 6, peer]
            tgt = req_tgt[i >> 6, peer]
            peer_y = peer >> 4
            peer_z = peer & 15
            dx = (box >> 2) - (tgt >> 2)
            dy = (peer_y - my_y) * 2 + ((box >> 1) & 1) - ((tgt >> 1) & 1)
            dz = (peer_z - my_z) * 2 + (box & 1) - (tgt & 1)
            ex = gaps[0] + dx.astype(F32)
            ey = gaps[1] + dy.astype(F32)
            ez = gaps[2] + dz.astype(F32)
            coupling = lax.rsqrt(1.0 + ex * ex + ey * ey + ez * ez).astype(BF16)
            rel_y = peer_y ^ my_y
            rel_z = peer_z ^ my_z
            at = (rel_z & 1) * 32 + ((rel_z >> 1) & 3) * 8 + rel_y * 2 + (rel_z >> 3)
            term = jnp.dot(coupling, slab[at], preferred_element_type=F32)
            wanted = jnp.where(k < used, box, -1)
            far_acc[tgt] += jnp.where(group == wanted, term, 0.0)
        return carry

    lax.fori_loop(0, (used + 7) >> 3, step, 0)
    lane = lax.broadcasted_iota(jnp.int32, (64, 128), 1)
    far_sums = jnp.zeros((64, 128), F32)
    live_points = jnp.int32(0)
    for b in range(BOXES):
        wide = far_acc[b]
        half = wide[:, 0:128] + wide[:, 128:256]
        half = half + pltpu.roll(half, 64, 1)
        half = half + pltpu.roll(half, 32, 1)
        rounded = half.astype(BF16)
        loc[b] = rounded
        moment = momf[:, (b // 4) * 128:(b // 4 + 1) * 128]
        far_sums = far_sums + jnp.where((lane >> 5) == b % 4, rounded.astype(F32) * moment, 0.0)
        live_points = live_points + count_of(counts, b)
    folded = jnp.sum(far_sums, axis=0, keepdims=True)
    folded = folded + pltpu.roll(folded, 64, 1)
    folded = folded + pltpu.roll(folded, 32, 1)
    lane32 = lax.broadcasted_iota(jnp.int32, (32, 128), 1)
    row32 = lax.broadcasted_iota(jnp.int32, (32, 128), 0)
    per_probe = jnp.sum(probe_sums[...], axis=1, keepdims=True)
    flat = jnp.sum(jnp.where(lane32 == row32, per_probe, 0.0), axis=0, keepdims=True)
    row_sums = jnp.where(lane32[0:1] < 32, flat + folded, jnp.where(lane32[0:1] == 32, live_points.astype(F32), 0.0))
    sums[...] = jnp.broadcast_to(row_sums.reshape(1, 1, 128), sums.shape)


def total_kernel(counts, near, r2, r0, r1, loc, tab, kv, done):
    points = tab.shape[-1]
    lane = lax.broadcasted_iota(jnp.int32, (1, points), 1)
    for b in range(BOXES):
        place = (b // 4, b // 2 % 2, b % 2)
        far = lax.dot_general(loc[b][:, 0:32], tab[b], (((0,), (0,)), ((), ())), preferred_element_type=F32)
        total = near[b] + far
        for axis, ref in enumerate((r0, r1, r2)):
            if place[axis] == 0:
                other = [d for d in range(3) if d != axis]
                total = total + ref[place[other[0]] * 2 + place[other[1]]]
        if b == 0:
            done[...] = jnp.zeros_like(done)
        kv[b] = jnp.where(lane < count_of(counts, b), total * (1.0 / math.sqrt(7.0 * points)), 0.0).astype(BF16)


def quad_kernel(gathered, after, quad):
    lane = lax.broadcasted_iota(jnp.int32, (1, 128), 1)
    whole = jnp.sum(gathered[...], axis=0)
    live_points = jnp.sum(jnp.where(lane == 32, whole, 0.0), axis=1, keepdims=True)
    scaled = whole * (1.0 / math.sqrt(7.0 * 1024)) / live_points
    quad[...] = scaled[0, 0:32]


VMEM = pl.BlockSpec(memory_space=pltpu.VMEM)
SMEM = pl.BlockSpec(memory_space=pltpu.SMEM)
ANY = pl.BlockSpec(memory_space=pl.ANY)
PARAMS = pltpu.CompilerParams(vmem_limit_bytes=20 * 2**20)


COST = pl.CostEstimate(flops=12 * 10**9, bytes_accessed=4 * 2**20, transcendentals=10**7)


def join(name, *arrays):
    return pl.pallas_call(
        lambda *refs: None,
        out_shape=[jax.ShapeDtypeStruct(a.shape, a.dtype) for a in arrays],
        in_specs=[ANY] * len(arrays),
        out_specs=[ANY] * len(arrays),
        input_output_aliases={i: i for i in range(len(arrays))},
        compiler_params=pltpu.CompilerParams(vmem_limit_bytes=2**20),
        name=name,
    )(*arrays)


def xor_permute(value, axis, bits):
    count = lax.axis_size(axis)
    return lax.ppermute(value, axis, [(i, i ^ bits) for i in range(count)])


def shards(offsets, probes, counts, req_box, req_tgt):
    points = offsets.shape[-1]
    shape = jax.ShapeDtypeStruct
    face = shape((4, ROWS, points), BF16)
    pay, fa, fb, tab, mom, momf, *faces = pl.pallas_call(
        prep_kernel,
        out_shape=[
            shape((BOXES + 1, ROWS, points), BF16),
            shape((BOXES + 1, FEATS, points), BF16),
            shape((BOXES, FEATS, points), BF16),
            shape((BOXES, 64, points), BF16),
            shape((64, 256), BF16),
            shape((64, 256), F32),
        ] + [face] * 3,
        in_specs=[SMEM, VMEM, VMEM],
        out_specs=[VMEM] * 9,
        scratch_shapes=[
            pltpu.VMEM((8, points), F32),
        ],
        compiler_params=PARAMS,
        name="prep",
    )(counts, jnp.swapaxes(offsets, 2, 3), probes)

    acc_shape = shape((BOXES, 32, points), F32)
    lists = [
        pltpu.VMEM((2, 2 * CHUNK, points), BF16),
        pltpu.VMEM((2, 2 * CHUNK, FEATS), BF16),
        pltpu.SMEM((len(WIDTHS) * REGION,), jnp.int32),
        pltpu.SMEM((len(WIDTHS) * REGION // 2,), jnp.int32),
        pltpu.SMEM((8,), jnp.int32),
    ]

    def inner(name, targets, sources_of, two_way, acc, after):
        has_acc = acc is not None

        def kernel(*refs):
            refs = list(refs)
            head = refs[:4]
            rest = refs[4:]
            acc_ref = rest.pop(0) if has_acc else None
            inner_kernel(targets, sources_of, two_way, *head, acc_ref, *rest)

        args = [counts, fa, pay, fb] + ([acc] if has_acc else []) + [after]
        return pl.pallas_call(
            kernel,
            out_shape=[shape((BOXES + 1, 32, points), F32), shape((8, 128), F32)],
            in_specs=[SMEM, VMEM, VMEM, VMEM] + [VMEM] * has_acc + [ANY],
            out_specs=[VMEM, VMEM],
            scratch_shapes=lists,
            compiler_params=PARAMS,
            cost_estimate=COST,
            name=name,
        )(*args)

    def along(axis, value, step):
        name = ("gx", "gy", "gz")[axis]
        size = lax.axis_size(name)
        return lax.ppermute(value, name, [(i, (i + step) % size) for i in range(size)])

    block = mom.reshape(1, 64, 256)
    twin = xor_permute(block, "gz", 8)
    got = [None] * 3
    for axis in (2, 0, 1):
        got[axis] = along(axis, faces[axis], -1)
    acc_self, tick = inner("self_tiles", list(range(BOXES)), lambda b: [b], False, None, mom)
    tick, twin, got[0], got[1] = join("join_first", tick, twin, got[0], got[1])
    block = jnp.concatenate([block, twin], axis=0)
    more = [xor_permute(block, "gy", k) for k in (1, 2, 3)]
    acc, tick = inner("pairs_low", [1, 2, 4, 3], lambda b: INNER[b], True, None, tick)
    tick, got[2], *more = join("join_second", tick, got[2], *more)
    block = jnp.concatenate([block] + more, axis=0)
    more = [xor_permute(block, "gz", 2 * k) for k in (1, 2, 3)]
    acc, tick = inner("pairs_high", [5, 6, 7], lambda b: INNER[b], True, acc, tick)
    tick, *more = join("join_third", tick, *more)
    block = jnp.concatenate([block] + more, axis=0)
    other = xor_permute(block, "gz", 1)
    near, *backs, probe_sums = pl.pallas_call(
        outer_kernel,
        out_shape=[acc_shape] + [shape((4, 32, points), F32)] * 3 + [shape((32, 128), F32)],
        in_specs=[SMEM, VMEM, VMEM, VMEM, VMEM, ANY, VMEM, VMEM, VMEM],
        out_specs=[VMEM] * 5,
        scratch_shapes=[
            pltpu.VMEM((13, FEATS, points), BF16),
            pltpu.VMEM((13, 32, points), BF16),
            pltpu.VMEM((BOXES, 32, points), F32),
            pltpu.VMEM((13, 32, points), F32),
        ] + lists + [pltpu.SMEM((16,), jnp.int32)],
        compiler_params=PARAMS,
        cost_estimate=COST,
        name="face_tiles",
    )(counts, fb, pay, acc_self, acc, tick, *got)
    returned = [None] * 3
    for axis in (2, 0, 1):
        returned[axis] = along(axis, backs[axis], 1)
    devices = lax.axis_size("gx") * lax.axis_size("gy") * lax.axis_size("gz")
    loc, sums = pl.pallas_call(
        local_kernel,
        out_shape=[shape((BOXES, 64, 128), BF16), shape((devices, 1, 128), F32)],
        in_specs=[SMEM, SMEM, SMEM, ANY, ANY, VMEM, VMEM],
        out_specs=[VMEM, VMEM],
        scratch_shapes=[
            pltpu.VMEM((64, 64, 256), BF16),
            pltpu.VMEM((BOXES, 64, 256), F32),
            pltpu.SMEM((136,), jnp.int32),
            pltpu.SemaphoreType.DMA((2,)),
        ],
        compiler_params=PARAMS,
        name="locals",
    )(counts, *[jnp.swapaxes(r, 3, 4).reshape(2, 64) for r in (req_box, req_tgt)], block, other, momf, probe_sums)
    gathered = lax.all_to_all(sums, ("gx", "gy", "gz"), 0, 0, tiled=True)
    kv, total_tick = pl.pallas_call(
        total_kernel,
        out_shape=[shape((BOXES, 32, points), BF16), shape((8, 128), F32)],
        in_specs=[SMEM] + [VMEM] * 6,
        out_specs=[VMEM, VMEM],
        compiler_params=PARAMS,
        cost_estimate=COST,
        name="total",
    )(counts, near, returned[2], returned[0], returned[1], loc, tab)
    quad = pl.pallas_call(
        quad_kernel,
        out_shape=shape((32,), F32),
        in_specs=[VMEM, ANY],
        out_specs=VMEM,
        compiler_params=pltpu.CompilerParams(vmem_limit_bytes=2**21),
        name="quad",
    )(gathered, total_tick)
    return kv.reshape(probes.shape), quad


def solution(mesh):
    placed = (
        P("gx", "gy", "gz", None, None),
        P("gx", "gy", "gz", None, None),
        P("gx", "gy", "gz"),
        P("gx", "gy", "gz", None, None),
        P("gx", "gy", "gz", None, None),
    )
    return jax.shard_map(
        shards,
        mesh=mesh,
        in_specs=placed,
        out_specs=(P("gx", "gy", "gz", None, None), P()),
        check_vma=False,
    )
```

```python
import functools
import math

import jax
import jax.numpy as jnp
from jax import lax
from jax.experimental import pallas as pl
from jax.experimental.pallas import tpu as pltpu
from jax.sharding import PartitionSpec as P

ORDER = 4
CHUNK = 128
BOXES = 8
FEATS = 48
ROWS = 48
F32 = jnp.float32
BF16 = jnp.bfloat16
NODES = [math.cos((2.0 * a + 1.0) * math.pi / (2.0 * ORDER)) for a in range(ORDER)]


def box_id(axis, at, first, second):
    place = [0, 0, 0]
    rest = [d for d in range(3) if d != axis]
    place[axis] = at
    place[rest[0]] = first
    place[rest[1]] = second
    return (place[0] * 2 + place[1]) * 2 + place[2]


def face_boxes(axis, at):
    return [box_id(axis, at, i, j) for i in range(2) for j in range(2)]


def split3(value):
    high = value.astype(BF16).astype(F32)
    rest = value - high
    mid = rest.astype(BF16).astype(F32)
    return high, mid, rest - mid


def row_ids(points):
    return lax.broadcasted_iota(jnp.int32, (8, points), 0)


def source_rows(pos, row):
    p1, p2, p3 = split3(pos)
    n1, n2, n3 = split3(1.0 + jnp.sum(pos * pos, axis=0, keepdims=True))
    s1 = jnp.where(row < 3, p1, jnp.where(row == 3, n1, jnp.where(row == 4, n2, jnp.where(row == 5, n3, 1.0))))
    s2 = p2 + pltpu.roll(p3, 3, 0)
    return jnp.concatenate([s1, s1, s2, s2, s1, jnp.zeros_like(s1)], axis=0).astype(BF16)


def target_rows(pos, row):
    p1, p2, p3 = split3(-2.0 * pos)
    m1, m2, m3 = split3(jnp.sum(pos * pos, axis=0, keepdims=True))
    qa = jnp.where(row < 3, p1, jnp.where(row < 6, 1.0, jnp.where(row == 6, m1, m2)))
    qb = jnp.where(row < 3, p2, jnp.where(row == 6, m3, 0.0))
    qc = p1 + pltpu.roll(p1, 3, 0)
    return jnp.concatenate([qa, qb, qc, p2, p3, jnp.zeros_like(qa)], axis=0).astype(BF16)


def prep_kernel(counts, offs, probes, pay, fa, fb, tab, mom, momf, f0, f1, f2, pad):
    points = offs.shape[-1]
    row = row_ids(points)
    lane = lax.broadcasted_iota(jnp.int32, (1, points), 1)
    faces = (f0, f1, f2)
    pay[BOXES] = jnp.zeros_like(pay[BOXES])
    for k in range(BOXES):
        place = (k // 4, k // 2 % 2, k % 2)
        pad[...] = jnp.zeros_like(pad)
        for d in range(3):
            pad[d:d + 1, :] = offs[place[0], place[1], d, place[2]:place[2] + 1, :]
        off = pad[...]
        shift = jnp.where(row == 0, place[0] - 1.0, jnp.where(row == 1, place[1] - 1.0, jnp.where(row == 2, place[2] - 1.0, 0.0)))
        pos = off + shift
        src = source_rows(pos, row)
        fa[k] = src
        fb[k] = target_rows(pos, row)
        if k == 0:
            fa[BOXES] = src
        count = counts[place]
        chunks = ((count + CHUNK - 1) // CHUNK).astype(F32)
        p1, p2, p3 = split3(pos)
        rows_a = jnp.where(row == 6, chunks, p1 + pltpu.roll(p2, 3, 0))
        tail = jnp.concatenate([rows_a, p3], axis=0).astype(BF16)
        vec = jnp.where(lane < count, probes[place].astype(F32), 0.0).astype(BF16)
        pay[k, 0:32, :] = vec
        pay[k, 32:48, :] = tail
        for axis in range(3):
            if place[axis] == 0:
                other = [d for d in range(3) if d != axis]
                slot = place[other[0]] * 2 + place[other[1]]
                faces[axis][slot, 0:32, :] = vec
                faces[axis][slot, 32:48, :] = tail
        unit = 2.0 * off - 1.0
        t2 = 2.0 * unit * unit - 1.0
        t3 = 2.0 * unit * t2 - unit
        weights = []
        for c in NODES:
            e2 = 2.0 * c * c - 1.0
            e3 = 2.0 * c * e2 - c
            weights.append(0.25 + 0.5 * (c * unit + e2 * t2 + e3 * t3))
        third = jnp.zeros_like(off)
        for d in range(ORDER):
            third = jnp.where(row % 4 == d, weights[d][2:3, :], third)
        seconds = []
        for half in range(2):
            seconds.append(jnp.where(row < 4, weights[2 * half][1:2, :], weights[2 * half + 1][1:2, :]))
        parts = []
        for a in range(ORDER):
            for half in range(2):
                parts.append(weights[a][0:1, :] * seconds[half] * third)
        table = jnp.concatenate(parts, axis=0).astype(BF16)
        tab[k] = table
        moment = lax.dot_general(table, vec, (((1,), (1,)), ((), ())), preferred_element_type=F32)
        momf[:, k * 32:(k + 1) * 32] = moment
    mom[...] = momf[...].astype(BF16)


WIDTHS = (768, 1024)
REGION = 160


def run_steps(targets, sources_of, chunks_of, width_of, dummy, fa, vec, fb, own, out, back, tiles, flips, steps, owner, filled):
    for c in range(len(WIDTHS)):
        filled[c] = 0
    for b in targets:
        count_b = width_of(b)
        kind = jnp.int32(0)
        for width in WIDTHS[:-1]:
            kind = kind + (count_b > width).astype(jnp.int32)
        base = kind * REGION
        at = base + filled[kind]
        for s in sources_of(b):
            for c in range(8):
                steps[at + c] = s * 8 + c
            for c in range(5):
                owner[(at >> 1) + c] = b
            at = at + chunks_of(s)
        steps[at] = dummy * 8
        at = at + (at & 1)
        filled[kind] = at - base
    for c in range(len(WIDTHS)):
        end = c * REGION + filled[c]
        for extra in range(8):
            steps[end + extra] = dummy * 8
            owner[(end + extra) >> 1] = targets[0]

    def columns(index):
        return pl.ds(pl.multiple_of((index & 7) * CHUNK, CHUNK), CHUNK)

    for c, width in enumerate(WIDTHS):
        first_step = c * (REGION // 2)
        total = filled[c] >> 1

        def flip(t, slot):
            for h in range(2):
                index = steps[2 * t + h]
                flips[slot, h * CHUNK:(h + 1) * CHUNK, :] = fa[index >> 3, :, columns(index)].T

        def make(t, slot, width=width):
            target = fb[owner[t], :, 0:width]
            squares = jnp.dot(flips[slot], target, preferred_element_type=F32)
            tiles[slot, :, 0:width] = lax.rsqrt(squares).astype(BF16)

        def use(t, slot, width=width):
            b = owner[t]
            first = steps[2 * t]
            second = steps[2 * t + 1]
            tile = tiles[slot, :, 0:width]
            both = jnp.concatenate([vec[first >> 3, 0:32, columns(first)], vec[second >> 3, 0:32, columns(second)]], axis=1)
            out[b, :, 0:width] += jnp.dot(both, tile, preferred_element_type=F32)
            if back is not None:
                sent = lax.dot_general(own[b, 0:32, 0:width], tile, (((1,), (1,)), ((), ())), preferred_element_type=F32)
                back[first >> 3, :, columns(first)] += sent[:, 0:CHUNK]
                back[second >> 3, :, columns(second)] += sent[:, CHUNK:]

        @pl.when(total > 0)
        def _(flip=flip, make=make, use=use, first_step=first_step, total=total):
            flip(first_step, 0)
            flip(first_step + 1, 1)
            make(first_step, 0)

            def body(k, carry):
                t = first_step + 2 * k
                make(t + 1, 1)
                flip(t + 2, 0)
                use(t, 0)
                make(t + 2, 0)
                flip(t + 3, 1)
                use(t + 1, 1)
                return carry

            lax.fori_loop(0, (total + 1) >> 1, body, 0)


INNER = {4: (0,), 2: (0,), 1: (0,), 6: (2, 4), 5: (1, 4), 3: (1, 2), 7: (3, 5, 6)}


def count_of(counts, k):
    return counts[k // 4, k // 2 % 2, k % 2]


def inner_kernel(targets, sources_of, two_way, counts, fa, pay, fb, acc_in, after, out, done, tiles, flips, steps, owner, filled):
    if acc_in is None:
        out[...] = jnp.zeros_like(out)
    else:
        out[...] = acc_in[...]
    run_steps(
        targets, sources_of, lambda s: (count_of(counts, s) + CHUNK - 1) >> 7, lambda b: count_of(counts, b), BOXES,
        fa, pay, fb, pay, out, out if two_way else None, tiles, flips, steps, owner, filled,
    )
    done[...] = jnp.zeros_like(done)


def outer_kernel(counts, fb, pay, acc_self, acc_in, after, halo0, halo1, halo2, near, b0, b1, b2, probe_sums,
                 fa, vec, plus, back, tiles, flips, steps, owner, filled, chunk_no):
    halos = (halo0, halo1, halo2)
    points = fb.shape[-1]
    row = row_ids(points)
    plus[...] = jnp.zeros_like(plus)
    back[...] = jnp.zeros_like(back)
    sources = {b: [] for b in range(BOXES)}
    spare = 12
    for axis in range(3):
        halo = halos[axis]
        name = ("gx", "gy", "gz")[axis]
        at_edge = lax.axis_index(name) == lax.axis_size(name) - 1
        targets = face_boxes(axis, 1)
        for i in range(4):
            s = axis * 4 + i
            sources[targets[i]].append(s)
            tail = halo[i, 32:48, :].astype(F32)
            rows_a = tail[0:8]
            pos = rows_a + pltpu.roll(rows_a, 5, 0) + tail[8:16]
            pos = jnp.where(row < 3, pos + jnp.where(row == axis, 2.0, 0.0), 0.0)
            feats = source_rows(pos, row)
            fa[s] = feats
            if s == 0:
                fa[spare] = feats
            vec[s] = halo[i, 0:32, :]
            chunk_no[s] = jnp.where(at_edge, 0, jnp.max(rows_a[6:7, 0:128]).astype(jnp.int32))
    vec[spare] = jnp.zeros_like(vec[spare])
    order = [b for b in range(BOXES) if sources[b]]
    run_steps(
        order, lambda b: sources[b], lambda s: chunk_no[s], lambda b: count_of(counts, b), spare,
        fa, vec, fb, pay, plus, back, tiles, flips, steps, owner, filled,
    )
    total = jnp.zeros((32, 128), F32)
    for b in range(BOXES):
        extra = plus[b]
        base = acc_self[b] + acc_in[b]
        near[b] = base + extra
        weighted = pay[b, 0:32, :].astype(F32) * (base + 2.0 * extra)
        for j in range(points // 128):
            total = total + weighted[:, j * 128:(j + 1) * 128]
    probe_sums[...] = total
    for axis, ref in enumerate((b0, b1, b2)):
        ref[...] = back[4 * axis:4 * axis + 4]


def local_kernel(counts, req_box, req_tgt, here, there, momf, probe_sums, loc, sums, far_acc, live):
    my_y = lax.axis_index("gy")
    my_z = lax.axis_index("gz")
    far_acc[...] = jnp.zeros_like(far_acc)

    def keep(i, n):
        live[n] = i
        return n + (req_box[i >> 6, i & 63] >= 0).astype(jnp.int32)

    used = lax.fori_loop(0, 128, keep, jnp.int32(0), unroll=16)
    shape = (64, 64)
    source_q = lax.broadcasted_iota(jnp.int32, shape, 1)
    target_q = lax.broadcasted_iota(jnp.int32, shape, 0)

    def node(index):
        value = jnp.full(shape, 0.5 + 0.5 * NODES[0], F32)
        for a in range(1, ORDER):
            value = jnp.where(index == a, 0.5 + 0.5 * NODES[a], value)
        return value

    gaps = [node((source_q >> s) & 3) - node((target_q >> s) & 3) for s in (4, 2, 0)]
    group = lax.broadcasted_iota(jnp.int32, (64, 256), 1) >> 5

    def step(g, carry):
        for u in range(8):
            k = g * 8 + u
            i = live[jnp.minimum(k, used - 1)]
            peer = i & 63
            box = req_box[i >> 6, peer]
            tgt = req_tgt[i >> 6, peer]
            peer_y = peer >> 4
            peer_z = peer & 15
            dx = (box >> 2) - (tgt >> 2)
            dy = (peer_y - my_y) * 2 + ((box >> 1) & 1) - ((tgt >> 1) & 1)
            dz = (peer_z - my_z) * 2 + (box & 1) - (tgt & 1)
            ex = gaps[0] + dx.astype(F32)
            ey = gaps[1] + dy.astype(F32)
            ez = gaps[2] + dz.astype(F32)
            coupling = lax.rsqrt(1.0 + ex * ex + ey * ey + ez * ez).astype(BF16)
            rel_y = peer_y ^ my_y
            rel_z = peer_z ^ my_z
            at = ((rel_z >> 1) & 3) * 8 + rel_y * 2 + (rel_z >> 3)
            block = jnp.where((rel_z & 1) == 0, here[at], there[at])
            term = jnp.dot(coupling, block, preferred_element_type=F32)
            wanted = jnp.where(k < used, box, -1)
            far_acc[tgt] += jnp.where(group == wanted, term, 0.0)
        return carry

    lax.fori_loop(0, (used + 7) >> 3, step, 0)
    lane = lax.broadcasted_iota(jnp.int32, (64, 128), 1)
    far_sums = jnp.zeros((64, 128), F32)
    live_points = jnp.int32(0)
    for b in range(BOXES):
        wide = far_acc[b]
        half = wide[:, 0:128] + wide[:, 128:256]
        half = half + pltpu.roll(half, 64, 1)
        half = half + pltpu.roll(half, 32, 1)
        rounded = half.astype(BF16)
        loc[b] = rounded
        moment = momf[:, (b // 4) * 128:(b // 4 + 1) * 128]
        far_sums = far_sums + jnp.where((lane >> 5) == b % 4, rounded.astype(F32) * moment, 0.0)
        live_points = live_points + count_of(counts, b)
    folded = jnp.sum(far_sums, axis=0, keepdims=True)
    folded = folded + pltpu.roll(folded, 64, 1)
    folded = folded + pltpu.roll(folded, 32, 1)
    lane32 = lax.broadcasted_iota(jnp.int32, (32, 128), 1)
    row32 = lax.broadcasted_iota(jnp.int32, (32, 128), 0)
    per_probe = jnp.sum(probe_sums[...], axis=1, keepdims=True)
    flat = jnp.sum(jnp.where(lane32 == row32, per_probe, 0.0), axis=0, keepdims=True)
    row_sums = jnp.where(lane32[0:1] < 32, flat + folded, jnp.where(lane32[0:1] == 32, live_points.astype(F32), 0.0))
    sums[...] = jnp.broadcast_to(row_sums.reshape(1, 1, 128), sums.shape)


def total_kernel(counts, near, r2, r0, r1, loc, tab, kv, done):
    points = tab.shape[-1]
    lane = lax.broadcasted_iota(jnp.int32, (1, points), 1)
    for b in range(BOXES):
        place = (b // 4, b // 2 % 2, b % 2)
        far = lax.dot_general(loc[b][:, 0:32], tab[b], (((0,), (0,)), ((), ())), preferred_element_type=F32)
        total = near[b] + far
        for axis, ref in enumerate((r0, r1, r2)):
            if place[axis] == 0:
                other = [d for d in range(3) if d != axis]
                total = total + ref[place[other[0]] * 2 + place[other[1]]]
        if b == 0:
            done[...] = jnp.zeros_like(done)
        kv[b] = jnp.where(lane < count_of(counts, b), total * (1.0 / math.sqrt(7.0 * points)), 0.0).astype(BF16)


def quad_kernel(gathered, after, quad):
    lane = lax.broadcasted_iota(jnp.int32, (1, 128), 1)
    whole = jnp.sum(gathered[...], axis=0)
    live_points = jnp.sum(jnp.where(lane == 32, whole, 0.0), axis=1, keepdims=True)
    scaled = whole * (1.0 / math.sqrt(7.0 * 1024)) / live_points
    quad[...] = scaled[0, 0:32]


VMEM = pl.BlockSpec(memory_space=pltpu.VMEM)
SMEM = pl.BlockSpec(memory_space=pltpu.SMEM)
ANY = pl.BlockSpec(memory_space=pl.ANY)
PARAMS = pltpu.CompilerParams(vmem_limit_bytes=20 * 2**20)


COST = pl.CostEstimate(flops=12 * 10**9, bytes_accessed=4 * 2**20, transcendentals=10**7)


def join(name, *arrays):
    return pl.pallas_call(
        lambda *refs: None,
        out_shape=[jax.ShapeDtypeStruct(a.shape, a.dtype) for a in arrays],
        in_specs=[ANY] * len(arrays),
        out_specs=[ANY] * len(arrays),
        input_output_aliases={i: i for i in range(len(arrays))},
        compiler_params=pltpu.CompilerParams(vmem_limit_bytes=2**20),
        name=name,
    )(*arrays)


def xor_permute(value, axis, bits):
    count = lax.axis_size(axis)
    return lax.ppermute(value, axis, [(i, i ^ bits) for i in range(count)])


def shards(offsets, probes, counts, req_box, req_tgt):
    points = offsets.shape[-1]
    shape = jax.ShapeDtypeStruct
    face = shape((4, ROWS, points), BF16)
    pay, fa, fb, tab, mom, momf, *faces = pl.pallas_call(
        prep_kernel,
        out_shape=[
            shape((BOXES + 1, ROWS, points), BF16),
            shape((BOXES + 1, FEATS, points), BF16),
            shape((BOXES, FEATS, points), BF16),
            shape((BOXES, 64, points), BF16),
            shape((64, 256), BF16),
            shape((64, 256), F32),
        ] + [face] * 3,
        in_specs=[SMEM, VMEM, VMEM],
        out_specs=[VMEM] * 9,
        scratch_shapes=[
            pltpu.VMEM((8, points), F32),
        ],
        compiler_params=PARAMS,
        name="prep",
    )(counts, jnp.swapaxes(offsets, 2, 3), probes)

    acc_shape = shape((BOXES, 32, points), F32)
    lists = [
        pltpu.VMEM((2, 2 * CHUNK, points), BF16),
        pltpu.VMEM((2, 2 * CHUNK, FEATS), BF16),
        pltpu.SMEM((len(WIDTHS) * REGION,), jnp.int32),
        pltpu.SMEM((len(WIDTHS) * REGION // 2,), jnp.int32),
        pltpu.SMEM((8,), jnp.int32),
    ]

    def inner(name, targets, sources_of, two_way, acc, after):
        has_acc = acc is not None

        def kernel(*refs):
            refs = list(refs)
            head = refs[:4]
            rest = refs[4:]
            acc_ref = rest.pop(0) if has_acc else None
            inner_kernel(targets, sources_of, two_way, *head, acc_ref, *rest)

        args = [counts, fa, pay, fb] + ([acc] if has_acc else []) + [after]
        return pl.pallas_call(
            kernel,
            out_shape=[shape((BOXES + 1, 32, points), F32), shape((8, 128), F32)],
            in_specs=[SMEM, VMEM, VMEM, VMEM] + [VMEM] * has_acc + [ANY],
            out_specs=[VMEM, VMEM],
            scratch_shapes=lists,
            compiler_params=PARAMS,
            cost_estimate=COST,
            name=name,
        )(*args)

    def along(axis, value, step):
        name = ("gx", "gy", "gz")[axis]
        size = lax.axis_size(name)
        return lax.ppermute(value, name, [(i, (i + step) % size) for i in range(size)])

    block = mom.reshape(1, 64, 256)
    twin = xor_permute(block, "gz", 8)
    got = [None] * 3
    for axis in (2, 0, 1):
        got[axis] = along(axis, faces[axis], -1)
    acc_self, tick = inner("self_tiles", list(range(BOXES)), lambda b: [b], False, None, mom)
    tick, twin, got[0] = join("join_first", tick, twin, got[0])
    block = jnp.concatenate([block, twin], axis=0)
    more = [xor_permute(block, "gy", k) for k in (1, 2, 3)]
    acc, tick = inner("pairs_low", [1, 2, 4, 3], lambda b: INNER[b], True, None, tick)
    tick, got[1], got[2], *more = join("join_second", tick, got[1], got[2], *more)
    block = jnp.concatenate([block] + more, axis=0)
    more = [xor_permute(block, "gz", 2 * k) for k in (1, 2, 3)]
    acc, tick = inner("pairs_high", [5, 6, 7], lambda b: INNER[b], True, acc, tick)
    tick, *more = join("join_third", tick, *more)
    block = jnp.concatenate([block] + more, axis=0)
    other = xor_permute(block, "gz", 1)
    near, *backs, probe_sums = pl.pallas_call(
        outer_kernel,
        out_shape=[acc_shape] + [shape((4, 32, points), F32)] * 3 + [shape((32, 128), F32)],
        in_specs=[SMEM, VMEM, VMEM, VMEM, VMEM, ANY, VMEM, VMEM, VMEM],
        out_specs=[VMEM] * 5,
        scratch_shapes=[
            pltpu.VMEM((13, FEATS, points), BF16),
            pltpu.VMEM((13, 32, points), BF16),
            pltpu.VMEM((BOXES, 32, points), F32),
            pltpu.VMEM((13, 32, points), F32),
        ] + lists + [pltpu.SMEM((16,), jnp.int32)],
        compiler_params=PARAMS,
        cost_estimate=COST,
        name="face_tiles",
    )(counts, fb, pay, acc_self, acc, tick, *got)
    returned = [None] * 3
    for axis in (2, 0, 1):
        returned[axis] = along(axis, backs[axis], 1)
    devices = lax.axis_size("gx") * lax.axis_size("gy") * lax.axis_size("gz")
    loc, sums = pl.pallas_call(
        local_kernel,
        out_shape=[shape((BOXES, 64, 128), BF16), shape((devices, 1, 128), F32)],
        in_specs=[SMEM, SMEM, SMEM, VMEM, VMEM, VMEM, VMEM],
        out_specs=[VMEM, VMEM],
        scratch_shapes=[
            pltpu.VMEM((BOXES, 64, 256), F32),
            pltpu.SMEM((136,), jnp.int32),
        ],
        compiler_params=PARAMS,
        name="locals",
    )(counts, *[jnp.swapaxes(r, 3, 4).reshape(2, 64) for r in (req_box, req_tgt)], block, other, momf, probe_sums)
    gathered = lax.all_to_all(sums, ("gx", "gy", "gz"), 0, 0, tiled=True)
    kv, total_tick = pl.pallas_call(
        total_kernel,
        out_shape=[shape((BOXES, 32, points), BF16), shape((8, 128), F32)],
        in_specs=[SMEM] + [VMEM] * 6,
        out_specs=[VMEM, VMEM],
        compiler_params=PARAMS,
        cost_estimate=COST,
        name="total",
    )(counts, near, returned[2], returned[0], returned[1], loc, tab)
    quad = pl.pallas_call(
        quad_kernel,
        out_shape=shape((32,), F32),
        in_specs=[VMEM, ANY],
        out_specs=VMEM,
        compiler_params=pltpu.CompilerParams(vmem_limit_bytes=2**21),
        name="quad",
    )(gathered, total_tick)
    return kv.reshape(probes.shape), quad


def solution(mesh):
    placed = (
        P("gx", "gy", "gz", None, None),
        P("gx", "gy", "gz", None, None),
        P("gx", "gy", "gz"),
        P("gx", "gy", "gz", None, None),
        P("gx", "gy", "gz", None, None),
    )
    return jax.shard_map(
        shards,
        mesh=mesh,
        in_specs=placed,
        out_specs=(P("gx", "gy", "gz", None, None), P()),
        check_vma=False,
    )
```

```python
import functools
import math

import jax
import jax.numpy as jnp
from jax import lax
from jax.experimental import pallas as pl
from jax.experimental.pallas import tpu as pltpu
from jax.sharding import PartitionSpec as P

ORDER = 4
CHUNK = 128
BOXES = 8
FEATS = 48
ROWS = 48
F32 = jnp.float32
BF16 = jnp.bfloat16
NODES = [math.cos((2.0 * a + 1.0) * math.pi / (2.0 * ORDER)) for a in range(ORDER)]


def box_id(axis, at, first, second):
    place = [0, 0, 0]
    rest = [d for d in range(3) if d != axis]
    place[axis] = at
    place[rest[0]] = first
    place[rest[1]] = second
    return (place[0] * 2 + place[1]) * 2 + place[2]


def face_boxes(axis, at):
    return [box_id(axis, at, i, j) for i in range(2) for j in range(2)]


def split3(value):
    high = value.astype(BF16).astype(F32)
    rest = value - high
    mid = rest.astype(BF16).astype(F32)
    return high, mid, rest - mid


def row_ids(points):
    return lax.broadcasted_iota(jnp.int32, (8, points), 0)


def source_rows(pos, row):
    p1, p2, p3 = split3(pos)
    n1, n2, n3 = split3(1.0 + jnp.sum(pos * pos, axis=0, keepdims=True))
    s1 = jnp.where(row < 3, p1, jnp.where(row == 3, n1, jnp.where(row == 4, n2, jnp.where(row == 5, n3, 1.0))))
    s2 = p2 + pltpu.roll(p3, 3, 0)
    return jnp.concatenate([s1, s1, s2, s2, s1, jnp.zeros_like(s1)], axis=0).astype(BF16)


def target_rows(pos, row):
    p1, p2, p3 = split3(-2.0 * pos)
    m1, m2, m3 = split3(jnp.sum(pos * pos, axis=0, keepdims=True))
    qa = jnp.where(row < 3, p1, jnp.where(row < 6, 1.0, jnp.where(row == 6, m1, m2)))
    qb = jnp.where(row < 3, p2, jnp.where(row == 6, m3, 0.0))
    qc = p1 + pltpu.roll(p1, 3, 0)
    return jnp.concatenate([qa, qb, qc, p2, p3, jnp.zeros_like(qa)], axis=0).astype(BF16)


def prep_kernel(counts, offs, probes, pay, fa, fb, tab, mom, momf, f0, f1, f2, pad):
    points = offs.shape[-1]
    row = row_ids(points)
    lane = lax.broadcasted_iota(jnp.int32, (1, points), 1)
    faces = (f0, f1, f2)
    pay[BOXES] = jnp.zeros_like(pay[BOXES])
    for k in range(BOXES):
        place = (k // 4, k // 2 % 2, k % 2)
        pad[...] = jnp.zeros_like(pad)
        for d in range(3):
            pad[d:d + 1, :] = offs[place[0], place[1], d, place[2]:place[2] + 1, :]
        off = pad[...]
        shift = jnp.where(row == 0, place[0] - 1.0, jnp.where(row == 1, place[1] - 1.0, jnp.where(row == 2, place[2] - 1.0, 0.0)))
        pos = off + shift
        src = source_rows(pos, row)
        fa[k] = src
        fb[k] = target_rows(pos, row)
        if k == 0:
            fa[BOXES] = src
        count = counts[place]
        chunks = ((count + CHUNK - 1) // CHUNK).astype(F32)
        p1, p2, p3 = split3(pos)
        rows_a = jnp.where(row == 6, chunks, p1 + pltpu.roll(p2, 3, 0))
        tail = jnp.concatenate([rows_a, p3], axis=0).astype(BF16)
        vec = jnp.where(lane < count, probes[place].astype(F32), 0.0).astype(BF16)
        pay[k, 0:32, :] = vec
        pay[k, 32:48, :] = tail
        for axis in range(3):
            if place[axis] == 0:
                other = [d for d in range(3) if d != axis]
                slot = place[other[0]] * 2 + place[other[1]]
                faces[axis][slot, 0:32, :] = vec
                faces[axis][slot, 32:48, :] = tail
        unit = 2.0 * off - 1.0
        t2 = 2.0 * unit * unit - 1.0
        t3 = 2.0 * unit * t2 - unit
        weights = []
        for c in NODES:
            e2 = 2.0 * c * c - 1.0
            e3 = 2.0 * c * e2 - c
            weights.append(0.25 + 0.5 * (c * unit + e2 * t2 + e3 * t3))
        third = jnp.zeros_like(off)
        for d in range(ORDER):
            third = jnp.where(row % 4 == d, weights[d][2:3, :], third)
        seconds = []
        for half in range(2):
            seconds.append(jnp.where(row < 4, weights[2 * half][1:2, :], weights[2 * half + 1][1:2, :]))
        parts = []
        for a in range(ORDER):
            for half in range(2):
                parts.append(weights[a][0:1, :] * seconds[half] * third)
        table = jnp.concatenate(parts, axis=0).astype(BF16)
        tab[k] = table
        moment = lax.dot_general(table, vec, (((1,), (1,)), ((), ())), preferred_element_type=F32)
        momf[:, k * 32:(k + 1) * 32] = moment
    mom[...] = momf[...].astype(BF16)


WIDTHS = (512, 768, 1024)
REGION = 160


def run_steps(targets, sources_of, chunks_of, width_of, dummy, fa, vec, fb, own, out, back, tiles, flips, steps, owner, filled):
    for c in range(len(WIDTHS)):
        filled[c] = 0
    for b in targets:
        count_b = width_of(b)
        kind = jnp.int32(0)
        for width in WIDTHS[:-1]:
            kind = kind + (count_b > width).astype(jnp.int32)
        base = kind * REGION
        at = base + filled[kind]
        for s in sources_of(b):
            for c in range(8):
                steps[at + c] = s * 8 + c
            for c in range(5):
                owner[(at >> 1) + c] = b
            at = at + chunks_of(s)
        steps[at] = dummy * 8
        at = at + (at & 1)
        filled[kind] = at - base
    for c in range(len(WIDTHS)):
        end = c * REGION + filled[c]
        for extra in range(12):
            steps[end + extra] = dummy * 8
            owner[(end + extra) >> 1] = targets[0]

    def columns(index):
        return pl.ds(pl.multiple_of((index & 7) * CHUNK, CHUNK), CHUNK)

    for c, width in enumerate(WIDTHS):
        first_step = c * (REGION // 2)
        total = filled[c] >> 1

        def flip(t, slot):
            for h in range(2):
                index = steps[2 * t + h]
                flips[slot, h * CHUNK:(h + 1) * CHUNK, :] = fa[index >> 3, :, columns(index)].T

        def make(t, slot, width=width):
            target = fb[owner[t], :, 0:width]
            squares = jnp.dot(flips[slot], target, preferred_element_type=F32)
            tiles[slot, :, 0:width] = lax.rsqrt(squares).astype(BF16)

        def use(t, slot, width=width):
            b = owner[t]
            first = steps[2 * t]
            second = steps[2 * t + 1]
            tile = tiles[slot, :, 0:width]
            both = jnp.concatenate([vec[first >> 3, 0:32, columns(first)], vec[second >> 3, 0:32, columns(second)]], axis=1)
            out[b, :, 0:width] += jnp.dot(both, tile, preferred_element_type=F32)
            if back is not None:
                sent = lax.dot_general(own[b, 0:32, 0:width], tile, (((1,), (1,)), ((), ())), preferred_element_type=F32)
                back[first >> 3, :, columns(first)] += sent[:, 0:CHUNK]
                back[second >> 3, :, columns(second)] += sent[:, CHUNK:]

        @pl.when(total > 0)
        def _(flip=flip, make=make, use=use, first_step=first_step, total=total):
            end = first_step + total
            for slot in range(4):
                flip(first_step + slot, slot)
            make(first_step, 0)
            make(first_step + 1, 1)

            def half(t, now, later):
                make(t + 2, later)
                make(t + 3, later + 1)
                flip(t + 4, now)
                flip(t + 5, now + 1)
                use(t, now)
                use(t + 1, now + 1)

            def body(k, carry):
                t = first_step + 4 * k
                half(t, 0, 2)

                @pl.when(t + 2 < end)
                def _():
                    half(t + 2, 2, 0)

                return carry

            lax.fori_loop(0, (total + 3) >> 2, body, 0)


INNER = {4: (0,), 2: (0,), 1: (0,), 6: (2, 4), 5: (1, 4), 3: (1, 2), 7: (3, 5, 6)}


def count_of(counts, k):
    return counts[k // 4, k // 2 % 2, k % 2]


def inner_kernel(targets, sources_of, two_way, counts, fa, pay, fb, acc_in, after, out, done, tiles, flips, steps, owner, filled):
    if acc_in is None:
        out[...] = jnp.zeros_like(out)
    else:
        out[...] = acc_in[...]
    run_steps(
        targets, sources_of, lambda s: (count_of(counts, s) + CHUNK - 1) >> 7, lambda b: count_of(counts, b), BOXES,
        fa, pay, fb, pay, out, out if two_way else None, tiles, flips, steps, owner, filled,
    )
    done[...] = jnp.zeros_like(done)


def outer_kernel(counts, fb, pay, acc_self, acc_in, after, halo0, halo1, halo2, near, b0, b1, b2, probe_sums,
                 fa, vec, plus, back, tiles, flips, steps, owner, filled, chunk_no):
    halos = (halo0, halo1, halo2)
    points = fb.shape[-1]
    row = row_ids(points)
    plus[...] = jnp.zeros_like(plus)
    back[...] = jnp.zeros_like(back)
    sources = {b: [] for b in range(BOXES)}
    spare = 12
    for axis in range(3):
        halo = halos[axis]
        name = ("gx", "gy", "gz")[axis]
        at_edge = lax.axis_index(name) == lax.axis_size(name) - 1
        targets = face_boxes(axis, 1)
        for i in range(4):
            s = axis * 4 + i
            sources[targets[i]].append(s)
            tail = halo[i, 32:48, :].astype(F32)
            rows_a = tail[0:8]
            pos = rows_a + pltpu.roll(rows_a, 5, 0) + tail[8:16]
            pos = jnp.where(row < 3, pos + jnp.where(row == axis, 2.0, 0.0), 0.0)
            feats = source_rows(pos, row)
            fa[s] = feats
            if s == 0:
                fa[spare] = feats
            vec[s] = halo[i, 0:32, :]
            chunk_no[s] = jnp.where(at_edge, 0, jnp.max(rows_a[6:7, 0:128]).astype(jnp.int32))
    vec[spare] = jnp.zeros_like(vec[spare])
    order = [b for b in range(BOXES) if sources[b]]
    run_steps(
        order, lambda b: sources[b], lambda s: chunk_no[s], lambda b: count_of(counts, b), spare,
        fa, vec, fb, pay, plus, back, tiles, flips, steps, owner, filled,
    )
    total = jnp.zeros((32, 128), F32)
    for b in range(BOXES):
        extra = plus[b]
        base = acc_self[b] + acc_in[b]
        near[b] = base + extra
        weighted = pay[b, 0:32, :].astype(F32) * (base + 2.0 * extra)
        for j in range(points // 128):
            total = total + weighted[:, j * 128:(j + 1) * 128]
    probe_sums[...] = total
    for axis, ref in enumerate((b0, b1, b2)):
        ref[...] = back[4 * axis:4 * axis + 4]


def local_kernel(counts, req_box, req_tgt, here, there, momf, probe_sums, loc, sums, far_acc, live):
    my_y = lax.axis_index("gy")
    my_z = lax.axis_index("gz")
    far_acc[...] = jnp.zeros_like(far_acc)

    def keep(i, n):
        live[n] = i
        return n + (req_box[i >> 6, i & 63] >= 0).astype(jnp.int32)

    used = lax.fori_loop(0, 128, keep, jnp.int32(0), unroll=16)
    shape = (64, 64)
    source_q = lax.broadcasted_iota(jnp.int32, shape, 1)
    target_q = lax.broadcasted_iota(jnp.int32, shape, 0)

    def node(index):
        value = jnp.full(shape, 0.5 + 0.5 * NODES[0], F32)
        for a in range(1, ORDER):
            value = jnp.where(index == a, 0.5 + 0.5 * NODES[a], value)
        return value

    gaps = [node((source_q >> s) & 3) - node((target_q >> s) & 3) for s in (4, 2, 0)]
    group = lax.broadcasted_iota(jnp.int32, (64, 256), 1) >> 5

    def step(g, carry):
        for u in range(8):
            k = g * 8 + u
            i = live[jnp.minimum(k, used - 1)]
            peer = i & 63
            box = req_box[i >> 6, peer]
            tgt = req_tgt[i >> 6, peer]
            peer_y = peer >> 4
            peer_z = peer & 15
            dx = (box >> 2) - (tgt >> 2)
            dy = (peer_y - my_y) * 2 + ((box >> 1) & 1) - ((tgt >> 1) & 1)
            dz = (peer_z - my_z) * 2 + (box & 1) - (tgt & 1)
            ex = gaps[0] + dx.astype(F32)
            ey = gaps[1] + dy.astype(F32)
            ez = gaps[2] + dz.astype(F32)
            coupling = lax.rsqrt(1.0 + ex * ex + ey * ey + ez * ez).astype(BF16)
            rel_y = peer_y ^ my_y
            rel_z = peer_z ^ my_z
            at = ((rel_z >> 1) & 3) * 8 + rel_y * 2 + (rel_z >> 3)
            block = jnp.where((rel_z & 1) == 0, here[at], there[at])
            term = jnp.dot(coupling, block, preferred_element_type=F32)
            wanted = jnp.where(k < used, box, -1)
            far_acc[tgt] += jnp.where(group == wanted, term, 0.0)
        return carry

    lax.fori_loop(0, (used + 7) >> 3, step, 0)
    lane = lax.broadcasted_iota(jnp.int32, (64, 128), 1)
    far_sums = jnp.zeros((64, 128), F32)
    live_points = jnp.int32(0)
    for b in range(BOXES):
        wide = far_acc[b]
        half = wide[:, 0:128] + wide[:, 128:256]
        half = half + pltpu.roll(half, 64, 1)
        half = half + pltpu.roll(half, 32, 1)
        rounded = half.astype(BF16)
        loc[b] = rounded
        moment = momf[:, (b // 4) * 128:(b // 4 + 1) * 128]
        far_sums = far_sums + jnp.where((lane >> 5) == b % 4, rounded.astype(F32) * moment, 0.0)
        live_points = live_points + count_of(counts, b)
    folded = jnp.sum(far_sums, axis=0, keepdims=True)
    folded = folded + pltpu.roll(folded, 64, 1)
    folded = folded + pltpu.roll(folded, 32, 1)
    lane32 = lax.broadcasted_iota(jnp.int32, (32, 128), 1)
    row32 = lax.broadcasted_iota(jnp.int32, (32, 128), 0)
    per_probe = jnp.sum(probe_sums[...], axis=1, keepdims=True)
    flat = jnp.sum(jnp.where(lane32 == row32, per_probe, 0.0), axis=0, keepdims=True)
    row_sums = jnp.where(lane32[0:1] < 32, flat + folded, jnp.where(lane32[0:1] == 32, live_points.astype(F32), 0.0))
    sums[...] = jnp.broadcast_to(row_sums.reshape(1, 1, 128), sums.shape)


def total_kernel(counts, near, r2, r0, r1, loc, tab, kv, done):
    points = tab.shape[-1]
    lane = lax.broadcasted_iota(jnp.int32, (1, points), 1)
    for b in range(BOXES):
        place = (b // 4, b // 2 % 2, b % 2)
        far = lax.dot_general(loc[b][:, 0:32], tab[b], (((0,), (0,)), ((), ())), preferred_element_type=F32)
        total = near[b] + far
        for axis, ref in enumerate((r0, r1, r2)):
            if place[axis] == 0:
                other = [d for d in range(3) if d != axis]
                total = total + ref[place[other[0]] * 2 + place[other[1]]]
        if b == 0:
            done[...] = jnp.zeros_like(done)
        kv[b] = jnp.where(lane < count_of(counts, b), total * (1.0 / math.sqrt(7.0 * points)), 0.0).astype(BF16)


def quad_kernel(gathered, after, quad):
    lane = lax.broadcasted_iota(jnp.int32, (1, 128), 1)
    whole = jnp.sum(gathered[...], axis=0)
    live_points = jnp.sum(jnp.where(lane == 32, whole, 0.0), axis=1, keepdims=True)
    scaled = whole * (1.0 / math.sqrt(7.0 * 1024)) / live_points
    quad[...] = scaled[0, 0:32]


VMEM = pl.BlockSpec(memory_space=pltpu.VMEM)
SMEM = pl.BlockSpec(memory_space=pltpu.SMEM)
ANY = pl.BlockSpec(memory_space=pl.ANY)
PARAMS = pltpu.CompilerParams(vmem_limit_bytes=20 * 2**20)


COST = pl.CostEstimate(flops=12 * 10**9, bytes_accessed=4 * 2**20, transcendentals=10**7)


def join(name, *arrays):
    return pl.pallas_call(
        lambda *refs: None,
        out_shape=[jax.ShapeDtypeStruct(a.shape, a.dtype) for a in arrays],
        in_specs=[ANY] * len(arrays),
        out_specs=[ANY] * len(arrays),
        input_output_aliases={i: i for i in range(len(arrays))},
        compiler_params=pltpu.CompilerParams(vmem_limit_bytes=2**20),
        name=name,
    )(*arrays)


def xor_permute(value, axis, bits):
    count = lax.axis_size(axis)
    return lax.ppermute(value, axis, [(i, i ^ bits) for i in range(count)])


def shards(offsets, probes, counts, req_box, req_tgt):
    points = offsets.shape[-1]
    shape = jax.ShapeDtypeStruct
    face = shape((4, ROWS, points), BF16)
    pay, fa, fb, tab, mom, momf, *faces = pl.pallas_call(
        prep_kernel,
        out_shape=[
            shape((BOXES + 1, ROWS, points), BF16),
            shape((BOXES + 1, FEATS, points), BF16),
            shape((BOXES, FEATS, points), BF16),
            shape((BOXES, 64, points), BF16),
            shape((64, 256), BF16),
            shape((64, 256), F32),
        ] + [face] * 3,
        in_specs=[SMEM, VMEM, VMEM],
        out_specs=[VMEM] * 9,
        scratch_shapes=[
            pltpu.VMEM((8, points), F32),
        ],
        compiler_params=PARAMS,
        name="prep",
    )(counts, jnp.swapaxes(offsets, 2, 3), probes)

    acc_shape = shape((BOXES, 32, points), F32)
    lists = [
        pltpu.VMEM((4, 2 * CHUNK, points), BF16),
        pltpu.VMEM((4, 2 * CHUNK, FEATS), BF16),
        pltpu.SMEM((len(WIDTHS) * REGION,), jnp.int32),
        pltpu.SMEM((len(WIDTHS) * REGION // 2,), jnp.int32),
        pltpu.SMEM((8,), jnp.int32),
    ]

    def inner(name, targets, sources_of, two_way, acc, after):
        has_acc = acc is not None

        def kernel(*refs):
            refs = list(refs)
            head = refs[:4]
            rest = refs[4:]
            acc_ref = rest.pop(0) if has_acc else None
            inner_kernel(targets, sources_of, two_way, *head, acc_ref, *rest)

        args = [counts, fa, pay, fb] + ([acc] if has_acc else []) + [after]
        return pl.pallas_call(
            kernel,
            out_shape=[shape((BOXES + 1, 32, points), F32), shape((8, 128), F32)],
            in_specs=[SMEM, VMEM, VMEM, VMEM] + [VMEM] * has_acc + [ANY],
            out_specs=[VMEM, VMEM],
            scratch_shapes=lists,
            compiler_params=PARAMS,
            cost_estimate=COST,
            name=name,
        )(*args)

    def along(axis, value, step):
        name = ("gx", "gy", "gz")[axis]
        size = lax.axis_size(name)
        return lax.ppermute(value, name, [(i, (i + step) % size) for i in range(size)])

    block = mom.reshape(1, 64, 256)
    twin = xor_permute(block, "gz", 8)
    got = [None] * 3
    for axis in (2, 0, 1):
        got[axis] = along(axis, faces[axis], -1)
    acc_self, tick = inner("self_tiles", list(range(BOXES)), lambda b: [b], False, None, mom)
    tick, twin, got[0] = join("join_first", tick, twin, got[0])
    block = jnp.concatenate([block, twin], axis=0)
    more = [xor_permute(block, "gy", k) for k in (1, 2, 3)]
    acc, tick = inner("pairs_low", [1, 2, 4, 3], lambda b: INNER[b], True, None, tick)
    tick, got[1], got[2], *more = join("join_second", tick, got[1], got[2], *more)
    block = jnp.concatenate([block] + more, axis=0)
    more = [xor_permute(block, "gz", 2 * k) for k in (1, 2, 3)]
    acc, tick = inner("pairs_high", [5, 6, 7], lambda b: INNER[b], True, acc, tick)
    tick, *more = join("join_third", tick, *more)
    block = jnp.concatenate([block] + more, axis=0)
    other = xor_permute(block, "gz", 1)
    near, *backs, probe_sums = pl.pallas_call(
        outer_kernel,
        out_shape=[acc_shape] + [shape((4, 32, points), F32)] * 3 + [shape((32, 128), F32)],
        in_specs=[SMEM, VMEM, VMEM, VMEM, VMEM, ANY, VMEM, VMEM, VMEM],
        out_specs=[VMEM] * 5,
        scratch_shapes=[
            pltpu.VMEM((13, FEATS, points), BF16),
            pltpu.VMEM((13, 32, points), BF16),
            pltpu.VMEM((BOXES, 32, points), F32),
            pltpu.VMEM((13, 32, points), F32),
        ] + lists + [pltpu.SMEM((16,), jnp.int32)],
        compiler_params=PARAMS,
        cost_estimate=COST,
        name="face_tiles",
    )(counts, fb, pay, acc_self, acc, tick, *got)
    returned = [None] * 3
    for axis in (2, 0, 1):
        returned[axis] = along(axis, backs[axis], 1)
    devices = lax.axis_size("gx") * lax.axis_size("gy") * lax.axis_size("gz")
    loc, sums = pl.pallas_call(
        local_kernel,
        out_shape=[shape((BOXES, 64, 128), BF16), shape((devices, 1, 128), F32)],
        in_specs=[SMEM, SMEM, SMEM, VMEM, VMEM, VMEM, VMEM],
        out_specs=[VMEM, VMEM],
        scratch_shapes=[
            pltpu.VMEM((BOXES, 64, 256), F32),
            pltpu.SMEM((136,), jnp.int32),
        ],
        compiler_params=PARAMS,
        name="locals",
    )(counts, *[jnp.swapaxes(r, 3, 4).reshape(2, 64) for r in (req_box, req_tgt)], block, other, momf, probe_sums)
    gathered = lax.all_to_all(sums, ("gx", "gy", "gz"), 0, 0, tiled=True)
    kv, total_tick = pl.pallas_call(
        total_kernel,
        out_shape=[shape((BOXES, 32, points), BF16), shape((8, 128), F32)],
        in_specs=[SMEM] + [VMEM] * 6,
        out_specs=[VMEM, VMEM],
        compiler_params=PARAMS,
        cost_estimate=COST,
        name="total",
    )(counts, near, returned[2], returned[0], returned[1], loc, tab)
    quad = pl.pallas_call(
        quad_kernel,
        out_shape=shape((32,), F32),
        in_specs=[VMEM, ANY],
        out_specs=VMEM,
        compiler_params=pltpu.CompilerParams(vmem_limit_bytes=2**21),
        name="quad",
    )(gathered, total_tick)
    return kv.reshape(probes.shape), quad


def solution(mesh):
    placed = (
        P("gx", "gy", "gz", None, None),
        P("gx", "gy", "gz", None, None),
        P("gx", "gy", "gz"),
        P("gx", "gy", "gz", None, None),
        P("gx", "gy", "gz", None, None),
    )
    return jax.shard_map(
        shards,
        mesh=mesh,
        in_specs=placed,
        out_specs=(P("gx", "gy", "gz", None, None), P()),
        check_vma=False,
    )
```

```python
import functools
import math

import jax
import jax.numpy as jnp
from jax import lax
from jax.experimental import pallas as pl
from jax.experimental.pallas import tpu as pltpu
from jax.sharding import PartitionSpec as P

ORDER = 4
CHUNK = 128
BOXES = 8
FEATS = 48
ROWS = 48
F32 = jnp.float32
BF16 = jnp.bfloat16
NODES = [math.cos((2.0 * a + 1.0) * math.pi / (2.0 * ORDER)) for a in range(ORDER)]


def box_id(axis, at, first, second):
    place = [0, 0, 0]
    rest = [d for d in range(3) if d != axis]
    place[axis] = at
    place[rest[0]] = first
    place[rest[1]] = second
    return (place[0] * 2 + place[1]) * 2 + place[2]


def face_boxes(axis, at):
    return [box_id(axis, at, i, j) for i in range(2) for j in range(2)]


def split3(value):
    high = value.astype(BF16).astype(F32)
    rest = value - high
    mid = rest.astype(BF16).astype(F32)
    return high, mid, rest - mid


def row_ids(points):
    return lax.broadcasted_iota(jnp.int32, (8, points), 0)


def source_rows(pos, row):
    p1, p2, p3 = split3(pos)
    n1, n2, n3 = split3(1.0 + jnp.sum(pos * pos, axis=0, keepdims=True))
    s1 = jnp.where(row < 3, p1, jnp.where(row == 3, n1, jnp.where(row == 4, n2, jnp.where(row == 5, n3, 1.0))))
    s2 = p2 + pltpu.roll(p3, 3, 0)
    return jnp.concatenate([s1, s1, s2, s2, s1, jnp.zeros_like(s1)], axis=0).astype(BF16)


def target_rows(pos, row):
    p1, p2, p3 = split3(-2.0 * pos)
    m1, m2, m3 = split3(jnp.sum(pos * pos, axis=0, keepdims=True))
    qa = jnp.where(row < 3, p1, jnp.where(row < 6, 1.0, jnp.where(row == 6, m1, m2)))
    qb = jnp.where(row < 3, p2, jnp.where(row == 6, m3, 0.0))
    qc = p1 + pltpu.roll(p1, 3, 0)
    return jnp.concatenate([qa, qb, qc, p2, p3, jnp.zeros_like(qa)], axis=0).astype(BF16)


def prep_kernel(counts, offs, probes, pay, fa, fb, tab, mom, momf, f0, f1, f2, pad):
    points = offs.shape[-1]
    row = row_ids(points)
    lane = lax.broadcasted_iota(jnp.int32, (1, points), 1)
    faces = (f0, f1, f2)
    pay[BOXES] = jnp.zeros_like(pay[BOXES])
    for k in range(BOXES):
        place = (k // 4, k // 2 % 2, k % 2)
        pad[...] = jnp.zeros_like(pad)
        for d in range(3):
            pad[d:d + 1, :] = offs[place[0], place[1], d, place[2]:place[2] + 1, :]
        off = pad[...]
        shift = jnp.where(row == 0, place[0] - 1.0, jnp.where(row == 1, place[1] - 1.0, jnp.where(row == 2, place[2] - 1.0, 0.0)))
        pos = off + shift
        src = source_rows(pos, row)
        fa[k] = src
        fb[k] = target_rows(pos, row)
        if k == 0:
            fa[BOXES] = src
        count = counts[place]
        chunks = ((count + CHUNK - 1) // CHUNK).astype(F32)
        p1, p2, p3 = split3(pos)
        rows_a = jnp.where(row == 6, chunks, p1 + pltpu.roll(p2, 3, 0))
        tail = jnp.concatenate([rows_a, p3], axis=0).astype(BF16)
        vec = jnp.where(lane < count, probes[place].astype(F32), 0.0).astype(BF16)
        pay[k, 0:32, :] = vec
        pay[k, 32:48, :] = tail
        for axis in range(3):
            if place[axis] == 0:
                other = [d for d in range(3) if d != axis]
                slot = place[other[0]] * 2 + place[other[1]]
                faces[axis][slot, 0:32, :] = vec
                faces[axis][slot, 32:48, :] = tail
        unit = 2.0 * off - 1.0
        t2 = 2.0 * unit * unit - 1.0
        t3 = 2.0 * unit * t2 - unit
        weights = []
        for c in NODES:
            e2 = 2.0 * c * c - 1.0
            e3 = 2.0 * c * e2 - c
            weights.append(0.25 + 0.5 * (c * unit + e2 * t2 + e3 * t3))
        third = jnp.zeros_like(off)
        for d in range(ORDER):
            third = jnp.where(row % 4 == d, weights[d][2:3, :], third)
        seconds = []
        for half in range(2):
            seconds.append(jnp.where(row < 4, weights[2 * half][1:2, :], weights[2 * half + 1][1:2, :]))
        parts = []
        for a in range(ORDER):
            for half in range(2):
                parts.append(weights[a][0:1, :] * seconds[half] * third)
        table = jnp.concatenate(parts, axis=0).astype(BF16)
        tab[k] = table
        moment = lax.dot_general(table, vec, (((1,), (1,)), ((), ())), preferred_element_type=F32)
        momf[:, k * 32:(k + 1) * 32] = moment
    mom[...] = momf[...].astype(BF16)


WIDTHS = (768, 1024)
REGION = 160


def run_steps(targets, sources_of, chunks_of, width_of, dummy, fa, vec, fb, own, out, back, tiles, flips, steps, owner, filled):
    for c in range(len(WIDTHS)):
        filled[c] = 0
    for b in targets:
        count_b = width_of(b)
        kind = jnp.int32(0)
        for width in WIDTHS[:-1]:
            kind = kind + (count_b > width).astype(jnp.int32)
        base = kind * REGION
        at = base + filled[kind]
        for s in sources_of(b):
            for c in range(8):
                steps[at + c] = s * 8 + c
            for c in range(5):
                owner[(at >> 1) + c] = b
            at = at + chunks_of(s)
        steps[at] = dummy * 8
        at = at + (at & 1)
        filled[kind] = at - base
    for c in range(len(WIDTHS)):
        end = c * REGION + filled[c]
        for extra in range(8):
            steps[end + extra] = dummy * 8
            owner[(end + extra) >> 1] = targets[0]

    def columns(index):
        return pl.ds(pl.multiple_of((index & 7) * CHUNK, CHUNK), CHUNK)

    for c, width in enumerate(WIDTHS):
        first_step = c * (REGION // 2)
        total = filled[c] >> 1

        def flip(t, slot):
            for h in range(2):
                index = steps[2 * t + h]
                flips[slot, h * CHUNK:(h + 1) * CHUNK, :] = fa[index >> 3, :, columns(index)].T

        def make(t, slot, width=width):
            target = fb[owner[t], :, 0:width]
            squares = jnp.dot(flips[slot], target, preferred_element_type=F32)
            tiles[slot, :, 0:width] = lax.rsqrt(squares).astype(BF16)

        def use(t, slot, width=width):
            b = owner[t]
            first = steps[2 * t]
            second = steps[2 * t + 1]
            tile = tiles[slot, :, 0:width]
            both = jnp.concatenate([vec[first >> 3, 0:32, columns(first)], vec[second >> 3, 0:32, columns(second)]], axis=1)
            out[b, :, 0:width] += jnp.dot(both, tile, preferred_element_type=F32)
            if back is not None:
                sent = lax.dot_general(own[b, 0:32, 0:width], tile, (((1,), (1,)), ((), ())), preferred_element_type=F32)
                back[first >> 3, :, columns(first)] += sent[:, 0:CHUNK]
                back[second >> 3, :, columns(second)] += sent[:, CHUNK:]

        @pl.when(total > 0)
        def _(flip=flip, make=make, use=use, first_step=first_step, total=total):
            flip(first_step, 0)
            flip(first_step + 1, 1)
            make(first_step, 0)

            def body(k, carry):
                t = first_step + 2 * k
                make(t + 1, 1)
                flip(t + 2, 0)
                use(t, 0)
                make(t + 2, 0)
                flip(t + 3, 1)
                use(t + 1, 1)
                return carry

            lax.fori_loop(0, (total + 1) >> 1, body, 0)


INNER = {4: (0,), 2: (0,), 1: (0,), 6: (2, 4), 5: (1, 4), 3: (1, 2), 7: (3, 5, 6)}


def count_of(counts, k):
    return counts[k // 4, k // 2 % 2, k % 2]


def inner_kernel(targets, sources_of, two_way, counts, fa, pay, fb, acc_in, after, out, done, tiles, flips, steps, owner, filled):
    if acc_in is None:
        out[...] = jnp.zeros_like(out)
    else:
        out[...] = acc_in[...]
    run_steps(
        targets, sources_of, lambda s: (count_of(counts, s) + CHUNK - 1) >> 7, lambda b: count_of(counts, b), BOXES,
        fa, pay, fb, pay, out, out if two_way else None, tiles, flips, steps, owner, filled,
    )
    done[...] = jnp.zeros_like(done)


def outer_kernel(counts, fb, pay, acc_self, acc_in, after, halo0, halo1, halo2, near, b0, b1, b2, probe_sums,
                 fa, vec, plus, back, tiles, flips, steps, owner, filled, chunk_no):
    halos = (halo0, halo1, halo2)
    points = fb.shape[-1]
    row = row_ids(points)
    plus[...] = jnp.zeros_like(plus)
    back[...] = jnp.zeros_like(back)
    sources = {b: [] for b in range(BOXES)}
    spare = 12
    for axis in range(3):
        halo = halos[axis]
        name = ("gx", "gy", "gz")[axis]
        at_edge = lax.axis_index(name) == lax.axis_size(name) - 1
        targets = face_boxes(axis, 1)
        for i in range(4):
            s = axis * 4 + i
            sources[targets[i]].append(s)
            tail = halo[i, 32:48, :].astype(F32)
            rows_a = tail[0:8]
            pos = rows_a + pltpu.roll(rows_a, 5, 0) + tail[8:16]
            pos = jnp.where(row < 3, pos + jnp.where(row == axis, 2.0, 0.0), 0.0)
            feats = source_rows(pos, row)
            fa[s] = feats
            if s == 0:
                fa[spare] = feats
            vec[s] = halo[i, 0:32, :]
            chunk_no[s] = jnp.where(at_edge, 0, jnp.max(rows_a[6:7, 0:128]).astype(jnp.int32))
    vec[spare] = jnp.zeros_like(vec[spare])
    order = [b for b in range(BOXES) if sources[b]]
    run_steps(
        order, lambda b: sources[b], lambda s: chunk_no[s], lambda b: count_of(counts, b), spare,
        fa, vec, fb, pay, plus, back, tiles, flips, steps, owner, filled,
    )
    total = jnp.zeros((32, 128), F32)
    for b in range(BOXES):
        extra = plus[b]
        base = acc_self[b] + acc_in[b]
        near[b] = base + extra
        weighted = pay[b, 0:32, :].astype(F32) * (base + 2.0 * extra)
        for j in range(points // 128):
            total = total + weighted[:, j * 128:(j + 1) * 128]
    probe_sums[...] = total
    for axis, ref in enumerate((b0, b1, b2)):
        ref[...] = back[4 * axis:4 * axis + 4]


def local_kernel(counts, req_box, req_tgt, here, there, momf, probe_sums, loc, sums, far_acc, live):
    my_y = lax.axis_index("gy")
    my_z = lax.axis_index("gz")
    far_acc[...] = jnp.zeros_like(far_acc)

    def keep(i, n):
        live[n] = i
        return n + (req_box[i >> 6, i & 63] >= 0).astype(jnp.int32)

    used = lax.fori_loop(0, 128, keep, jnp.int32(0), unroll=16)
    shape = (64, 64)
    source_q = lax.broadcasted_iota(jnp.int32, shape, 1)
    target_q = lax.broadcasted_iota(jnp.int32, shape, 0)

    def node(index):
        value = jnp.full(shape, 0.5 + 0.5 * NODES[0], F32)
        for a in range(1, ORDER):
            value = jnp.where(index == a, 0.5 + 0.5 * NODES[a], value)
        return value

    gaps = [node((source_q >> s) & 3) - node((target_q >> s) & 3) for s in (4, 2, 0)]
    group = lax.broadcasted_iota(jnp.int32, (64, 256), 1) >> 5

    def step(g, carry):
        for u in range(8):
            k = g * 8 + u
            i = live[jnp.minimum(k, used - 1)]
            peer = i & 63
            box = req_box[i >> 6, peer]
            tgt = req_tgt[i >> 6, peer]
            peer_y = peer >> 4
            peer_z = peer & 15
            dx = (box >> 2) - (tgt >> 2)
            dy = (peer_y - my_y) * 2 + ((box >> 1) & 1) - ((tgt >> 1) & 1)
            dz = (peer_z - my_z) * 2 + (box & 1) - (tgt & 1)
            ex = gaps[0] + dx.astype(F32)
            ey = gaps[1] + dy.astype(F32)
            ez = gaps[2] + dz.astype(F32)
            coupling = lax.rsqrt(1.0 + ex * ex + ey * ey + ez * ez).astype(BF16)
            rel_y = peer_y ^ my_y
            rel_z = peer_z ^ my_z
            at = ((rel_z >> 1) & 3) * 8 + rel_y * 2 + (rel_z >> 3)
            block = jnp.where((rel_z & 1) == 0, here[at], there[at])
            term = jnp.dot(coupling, block, preferred_element_type=F32)
            wanted = jnp.where(k < used, box, -1)
            far_acc[tgt] += jnp.where(group == wanted, term, 0.0)
        return carry

    lax.fori_loop(0, (used + 7) >> 3, step, 0)
    lane = lax.broadcasted_iota(jnp.int32, (64, 128), 1)
    far_sums = jnp.zeros((64, 128), F32)
    live_points = jnp.int32(0)
    for b in range(BOXES):
        wide = far_acc[b]
        half = wide[:, 0:128] + wide[:, 128:256]
        half = half + pltpu.roll(half, 64, 1)
        half = half + pltpu.roll(half, 32, 1)
        rounded = half.astype(BF16)
        loc[b] = rounded
        moment = momf[:, (b // 4) * 128:(b // 4 + 1) * 128]
        far_sums = far_sums + jnp.where((lane >> 5) == b % 4, rounded.astype(F32) * moment, 0.0)
        live_points = live_points + count_of(counts, b)
    folded = jnp.sum(far_sums, axis=0, keepdims=True)
    folded = folded + pltpu.roll(folded, 64, 1)
    folded = folded + pltpu.roll(folded, 32, 1)
    lane32 = lax.broadcasted_iota(jnp.int32, (32, 128), 1)
    row32 = lax.broadcasted_iota(jnp.int32, (32, 128), 0)
    per_probe = jnp.sum(probe_sums[...], axis=1, keepdims=True)
    flat = jnp.sum(jnp.where(lane32 == row32, per_probe, 0.0), axis=0, keepdims=True)
    row_sums = jnp.where(lane32[0:1] < 32, flat + folded, jnp.where(lane32[0:1] == 32, live_points.astype(F32), 0.0))
    sums[...] = jnp.broadcast_to(row_sums.reshape(1, 1, 128), sums.shape)


def total_kernel(counts, near, r2, r0, r1, loc, tab, kv, done):
    points = tab.shape[-1]
    lane = lax.broadcasted_iota(jnp.int32, (1, points), 1)
    for b in range(BOXES):
        place = (b // 4, b // 2 % 2, b % 2)
        far = lax.dot_general(loc[b][:, 0:32], tab[b], (((0,), (0,)), ((), ())), preferred_element_type=F32)
        total = near[b] + far
        for axis, ref in enumerate((r0, r1, r2)):
            if place[axis] == 0:
                other = [d for d in range(3) if d != axis]
                total = total + ref[place[other[0]] * 2 + place[other[1]]]
        if b == 0:
            done[...] = jnp.zeros_like(done)
        kv[b] = jnp.where(lane < count_of(counts, b), total * (1.0 / math.sqrt(7.0 * points)), 0.0).astype(BF16)


def quad_kernel(gathered, after, quad):
    lane = lax.broadcasted_iota(jnp.int32, (1, 128), 1)
    whole = jnp.sum(gathered[...], axis=0)
    live_points = jnp.sum(jnp.where(lane == 32, whole, 0.0), axis=1, keepdims=True)
    scaled = whole * (1.0 / math.sqrt(7.0 * 1024)) / live_points
    quad[...] = scaled[0, 0:32]


VMEM = pl.BlockSpec(memory_space=pltpu.VMEM)
SMEM = pl.BlockSpec(memory_space=pltpu.SMEM)
ANY = pl.BlockSpec(memory_space=pl.ANY)
PARAMS = pltpu.CompilerParams(vmem_limit_bytes=20 * 2**20)


COST = pl.CostEstimate(flops=12 * 10**9, bytes_accessed=4 * 2**20, transcendentals=10**7)


def join(name, *arrays):
    return pl.pallas_call(
        lambda *refs: None,
        out_shape=[jax.ShapeDtypeStruct(a.shape, a.dtype) for a in arrays],
        in_specs=[ANY] * len(arrays),
        out_specs=[ANY] * len(arrays),
        input_output_aliases={i: i for i in range(len(arrays))},
        compiler_params=pltpu.CompilerParams(vmem_limit_bytes=2**20),
        name=name,
    )(*arrays)


def xor_permute(value, axis, bits):
    count = lax.axis_size(axis)
    return lax.ppermute(value, axis, [(i, i ^ bits) for i in range(count)])


def shards(offsets, probes, counts, req_box, req_tgt):
    points = offsets.shape[-1]
    shape = jax.ShapeDtypeStruct
    face = shape((4, ROWS, points), BF16)
    pay, fa, fb, tab, mom, momf, *faces = pl.pallas_call(
        prep_kernel,
        out_shape=[
            shape((BOXES + 1, ROWS, points), BF16),
            shape((BOXES + 1, FEATS, points), BF16),
            shape((BOXES, FEATS, points), BF16),
            shape((BOXES, 64, points), BF16),
            shape((64, 256), BF16),
            shape((64, 256), F32),
        ] + [face] * 3,
        in_specs=[SMEM, VMEM, VMEM],
        out_specs=[VMEM] * 9,
        scratch_shapes=[
            pltpu.VMEM((8, points), F32),
        ],
        compiler_params=PARAMS,
        name="prep",
    )(counts, jnp.swapaxes(offsets, 2, 3), probes)

    acc_shape = shape((BOXES, 32, points), F32)
    lists = [
        pltpu.VMEM((2, 2 * CHUNK, points), BF16),
        pltpu.VMEM((2, 2 * CHUNK, FEATS), BF16),
        pltpu.SMEM((len(WIDTHS) * REGION,), jnp.int32),
        pltpu.SMEM((len(WIDTHS) * REGION // 2,), jnp.int32),
        pltpu.SMEM((8,), jnp.int32),
    ]

    def inner(name, targets, sources_of, two_way, acc, after):
        has_acc = acc is not None

        def kernel(*refs):
            refs = list(refs)
            head = refs[:4]
            rest = refs[4:]
            acc_ref = rest.pop(0) if has_acc else None
            inner_kernel(targets, sources_of, two_way, *head, acc_ref, *rest)

        args = [counts, fa, pay, fb] + ([acc] if has_acc else []) + [after]
        return pl.pallas_call(
            kernel,
            out_shape=[shape((BOXES + 1, 32, points), F32), shape((8, 128), F32)],
            in_specs=[SMEM, VMEM, VMEM, VMEM] + [VMEM] * has_acc + [ANY],
            out_specs=[VMEM, VMEM],
            scratch_shapes=lists,
            compiler_params=PARAMS,
            cost_estimate=COST,
            name=name,
        )(*args)

    def along(axis, value, step):
        name = ("gx", "gy", "gz")[axis]
        size = lax.axis_size(name)
        return lax.ppermute(value, name, [(i, (i + step) % size) for i in range(size)])

    block = mom.reshape(1, 64, 256)
    twin = xor_permute(block, "gz", 8)
    got = [None] * 3
    got[2] = along(2, faces[2], -1)
    acc_self, tick = inner("self_tiles", list(range(BOXES)), lambda b: [b], False, None, mom)
    tick, twin, face_x = join("join_first", tick, twin, faces[0])
    block = jnp.concatenate([block, twin], axis=0)
    more = [xor_permute(block, "gy", k) for k in (1, 2, 3)]
    got[0] = along(0, face_x, -1)
    acc, tick = inner("pairs_low", [1, 2, 4, 3], lambda b: INNER[b], True, None, tick)
    tick, got[0], got[2], face_y, *more = join("join_second", tick, got[0], got[2], faces[1], *more)
    block = jnp.concatenate([block] + more, axis=0)
    more = [xor_permute(block, "gz", 2 * k) for k in (1, 2, 3)]
    got[1] = along(1, face_y, -1)
    acc, tick = inner("pairs_high", [5, 6, 7], lambda b: INNER[b], True, acc, tick)
    tick, got[1], *more = join("join_third", tick, got[1], *more)
    block = jnp.concatenate([block] + more, axis=0)
    other = xor_permute(block, "gz", 1)
    near, *backs, probe_sums = pl.pallas_call(
        outer_kernel,
        out_shape=[acc_shape] + [shape((4, 32, points), F32)] * 3 + [shape((32, 128), F32)],
        in_specs=[SMEM, VMEM, VMEM, VMEM, VMEM, ANY, VMEM, VMEM, VMEM],
        out_specs=[VMEM] * 5,
        scratch_shapes=[
            pltpu.VMEM((13, FEATS, points), BF16),
            pltpu.VMEM((13, 32, points), BF16),
            pltpu.VMEM((BOXES, 32, points), F32),
            pltpu.VMEM((13, 32, points), F32),
        ] + lists + [pltpu.SMEM((16,), jnp.int32)],
        compiler_params=PARAMS,
        cost_estimate=COST,
        name="face_tiles",
    )(counts, fb, pay, acc_self, acc, tick, *got)
    returned = [None] * 3
    for axis in (2, 0, 1):
        returned[axis] = along(axis, backs[axis], 1)
    devices = lax.axis_size("gx") * lax.axis_size("gy") * lax.axis_size("gz")
    loc, sums = pl.pallas_call(
        local_kernel,
        out_shape=[shape((BOXES, 64, 128), BF16), shape((devices, 1, 128), F32)],
        in_specs=[SMEM, SMEM, SMEM, VMEM, VMEM, VMEM, VMEM],
        out_specs=[VMEM, VMEM],
        scratch_shapes=[
            pltpu.VMEM((BOXES, 64, 256), F32),
            pltpu.SMEM((136,), jnp.int32),
        ],
        compiler_params=PARAMS,
        name="locals",
    )(counts, *[jnp.swapaxes(r, 3, 4).reshape(2, 64) for r in (req_box, req_tgt)], block, other, momf, probe_sums)
    gathered = lax.all_to_all(sums, ("gx", "gy", "gz"), 0, 0, tiled=True)
    kv, total_tick = pl.pallas_call(
        total_kernel,
        out_shape=[shape((BOXES, 32, points), BF16), shape((8, 128), F32)],
        in_specs=[SMEM] + [VMEM] * 6,
        out_specs=[VMEM, VMEM],
        compiler_params=PARAMS,
        cost_estimate=COST,
        name="total",
    )(counts, near, returned[2], returned[0], returned[1], loc, tab)
    quad = pl.pallas_call(
        quad_kernel,
        out_shape=shape((32,), F32),
        in_specs=[VMEM, ANY],
        out_specs=VMEM,
        compiler_params=pltpu.CompilerParams(vmem_limit_bytes=2**21),
        name="quad",
    )(gathered, total_tick)
    return kv.reshape(probes.shape), quad


def solution(mesh):
    placed = (
        P("gx", "gy", "gz", None, None),
        P("gx", "gy", "gz", None, None),
        P("gx", "gy", "gz"),
        P("gx", "gy", "gz", None, None),
        P("gx", "gy", "gz", None, None),
    )
    return jax.shard_map(
        shards,
        mesh=mesh,
        in_specs=placed,
        out_specs=(P("gx", "gy", "gz", None, None), P()),
        check_vma=False,
    )
```

```python
import functools
import math

import jax
import jax.numpy as jnp
from jax import lax
from jax.experimental import pallas as pl
from jax.experimental.pallas import tpu as pltpu
from jax.sharding import PartitionSpec as P

ORDER = 4
CHUNK = 128
BOXES = 8
FEATS = 48
ROWS = 48
F32 = jnp.float32
BF16 = jnp.bfloat16
NODES = [math.cos((2.0 * a + 1.0) * math.pi / (2.0 * ORDER)) for a in range(ORDER)]


def box_id(axis, at, first, second):
    place = [0, 0, 0]
    rest = [d for d in range(3) if d != axis]
    place[axis] = at
    place[rest[0]] = first
    place[rest[1]] = second
    return (place[0] * 2 + place[1]) * 2 + place[2]


def face_boxes(axis, at):
    return [box_id(axis, at, i, j) for i in range(2) for j in range(2)]


def split3(value):
    high = value.astype(BF16).astype(F32)
    rest = value - high
    mid = rest.astype(BF16).astype(F32)
    return high, mid, rest - mid


def row_ids(points):
    return lax.broadcasted_iota(jnp.int32, (8, points), 0)


def source_rows(pos, row):
    p1, p2, p3 = split3(pos)
    n1, n2, n3 = split3(1.0 + jnp.sum(pos * pos, axis=0, keepdims=True))
    s1 = jnp.where(row < 3, p1, jnp.where(row == 3, n1, jnp.where(row == 4, n2, jnp.where(row == 5, n3, 1.0))))
    s2 = p2 + pltpu.roll(p3, 3, 0)
    return jnp.concatenate([s1, s1, s2, s2, s1, jnp.zeros_like(s1)], axis=0).astype(BF16)


def target_rows(pos, row):
    p1, p2, p3 = split3(-2.0 * pos)
    m1, m2, m3 = split3(jnp.sum(pos * pos, axis=0, keepdims=True))
    qa = jnp.where(row < 3, p1, jnp.where(row < 6, 1.0, jnp.where(row == 6, m1, m2)))
    qb = jnp.where(row < 3, p2, jnp.where(row == 6, m3, 0.0))
    qc = p1 + pltpu.roll(p1, 3, 0)
    return jnp.concatenate([qa, qb, qc, p2, p3, jnp.zeros_like(qa)], axis=0).astype(BF16)


def prep_kernel(counts, offs, probes, pay, fa, fb, tab, mom, momf, f0, f1, f2, pad):
    points = offs.shape[-1]
    row = row_ids(points)
    lane = lax.broadcasted_iota(jnp.int32, (1, points), 1)
    faces = (f0, f1, f2)
    pay[BOXES] = jnp.zeros_like(pay[BOXES])
    for k in range(BOXES):
        place = (k // 4, k // 2 % 2, k % 2)
        pad[...] = jnp.zeros_like(pad)
        for d in range(3):
            pad[d:d + 1, :] = offs[place[0], place[1], d, place[2]:place[2] + 1, :]
        off = pad[...]
        shift = jnp.where(row == 0, place[0] - 1.0, jnp.where(row == 1, place[1] - 1.0, jnp.where(row == 2, place[2] - 1.0, 0.0)))
        pos = off + shift
        src = source_rows(pos, row)
        fa[k] = src
        fb[k] = target_rows(pos, row)
        if k == 0:
            fa[BOXES] = src
        count = counts[place]
        chunks = ((count + CHUNK - 1) // CHUNK).astype(F32)
        p1, p2, p3 = split3(pos)
        rows_a = jnp.where(row == 6, chunks, p1 + pltpu.roll(p2, 3, 0))
        tail = jnp.concatenate([rows_a, p3], axis=0).astype(BF16)
        vec = jnp.where(lane < count, probes[place].astype(F32), 0.0).astype(BF16)
        pay[k, 0:32, :] = vec
        pay[k, 32:48, :] = tail
        for axis in range(3):
            if place[axis] == 0:
                other = [d for d in range(3) if d != axis]
                slot = place[other[0]] * 2 + place[other[1]]
                faces[axis][slot, 0:32, :] = vec
                faces[axis][slot, 32:48, :] = tail
        unit = 2.0 * off - 1.0
        t2 = 2.0 * unit * unit - 1.0
        t3 = 2.0 * unit * t2 - unit
        weights = []
        for c in NODES:
            e2 = 2.0 * c * c - 1.0
            e3 = 2.0 * c * e2 - c
            weights.append(0.25 + 0.5 * (c * unit + e2 * t2 + e3 * t3))
        third = jnp.zeros_like(off)
        for d in range(ORDER):
            third = jnp.where(row % 4 == d, weights[d][2:3, :], third)
        seconds = []
        for half in range(2):
            seconds.append(jnp.where(row < 4, weights[2 * half][1:2, :], weights[2 * half + 1][1:2, :]))
        parts = []
        for a in range(ORDER):
            for half in range(2):
                parts.append(weights[a][0:1, :] * seconds[half] * third)
        table = jnp.concatenate(parts, axis=0).astype(BF16)
        tab[k] = table
        moment = lax.dot_general(table, vec, (((1,), (1,)), ((), ())), preferred_element_type=F32)
        momf[:, k * 32:(k + 1) * 32] = moment
    mom[...] = momf[...].astype(BF16)


WIDTHS = (768, 1024)
REGION = 160


def run_steps(targets, sources_of, chunks_of, width_of, dummy, fa, vec, fb, own, out, back, tiles, flips, steps, owner, filled):
    for c in range(len(WIDTHS)):
        filled[c] = 0
    for b in targets:
        count_b = width_of(b)
        kind = jnp.int32(0)
        for width in WIDTHS[:-1]:
            kind = kind + (count_b > width).astype(jnp.int32)
        base = kind * REGION
        at = base + filled[kind]
        for s in sources_of(b):
            for c in range(8):
                steps[at + c] = s * 8 + c
            for c in range(5):
                owner[(at >> 1) + c] = b
            at = at + chunks_of(s)
        steps[at] = dummy * 8
        at = at + (at & 1)
        filled[kind] = at - base
    for c in range(len(WIDTHS)):
        end = c * REGION + filled[c]
        for extra in range(8):
            steps[end + extra] = dummy * 8
            owner[(end + extra) >> 1] = targets[0]

    def columns(index):
        return pl.ds(pl.multiple_of((index & 7) * CHUNK, CHUNK), CHUNK)

    for c, width in enumerate(WIDTHS):
        first_step = c * (REGION // 2)
        total = filled[c] >> 1

        def flip(t, slot):
            for h in range(2):
                index = steps[2 * t + h]
                flips[slot, h * CHUNK:(h + 1) * CHUNK, :] = fa[index >> 3, :, columns(index)].T

        def make(t, slot, width=width):
            target = fb[owner[t], :, 0:width]
            squares = jnp.dot(flips[slot], target, preferred_element_type=F32)
            tiles[slot, :, 0:width] = lax.rsqrt(squares).astype(BF16)

        def use(t, slot, width=width):
            b = owner[t]
            first = steps[2 * t]
            second = steps[2 * t + 1]
            tile = tiles[slot, :, 0:width]
            both = jnp.concatenate([vec[first >> 3, 0:32, columns(first)], vec[second >> 3, 0:32, columns(second)]], axis=1)
            out[b, :, 0:width] += jnp.dot(both, tile, preferred_element_type=F32)
            if back is not None:
                sent = lax.dot_general(own[b, 0:32, 0:width], tile, (((1,), (1,)), ((), ())), preferred_element_type=F32)
                back[first >> 3, :, columns(first)] += sent[:, 0:CHUNK]
                back[second >> 3, :, columns(second)] += sent[:, CHUNK:]

        @pl.when(total > 0)
        def _(flip=flip, make=make, use=use, first_step=first_step, total=total):
            flip(first_step, 0)
            flip(first_step + 1, 1)
            make(first_step, 0)

            def body(k, carry):
                t = first_step + 2 * k
                make(t + 1, 1)
                flip(t + 2, 0)
                use(t, 0)
                make(t + 2, 0)
                flip(t + 3, 1)
                use(t + 1, 1)
                return carry

            whole = (total - 1) >> 1
            lax.fori_loop(0, whole, body, 0)
            last = first_step + 2 * whole

            @pl.when((total & 1) == 1)
            def _():
                use(last, 0)

            @pl.when((total & 1) == 0)
            def _():
                make(last + 1, 1)
                use(last, 0)
                use(last + 1, 1)


INNER = {4: (0,), 2: (0,), 1: (0,), 6: (2, 4), 5: (1, 4), 3: (1, 2), 7: (3, 5, 6)}


def count_of(counts, k):
    return counts[k // 4, k // 2 % 2, k % 2]


def inner_kernel(targets, sources_of, two_way, counts, fa, pay, fb, acc_in, after, out, done, tiles, flips, steps, owner, filled):
    if acc_in is None:
        out[...] = jnp.zeros_like(out)
    else:
        out[...] = acc_in[...]
    run_steps(
        targets, sources_of, lambda s: (count_of(counts, s) + CHUNK - 1) >> 7, lambda b: count_of(counts, b), BOXES,
        fa, pay, fb, pay, out, out if two_way else None, tiles, flips, steps, owner, filled,
    )
    done[...] = jnp.zeros_like(done)


def outer_kernel(counts, fb, pay, acc_self, acc_in, after, halo0, halo1, halo2, near, b0, b1, b2, probe_sums,
                 fa, vec, plus, back, tiles, flips, steps, owner, filled, chunk_no):
    halos = (halo0, halo1, halo2)
    points = fb.shape[-1]
    row = row_ids(points)
    plus[...] = jnp.zeros_like(plus)
    back[...] = jnp.zeros_like(back)
    sources = {b: [] for b in range(BOXES)}
    spare = 12
    for axis in range(3):
        halo = halos[axis]
        name = ("gx", "gy", "gz")[axis]
        at_edge = lax.axis_index(name) == lax.axis_size(name) - 1
        targets = face_boxes(axis, 1)
        for i in range(4):
            s = axis * 4 + i
            sources[targets[i]].append(s)
            tail = halo[i, 32:48, :].astype(F32)
            rows_a = tail[0:8]
            pos = rows_a + pltpu.roll(rows_a, 5, 0) + tail[8:16]
            pos = jnp.where(row < 3, pos + jnp.where(row == axis, 2.0, 0.0), 0.0)
            feats = source_rows(pos, row)
            fa[s] = feats
            if s == 0:
                fa[spare] = feats
            vec[s] = halo[i, 0:32, :]
            chunk_no[s] = jnp.where(at_edge, 0, jnp.max(rows_a[6:7, 0:128]).astype(jnp.int32))
    vec[spare] = jnp.zeros_like(vec[spare])
    order = [b for b in range(BOXES) if sources[b]]
    run_steps(
        order, lambda b: sources[b], lambda s: chunk_no[s], lambda b: count_of(counts, b), spare,
        fa, vec, fb, pay, plus, back, tiles, flips, steps, owner, filled,
    )
    total = jnp.zeros((32, 128), F32)
    for b in range(BOXES):
        extra = plus[b]
        base = acc_self[b] + acc_in[b]
        near[b] = base + extra
        weighted = pay[b, 0:32, :].astype(F32) * (base + 2.0 * extra)
        for j in range(points // 128):
            total = total + weighted[:, j * 128:(j + 1) * 128]
    probe_sums[...] = total
    for axis, ref in enumerate((b0, b1, b2)):
        ref[...] = back[4 * axis:4 * axis + 4]


def local_kernel(counts, req_box, req_tgt, here, there, momf, probe_sums, loc, sums, far_acc, live):
    my_y = lax.axis_index("gy")
    my_z = lax.axis_index("gz")
    far_acc[...] = jnp.zeros_like(far_acc)

    def keep(i, n):
        live[n] = i
        return n + (req_box[i >> 6, i & 63] >= 0).astype(jnp.int32)

    used = lax.fori_loop(0, 128, keep, jnp.int32(0), unroll=16)
    shape = (64, 64)
    source_q = lax.broadcasted_iota(jnp.int32, shape, 1)
    target_q = lax.broadcasted_iota(jnp.int32, shape, 0)

    def node(index):
        value = jnp.full(shape, 0.5 + 0.5 * NODES[0], F32)
        for a in range(1, ORDER):
            value = jnp.where(index == a, 0.5 + 0.5 * NODES[a], value)
        return value

    gaps = [node((source_q >> s) & 3) - node((target_q >> s) & 3) for s in (4, 2, 0)]
    group = lax.broadcasted_iota(jnp.int32, (64, 256), 1) >> 5

    def step(g, carry):
        for u in range(8):
            k = g * 8 + u
            i = live[jnp.minimum(k, used - 1)]
            peer = i & 63
            box = req_box[i >> 6, peer]
            tgt = req_tgt[i >> 6, peer]
            peer_y = peer >> 4
            peer_z = peer & 15
            dx = (box >> 2) - (tgt >> 2)
            dy = (peer_y - my_y) * 2 + ((box >> 1) & 1) - ((tgt >> 1) & 1)
            dz = (peer_z - my_z) * 2 + (box & 1) - (tgt & 1)
            ex = gaps[0] + dx.astype(F32)
            ey = gaps[1] + dy.astype(F32)
            ez = gaps[2] + dz.astype(F32)
            coupling = lax.rsqrt(1.0 + ex * ex + ey * ey + ez * ez).astype(BF16)
            rel_y = peer_y ^ my_y
            rel_z = peer_z ^ my_z
            at = ((rel_z >> 1) & 3) * 8 + rel_y * 2 + (rel_z >> 3)
            block = jnp.where((rel_z & 1) == 0, here[at], there[at])
            term = jnp.dot(coupling, block, preferred_element_type=F32)
            wanted = jnp.where(k < used, box, -1)
            far_acc[tgt] += jnp.where(group == wanted, term, 0.0)
        return carry

    lax.fori_loop(0, (used + 7) >> 3, step, 0)
    lane = lax.broadcasted_iota(jnp.int32, (64, 128), 1)
    far_sums = jnp.zeros((64, 128), F32)
    live_points = jnp.int32(0)
    for b in range(BOXES):
        wide = far_acc[b]
        half = wide[:, 0:128] + wide[:, 128:256]
        half = half + pltpu.roll(half, 64, 1)
        half = half + pltpu.roll(half, 32, 1)
        rounded = half.astype(BF16)
        loc[b] = rounded
        moment = momf[:, (b // 4) * 128:(b // 4 + 1) * 128]
        far_sums = far_sums + jnp.where((lane >> 5) == b % 4, rounded.astype(F32) * moment, 0.0)
        live_points = live_points + count_of(counts, b)
    folded = jnp.sum(far_sums, axis=0, keepdims=True)
    folded = folded + pltpu.roll(folded, 64, 1)
    folded = folded + pltpu.roll(folded, 32, 1)
    lane32 = lax.broadcasted_iota(jnp.int32, (32, 128), 1)
    row32 = lax.broadcasted_iota(jnp.int32, (32, 128), 0)
    per_probe = jnp.sum(probe_sums[...], axis=1, keepdims=True)
    flat = jnp.sum(jnp.where(lane32 == row32, per_probe, 0.0), axis=0, keepdims=True)
    row_sums = jnp.where(lane32[0:1] < 32, flat + folded, jnp.where(lane32[0:1] == 32, live_points.astype(F32), 0.0))
    sums[...] = jnp.broadcast_to(row_sums.reshape(1, 1, 128), sums.shape)


def total_kernel(counts, near, r2, r0, r1, loc, tab, kv, done):
    points = tab.shape[-1]
    lane = lax.broadcasted_iota(jnp.int32, (1, points), 1)
    for b in range(BOXES):
        place = (b // 4, b // 2 % 2, b % 2)
        far = lax.dot_general(loc[b][:, 0:32], tab[b], (((0,), (0,)), ((), ())), preferred_element_type=F32)
        total = near[b] + far
        for axis, ref in enumerate((r0, r1, r2)):
            if place[axis] == 0:
                other = [d for d in range(3) if d != axis]
                total = total + ref[place[other[0]] * 2 + place[other[1]]]
        if b == 0:
            done[...] = jnp.zeros_like(done)
        kv[b] = jnp.where(lane < count_of(counts, b), total * (1.0 / math.sqrt(7.0 * points)), 0.0).astype(BF16)


def quad_kernel(gathered, after, quad):
    lane = lax.broadcasted_iota(jnp.int32, (1, 128), 1)
    whole = jnp.sum(gathered[...], axis=0)
    live_points = jnp.sum(jnp.where(lane == 32, whole, 0.0), axis=1, keepdims=True)
    scaled = whole * (1.0 / math.sqrt(7.0 * 1024)) / live_points
    quad[...] = scaled[0, 0:32]


VMEM = pl.BlockSpec(memory_space=pltpu.VMEM)
SMEM = pl.BlockSpec(memory_space=pltpu.SMEM)
ANY = pl.BlockSpec(memory_space=pl.ANY)
PARAMS = pltpu.CompilerParams(vmem_limit_bytes=20 * 2**20)


COST = pl.CostEstimate(flops=12 * 10**9, bytes_accessed=4 * 2**20, transcendentals=10**7)


def join(name, *arrays):
    return pl.pallas_call(
        lambda *refs: None,
        out_shape=[jax.ShapeDtypeStruct(a.shape, a.dtype) for a in arrays],
        in_specs=[ANY] * len(arrays),
        out_specs=[ANY] * len(arrays),
        input_output_aliases={i: i for i in range(len(arrays))},
        compiler_params=pltpu.CompilerParams(vmem_limit_bytes=2**20),
        name=name,
    )(*arrays)


def xor_permute(value, axis, bits):
    count = lax.axis_size(axis)
    return lax.ppermute(value, axis, [(i, i ^ bits) for i in range(count)])


def shards(offsets, probes, counts, req_box, req_tgt):
    points = offsets.shape[-1]
    shape = jax.ShapeDtypeStruct
    face = shape((4, ROWS, points), BF16)
    pay, fa, fb, tab, mom, momf, *faces = pl.pallas_call(
        prep_kernel,
        out_shape=[
            shape((BOXES + 1, ROWS, points), BF16),
            shape((BOXES + 1, FEATS, points), BF16),
            shape((BOXES, FEATS, points), BF16),
            shape((BOXES, 64, points), BF16),
            shape((64, 256), BF16),
            shape((64, 256), F32),
        ] + [face] * 3,
        in_specs=[SMEM, VMEM, VMEM],
        out_specs=[VMEM] * 9,
        scratch_shapes=[
            pltpu.VMEM((8, points), F32),
        ],
        compiler_params=PARAMS,
        name="prep",
    )(counts, jnp.swapaxes(offsets, 2, 3), probes)

    acc_shape = shape((BOXES, 32, points), F32)
    lists = [
        pltpu.VMEM((2, 2 * CHUNK, points), BF16),
        pltpu.VMEM((2, 2 * CHUNK, FEATS), BF16),
        pltpu.SMEM((len(WIDTHS) * REGION,), jnp.int32),
        pltpu.SMEM((len(WIDTHS) * REGION // 2,), jnp.int32),
        pltpu.SMEM((8,), jnp.int32),
    ]

    def inner(name, targets, sources_of, two_way, acc, after):
        has_acc = acc is not None

        def kernel(*refs):
            refs = list(refs)
            head = refs[:4]
            rest = refs[4:]
            acc_ref = rest.pop(0) if has_acc else None
            inner_kernel(targets, sources_of, two_way, *head, acc_ref, *rest)

        args = [counts, fa, pay, fb] + ([acc] if has_acc else []) + [after]
        return pl.pallas_call(
            kernel,
            out_shape=[shape((BOXES + 1, 32, points), F32), shape((8, 128), F32)],
            in_specs=[SMEM, VMEM, VMEM, VMEM] + [VMEM] * has_acc + [ANY],
            out_specs=[VMEM, VMEM],
            scratch_shapes=lists,
            compiler_params=PARAMS,
            cost_estimate=COST,
            name=name,
        )(*args)

    def along(axis, value, step):
        name = ("gx", "gy", "gz")[axis]
        size = lax.axis_size(name)
        return lax.ppermute(value, name, [(i, (i + step) % size) for i in range(size)])

    block = mom.reshape(1, 64, 256)
    twin = xor_permute(block, "gz", 8)
    got = [None] * 3
    got[2] = along(2, faces[2], -1)
    acc_self, tick = inner("self_tiles", list(range(BOXES)), lambda b: [b], False, None, mom)
    tick, twin, face_x = join("join_first", tick, twin, faces[0])
    block = jnp.concatenate([block, twin], axis=0)
    more = [xor_permute(block, "gy", k) for k in (1, 2, 3)]
    got[0] = along(0, face_x, -1)
    acc, tick = inner("pairs_low", [1, 2, 4, 3], lambda b: INNER[b], True, None, tick)
    tick, got[2], face_y, *more = join("join_second", tick, got[2], faces[1], *more)
    block = jnp.concatenate([block] + more, axis=0)
    more = [xor_permute(block, "gz", 2 * k) for k in (1, 2, 3)]
    got[1] = along(1, face_y, -1)
    acc, tick = inner("pairs_high", [5, 6, 7], lambda b: INNER[b], True, acc, tick)
    tick, got[0], got[1], *more = join("join_third", tick, got[0], got[1], *more)
    block = jnp.concatenate([block] + more, axis=0)
    other = xor_permute(block, "gz", 1)
    near, *backs, probe_sums = pl.pallas_call(
        outer_kernel,
        out_shape=[acc_shape] + [shape((4, 32, points), F32)] * 3 + [shape((32, 128), F32)],
        in_specs=[SMEM, VMEM, VMEM, VMEM, VMEM, ANY, VMEM, VMEM, VMEM],
        out_specs=[VMEM] * 5,
        scratch_shapes=[
            pltpu.VMEM((13, FEATS, points), BF16),
            pltpu.VMEM((13, 32, points), BF16),
            pltpu.VMEM((BOXES, 32, points), F32),
            pltpu.VMEM((13, 32, points), F32),
        ] + lists + [pltpu.SMEM((16,), jnp.int32)],
        compiler_params=PARAMS,
        cost_estimate=COST,
        name="face_tiles",
    )(counts, fb, pay, acc_self, acc, tick, *got)
    returned = [None] * 3
    for axis in (2, 0, 1):
        returned[axis] = along(axis, backs[axis], 1)
    devices = lax.axis_size("gx") * lax.axis_size("gy") * lax.axis_size("gz")
    loc, sums = pl.pallas_call(
        local_kernel,
        out_shape=[shape((BOXES, 64, 128), BF16), shape((devices, 1, 128), F32)],
        in_specs=[SMEM, SMEM, SMEM, VMEM, VMEM, VMEM, VMEM],
        out_specs=[VMEM, VMEM],
        scratch_shapes=[
            pltpu.VMEM((BOXES, 64, 256), F32),
            pltpu.SMEM((136,), jnp.int32),
        ],
        compiler_params=PARAMS,
        name="locals",
    )(counts, *[jnp.swapaxes(r, 3, 4).reshape(2, 64) for r in (req_box, req_tgt)], block, other, momf, probe_sums)
    gathered = lax.all_to_all(sums, ("gx", "gy", "gz"), 0, 0, tiled=True)
    kv, total_tick = pl.pallas_call(
        total_kernel,
        out_shape=[shape((BOXES, 32, points), BF16), shape((8, 128), F32)],
        in_specs=[SMEM] + [VMEM] * 6,
        out_specs=[VMEM, VMEM],
        compiler_params=PARAMS,
        cost_estimate=COST,
        name="total",
    )(counts, near, returned[2], returned[0], returned[1], loc, tab)
    quad = pl.pallas_call(
        quad_kernel,
        out_shape=shape((32,), F32),
        in_specs=[VMEM, ANY],
        out_specs=VMEM,
        compiler_params=pltpu.CompilerParams(vmem_limit_bytes=2**21),
        name="quad",
    )(gathered, total_tick)
    return kv.reshape(probes.shape), quad


def solution(mesh):
    placed = (
        P("gx", "gy", "gz", None, None),
        P("gx", "gy", "gz", None, None),
        P("gx", "gy", "gz"),
        P("gx", "gy", "gz", None, None),
        P("gx", "gy", "gz", None, None),
    )
    return jax.shard_map(
        shards,
        mesh=mesh,
        in_specs=placed,
        out_specs=(P("gx", "gy", "gz", None, None), P()),
        check_vma=False,
    )
```

```python
import functools
import math

import jax
import jax.numpy as jnp
from jax import lax
from jax.experimental import pallas as pl
from jax.experimental.pallas import tpu as pltpu
from jax.sharding import PartitionSpec as P

ORDER = 4
CHUNK = 128
BOXES = 8
FEATS = 48
ROWS = 48
F32 = jnp.float32
BF16 = jnp.bfloat16
NODES = [math.cos((2.0 * a + 1.0) * math.pi / (2.0 * ORDER)) for a in range(ORDER)]


def box_id(axis, at, first, second):
    place = [0, 0, 0]
    rest = [d for d in range(3) if d != axis]
    place[axis] = at
    place[rest[0]] = first
    place[rest[1]] = second
    return (place[0] * 2 + place[1]) * 2 + place[2]


def face_boxes(axis, at):
    return [box_id(axis, at, i, j) for i in range(2) for j in range(2)]


def split3(value):
    high = value.astype(BF16).astype(F32)
    rest = value - high
    mid = rest.astype(BF16).astype(F32)
    return high, mid, rest - mid


def row_ids(points):
    return lax.broadcasted_iota(jnp.int32, (8, points), 0)


def source_rows(pos, row):
    p1, p2, p3 = split3(pos)
    n1, n2, n3 = split3(1.0 + jnp.sum(pos * pos, axis=0, keepdims=True))
    s1 = jnp.where(row < 3, p1, jnp.where(row == 3, n1, jnp.where(row == 4, n2, jnp.where(row == 5, n3, 1.0))))
    s2 = p2 + pltpu.roll(p3, 3, 0)
    return jnp.concatenate([s1, s1, s2, s2, s1, jnp.zeros_like(s1)], axis=0).astype(BF16)


def target_rows(pos, row):
    p1, p2, p3 = split3(-2.0 * pos)
    m1, m2, m3 = split3(jnp.sum(pos * pos, axis=0, keepdims=True))
    qa = jnp.where(row < 3, p1, jnp.where(row < 6, 1.0, jnp.where(row == 6, m1, m2)))
    qb = jnp.where(row < 3, p2, jnp.where(row == 6, m3, 0.0))
    qc = p1 + pltpu.roll(p1, 3, 0)
    return jnp.concatenate([qa, qb, qc, p2, p3, jnp.zeros_like(qa)], axis=0).astype(BF16)


def prep_kernel(counts, offs, probes, pay, fa, fb, tab, mom, momf, f0, f1, f2, pad):
    points = offs.shape[-1]
    row = row_ids(points)
    lane = lax.broadcasted_iota(jnp.int32, (1, points), 1)
    faces = (f0, f1, f2)
    pay[BOXES] = jnp.zeros_like(pay[BOXES])
    for k in range(BOXES):
        place = (k // 4, k // 2 % 2, k % 2)
        pad[...] = jnp.zeros_like(pad)
        for d in range(3):
            pad[d:d + 1, :] = offs[place[0], place[1], d, place[2]:place[2] + 1, :]
        off = pad[...]
        shift = jnp.where(row == 0, place[0] - 1.0, jnp.where(row == 1, place[1] - 1.0, jnp.where(row == 2, place[2] - 1.0, 0.0)))
        pos = off + shift
        src = source_rows(pos, row)
        fa[k] = src
        fb[k] = target_rows(pos, row)
        if k == 0:
            fa[BOXES] = src
        count = counts[place]
        chunks = ((count + CHUNK - 1) // CHUNK).astype(F32)
        p1, p2, p3 = split3(pos)
        rows_a = jnp.where(row == 6, chunks, p1 + pltpu.roll(p2, 3, 0))
        tail = jnp.concatenate([rows_a, p3], axis=0).astype(BF16)
        vec = jnp.where(lane < count, probes[place].astype(F32), 0.0).astype(BF16)
        pay[k, 0:32, :] = vec
        pay[k, 32:48, :] = tail
        for axis in range(3):
            if place[axis] == 0:
                other = [d for d in range(3) if d != axis]
                slot = place[other[0]] * 2 + place[other[1]]
                faces[axis][slot, 0:32, :] = vec
                faces[axis][slot, 32:48, :] = tail
        unit = 2.0 * off - 1.0
        t2 = 2.0 * unit * unit - 1.0
        t3 = 2.0 * unit * t2 - unit
        weights = []
        for c in NODES:
            e2 = 2.0 * c * c - 1.0
            e3 = 2.0 * c * e2 - c
            weights.append(0.25 + 0.5 * (c * unit + e2 * t2 + e3 * t3))
        third = jnp.zeros_like(off)
        for d in range(ORDER):
            third = jnp.where(row % 4 == d, weights[d][2:3, :], third)
        seconds = []
        for half in range(2):
            seconds.append(jnp.where(row < 4, weights[2 * half][1:2, :], weights[2 * half + 1][1:2, :]))
        parts = []
        for a in range(ORDER):
            for half in range(2):
                parts.append(weights[a][0:1, :] * seconds[half] * third)
        table = jnp.concatenate(parts, axis=0).astype(BF16)
        tab[k] = table
        moment = lax.dot_general(table, vec, (((1,), (1,)), ((), ())), preferred_element_type=F32)
        momf[:, k * 32:(k + 1) * 32] = moment
    mom[...] = momf[...].astype(BF16)


WIDTHS = (768, 1024)
REGION = 160


def run_steps(targets, sources_of, chunks_of, width_of, dummy, fa, vec, fb, own, out, back, tiles, flips, steps, owner, filled):
    for c in range(len(WIDTHS)):
        filled[c] = 0
    for b in targets:
        count_b = width_of(b)
        kind = jnp.int32(0)
        for width in WIDTHS[:-1]:
            kind = kind + (count_b > width).astype(jnp.int32)
        base = kind * REGION
        at = base + filled[kind]
        for s in sources_of(b):
            for c in range(8):
                steps[at + c] = s * 8 + c
            for c in range(5):
                owner[(at >> 1) + c] = b
            at = at + chunks_of(s)
        steps[at] = dummy * 8
        at = at + (at & 1)
        filled[kind] = at - base
    for c in range(len(WIDTHS)):
        end = c * REGION + filled[c]
        for extra in range(8):
            steps[end + extra] = dummy * 8
            owner[(end + extra) >> 1] = targets[0]

    def columns(index):
        return pl.ds(pl.multiple_of((index & 7) * CHUNK, CHUNK), CHUNK)

    def flip(t, slot):
        for h in range(2):
            index = steps[2 * t + h]
            flips[slot, h * CHUNK:(h + 1) * CHUNK, :] = fa[index >> 3, :, columns(index)].T

    def make(t, slot, width):
        target = fb[owner[t], :, 0:width]
        squares = jnp.dot(flips[slot], target, preferred_element_type=F32)
        tiles[slot, :, 0:width] = lax.rsqrt(squares).astype(BF16)

    def use(t, slot, width):
        b = owner[t]
        first = steps[2 * t]
        second = steps[2 * t + 1]
        tile = tiles[slot, :, 0:width]
        both = jnp.concatenate([vec[first >> 3, 0:32, columns(first)], vec[second >> 3, 0:32, columns(second)]], axis=1)
        out[b, :, 0:width] += jnp.dot(both, tile, preferred_element_type=F32)
        if back is not None:
            sent = lax.dot_general(own[b, 0:32, 0:width], tile, (((1,), (1,)), ((), ())), preferred_element_type=F32)
            back[first >> 3, :, columns(first)] += sent[:, 0:CHUNK]
            back[second >> 3, :, columns(second)] += sent[:, CHUNK:]

    def begin(c):
        if c < len(WIDTHS):
            flip(c * (REGION // 2), 2 * c)
            flip(c * (REGION // 2) + 1, 2 * c + 1)
            make(c * (REGION // 2), 2 * c, WIDTHS[c])

    begin(0)
    for c, width in enumerate(WIDTHS):
        first_step = c * (REGION // 2)
        total = filled[c] >> 1
        even, odd = 2 * c, 2 * c + 1

        def body(k, carry, first_step=first_step, width=width, even=even, odd=odd):
            t = first_step + 2 * k
            make(t + 1, odd, width)
            flip(t + 2, even)
            use(t, even, width)
            make(t + 2, even, width)
            flip(t + 3, odd)
            use(t + 1, odd, width)
            return carry

        whole = jnp.maximum(total - 1, 0) >> 1
        lax.fori_loop(0, whole, body, 0)
        last = first_step + 2 * whole
        left = total - 2 * whole

        if c + 1 < len(WIDTHS):
            @pl.when(left == 0)
            def _(c=c):
                begin(c + 1)

        @pl.when(left == 1)
        def _(c=c, last=last, width=width, even=even):
            use(last, even, width)
            begin(c + 1)

        @pl.when(left == 2)
        def _(c=c, last=last, width=width, even=even, odd=odd):
            make(last + 1, odd, width)
            use(last, even, width)
            begin(c + 1)
            use(last + 1, odd, width)


INNER = {4: (0,), 2: (0,), 1: (0,), 6: (2, 4), 5: (1, 4), 3: (1, 2), 7: (3, 5, 6)}


def count_of(counts, k):
    return counts[k // 4, k // 2 % 2, k % 2]


def inner_kernel(targets, sources_of, two_way, counts, fa, pay, fb, acc_in, after, out, done, tiles, flips, steps, owner, filled):
    if acc_in is None:
        out[...] = jnp.zeros_like(out)
    else:
        out[...] = acc_in[...]
    run_steps(
        targets, sources_of, lambda s: (count_of(counts, s) + CHUNK - 1) >> 7, lambda b: count_of(counts, b), BOXES,
        fa, pay, fb, pay, out, out if two_way else None, tiles, flips, steps, owner, filled,
    )
    done[...] = jnp.zeros_like(done)


def outer_kernel(counts, fb, pay, acc_self, acc_in, after, halo0, halo1, halo2, near, b0, b1, b2, probe_sums,
                 fa, vec, plus, back, tiles, flips, steps, owner, filled, chunk_no):
    halos = (halo0, halo1, halo2)
    points = fb.shape[-1]
    row = row_ids(points)
    plus[...] = jnp.zeros_like(plus)
    back[...] = jnp.zeros_like(back)
    sources = {b: [] for b in range(BOXES)}
    spare = 12
    for axis in range(3):
        halo = halos[axis]
        name = ("gx", "gy", "gz")[axis]
        at_edge = lax.axis_index(name) == lax.axis_size(name) - 1
        targets = face_boxes(axis, 1)
        for i in range(4):
            s = axis * 4 + i
            sources[targets[i]].append(s)
            tail = halo[i, 32:48, :].astype(F32)
            rows_a = tail[0:8]
            pos = rows_a + pltpu.roll(rows_a, 5, 0) + tail[8:16]
            pos = jnp.where(row < 3, pos + jnp.where(row == axis, 2.0, 0.0), 0.0)
            feats = source_rows(pos, row)
            fa[s] = feats
            if s == 0:
                fa[spare] = feats
            vec[s] = halo[i, 0:32, :]
            chunk_no[s] = jnp.where(at_edge, 0, jnp.max(rows_a[6:7, 0:128]).astype(jnp.int32))
    vec[spare] = jnp.zeros_like(vec[spare])
    order = [b for b in range(BOXES) if sources[b]]
    run_steps(
        order, lambda b: sources[b], lambda s: chunk_no[s], lambda b: count_of(counts, b), spare,
        fa, vec, fb, pay, plus, back, tiles, flips, steps, owner, filled,
    )
    total = jnp.zeros((32, 128), F32)
    for b in range(BOXES):
        extra = plus[b]
        base = acc_self[b] + acc_in[b]
        near[b] = base + extra
        weighted = pay[b, 0:32, :].astype(F32) * (base + 2.0 * extra)
        for j in range(points // 128):
            total = total + weighted[:, j * 128:(j + 1) * 128]
    probe_sums[...] = total
    for axis, ref in enumerate((b0, b1, b2)):
        ref[...] = back[4 * axis:4 * axis + 4]


def local_kernel(counts, req_box, req_tgt, here, there, momf, probe_sums, loc, sums, far_acc, live):
    my_y = lax.axis_index("gy")
    my_z = lax.axis_index("gz")
    far_acc[...] = jnp.zeros_like(far_acc)

    def keep(i, n):
        live[n] = i
        return n + (req_box[i >> 6, i & 63] >= 0).astype(jnp.int32)

    used = lax.fori_loop(0, 128, keep, jnp.int32(0), unroll=16)
    shape = (64, 64)
    source_q = lax.broadcasted_iota(jnp.int32, shape, 1)
    target_q = lax.broadcasted_iota(jnp.int32, shape, 0)

    def node(index):
        value = jnp.full(shape, 0.5 + 0.5 * NODES[0], F32)
        for a in range(1, ORDER):
            value = jnp.where(index == a, 0.5 + 0.5 * NODES[a], value)
        return value

    gaps = [node((source_q >> s) & 3) - node((target_q >> s) & 3) for s in (4, 2, 0)]
    group = lax.broadcasted_iota(jnp.int32, (64, 256), 1) >> 5

    def step(g, carry):
        for u in range(8):
            k = g * 8 + u
            i = live[jnp.minimum(k, used - 1)]
            peer = i & 63
            box = req_box[i >> 6, peer]
            tgt = req_tgt[i >> 6, peer]
            peer_y = peer >> 4
            peer_z = peer & 15
            dx = (box >> 2) - (tgt >> 2)
            dy = (peer_y - my_y) * 2 + ((box >> 1) & 1) - ((tgt >> 1) & 1)
            dz = (peer_z - my_z) * 2 + (box & 1) - (tgt & 1)
            ex = gaps[0] + dx.astype(F32)
            ey = gaps[1] + dy.astype(F32)
            ez = gaps[2] + dz.astype(F32)
            coupling = lax.rsqrt(1.0 + ex * ex + ey * ey + ez * ez).astype(BF16)
            rel_y = peer_y ^ my_y
            rel_z = peer_z ^ my_z
            at = ((rel_z >> 1) & 3) * 8 + rel_y * 2 + (rel_z >> 3)
            block = jnp.where((rel_z & 1) == 0, here[at], there[at])
            term = jnp.dot(coupling, block, preferred_element_type=F32)
            wanted = jnp.where(k < used, box, -1)
            far_acc[tgt] += jnp.where(group == wanted, term, 0.0)
        return carry

    lax.fori_loop(0, (used + 7) >> 3, step, 0)
    lane = lax.broadcasted_iota(jnp.int32, (64, 128), 1)
    far_sums = jnp.zeros((64, 128), F32)
    live_points = jnp.int32(0)
    for b in range(BOXES):
        wide = far_acc[b]
        half = wide[:, 0:128] + wide[:, 128:256]
        half = half + pltpu.roll(half, 64, 1)
        half = half + pltpu.roll(half, 32, 1)
        rounded = half.astype(BF16)
        loc[b] = rounded
        moment = momf[:, (b // 4) * 128:(b // 4 + 1) * 128]
        far_sums = far_sums + jnp.where((lane >> 5) == b % 4, rounded.astype(F32) * moment, 0.0)
        live_points = live_points + count_of(counts, b)
    folded = jnp.sum(far_sums, axis=0, keepdims=True)
    folded = folded + pltpu.roll(folded, 64, 1)
    folded = folded + pltpu.roll(folded, 32, 1)
    lane32 = lax.broadcasted_iota(jnp.int32, (32, 128), 1)
    row32 = lax.broadcasted_iota(jnp.int32, (32, 128), 0)
    per_probe = jnp.sum(probe_sums[...], axis=1, keepdims=True)
    flat = jnp.sum(jnp.where(lane32 == row32, per_probe, 0.0), axis=0, keepdims=True)
    row_sums = jnp.where(lane32[0:1] < 32, flat + folded, jnp.where(lane32[0:1] == 32, live_points.astype(F32), 0.0))
    sums[...] = jnp.broadcast_to(row_sums.reshape(1, 1, 128), sums.shape)


def total_kernel(counts, near, r2, r1, r0, loc, tab, kv, done):
    points = tab.shape[-1]
    lane = lax.broadcasted_iota(jnp.int32, (1, points), 1)
    for b in range(BOXES):
        place = (b // 4, b // 2 % 2, b % 2)
        far = lax.dot_general(loc[b][:, 0:32], tab[b], (((0,), (0,)), ((), ())), preferred_element_type=F32)
        total = near[b] + far
        for axis, ref in enumerate((r0, r1, r2)):
            if place[axis] == 0:
                other = [d for d in range(3) if d != axis]
                total = total + ref[place[other[0]] * 2 + place[other[1]]]
        if b == 0:
            done[...] = jnp.zeros_like(done)
        kv[b] = jnp.where(lane < count_of(counts, b), total * (1.0 / math.sqrt(7.0 * points)), 0.0).astype(BF16)


def quad_kernel(gathered, after, quad):
    lane = lax.broadcasted_iota(jnp.int32, (1, 128), 1)
    whole = jnp.sum(gathered[...], axis=0)
    live_points = jnp.sum(jnp.where(lane == 32, whole, 0.0), axis=1, keepdims=True)
    scaled = whole * (1.0 / math.sqrt(7.0 * 1024)) / live_points
    quad[...] = scaled[0, 0:32]


VMEM = pl.BlockSpec(memory_space=pltpu.VMEM)
SMEM = pl.BlockSpec(memory_space=pltpu.SMEM)
ANY = pl.BlockSpec(memory_space=pl.ANY)
PARAMS = pltpu.CompilerParams(vmem_limit_bytes=20 * 2**20)


COST = pl.CostEstimate(flops=12 * 10**9, bytes_accessed=4 * 2**20, transcendentals=10**7)


def join(name, *arrays):
    return pl.pallas_call(
        lambda *refs: None,
        out_shape=[jax.ShapeDtypeStruct(a.shape, a.dtype) for a in arrays],
        in_specs=[ANY] * len(arrays),
        out_specs=[ANY] * len(arrays),
        input_output_aliases={i: i for i in range(len(arrays))},
        compiler_params=pltpu.CompilerParams(vmem_limit_bytes=2**20),
        name=name,
    )(*arrays)


def xor_permute(value, axis, bits):
    count = lax.axis_size(axis)
    return lax.ppermute(value, axis, [(i, i ^ bits) for i in range(count)])


def shards(offsets, probes, counts, req_box, req_tgt):
    points = offsets.shape[-1]
    shape = jax.ShapeDtypeStruct
    face = shape((4, ROWS, points), BF16)
    pay, fa, fb, tab, mom, momf, *faces = pl.pallas_call(
        prep_kernel,
        out_shape=[
            shape((BOXES + 1, ROWS, points), BF16),
            shape((BOXES + 1, FEATS, points), BF16),
            shape((BOXES, FEATS, points), BF16),
            shape((BOXES, 64, points), BF16),
            shape((64, 256), BF16),
            shape((64, 256), F32),
        ] + [face] * 3,
        in_specs=[SMEM, VMEM, VMEM],
        out_specs=[VMEM] * 9,
        scratch_shapes=[
            pltpu.VMEM((8, points), F32),
        ],
        compiler_params=PARAMS,
        name="prep",
    )(counts, jnp.swapaxes(offsets, 2, 3), probes)

    acc_shape = shape((BOXES, 32, points), F32)
    lists = [
        pltpu.VMEM((2 * len(WIDTHS), 2 * CHUNK, points), BF16),
        pltpu.VMEM((2 * len(WIDTHS), 2 * CHUNK, FEATS), BF16),
        pltpu.SMEM((len(WIDTHS) * REGION,), jnp.int32),
        pltpu.SMEM((len(WIDTHS) * REGION // 2,), jnp.int32),
        pltpu.SMEM((8,), jnp.int32),
    ]

    def inner(name, targets, sources_of, two_way, acc, after):
        has_acc = acc is not None

        def kernel(*refs):
            refs = list(refs)
            head = refs[:4]
            rest = refs[4:]
            acc_ref = rest.pop(0) if has_acc else None
            inner_kernel(targets, sources_of, two_way, *head, acc_ref, *rest)

        args = [counts, fa, pay, fb] + ([acc] if has_acc else []) + [after]
        return pl.pallas_call(
            kernel,
            out_shape=[shape((BOXES + 1, 32, points), F32), shape((8, 128), F32)],
            in_specs=[SMEM, VMEM, VMEM, VMEM] + [VMEM] * has_acc + [ANY],
            out_specs=[VMEM, VMEM],
            scratch_shapes=lists,
            compiler_params=PARAMS,
            cost_estimate=COST,
            name=name,
        )(*args)

    def along(axis, value, step):
        name = ("gx", "gy", "gz")[axis]
        size = lax.axis_size(name)
        return lax.ppermute(value, name, [(i, (i + step) % size) for i in range(size)])

    block = mom.reshape(1, 64, 256)
    twin = xor_permute(block, "gz", 8)
    got = [None] * 3
    got[2] = along(2, faces[2], -1)
    acc_self, tick = inner("self_tiles", list(range(BOXES)), lambda b: [b], False, None, mom)
    tick, twin, face_x = join("join_first", tick, twin, faces[0])
    block = jnp.concatenate([block, twin], axis=0)
    more = [xor_permute(block, "gy", k) for k in (1, 2, 3)]
    got[0] = along(0, face_x, -1)
    acc, tick = inner("pairs_low", [1, 2, 4, 3], lambda b: INNER[b], True, None, tick)
    tick, got[2], face_y, *more = join("join_second", tick, got[2], faces[1], *more)
    block = jnp.concatenate([block] + more, axis=0)
    more = [xor_permute(block, "gz", 2 * k) for k in (1, 2, 3)]
    got[1] = along(1, face_y, -1)
    acc, tick = inner("pairs_high", [5, 6, 7], lambda b: INNER[b], True, acc, tick)
    tick, got[0], got[1], *more = join("join_third", tick, got[0], got[1], *more)
    block = jnp.concatenate([block] + more, axis=0)
    other = xor_permute(block, "gz", 1)
    near, *backs, probe_sums = pl.pallas_call(
        outer_kernel,
        out_shape=[acc_shape] + [shape((4, 32, points), F32)] * 3 + [shape((32, 128), F32)],
        in_specs=[SMEM, VMEM, VMEM, VMEM, VMEM, ANY, VMEM, VMEM, VMEM],
        out_specs=[VMEM] * 5,
        scratch_shapes=[
            pltpu.VMEM((13, FEATS, points), BF16),
            pltpu.VMEM((13, 32, points), BF16),
            pltpu.VMEM((BOXES, 32, points), F32),
            pltpu.VMEM((13, 32, points), F32),
        ] + lists + [pltpu.SMEM((16,), jnp.int32)],
        compiler_params=PARAMS,
        cost_estimate=COST,
        name="face_tiles",
    )(counts, fb, pay, acc_self, acc, tick, *got)
    returned = [None] * 3
    for axis in (2, 0, 1):
        returned[axis] = along(axis, backs[axis], 1)
    devices = lax.axis_size("gx") * lax.axis_size("gy") * lax.axis_size("gz")
    loc, sums = pl.pallas_call(
        local_kernel,
        out_shape=[shape((BOXES, 64, 128), BF16), shape((devices, 1, 128), F32)],
        in_specs=[SMEM, SMEM, SMEM, VMEM, VMEM, VMEM, VMEM],
        out_specs=[VMEM, VMEM],
        scratch_shapes=[
            pltpu.VMEM((BOXES, 64, 256), F32),
            pltpu.SMEM((136,), jnp.int32),
        ],
        compiler_params=PARAMS,
        name="locals",
    )(counts, *[jnp.swapaxes(r, 3, 4).reshape(2, 64) for r in (req_box, req_tgt)], block, other, momf, probe_sums)
    gathered = lax.all_to_all(sums, ("gx", "gy", "gz"), 0, 0, tiled=True)
    kv, total_tick = pl.pallas_call(
        total_kernel,
        out_shape=[shape((BOXES, 32, points), BF16), shape((8, 128), F32)],
        in_specs=[SMEM] + [VMEM] * 6,
        out_specs=[VMEM, VMEM],
        compiler_params=PARAMS,
        cost_estimate=COST,
        name="total",
    )(counts, near, returned[2], returned[1], returned[0], loc, tab)
    quad = pl.pallas_call(
        quad_kernel,
        out_shape=shape((32,), F32),
        in_specs=[VMEM, ANY],
        out_specs=VMEM,
        compiler_params=pltpu.CompilerParams(vmem_limit_bytes=2**21),
        name="quad",
    )(gathered, total_tick)
    return kv.reshape(probes.shape), quad


def solution(mesh):
    placed = (
        P("gx", "gy", "gz", None, None),
        P("gx", "gy", "gz", None, None),
        P("gx", "gy", "gz"),
        P("gx", "gy", "gz", None, None),
        P("gx", "gy", "gz", None, None),
    )
    return jax.shard_map(
        shards,
        mesh=mesh,
        in_specs=placed,
        out_specs=(P("gx", "gy", "gz", None, None), P()),
        check_vma=False,
    )
```

```python
import functools
import math

import jax
import jax.numpy as jnp
from jax import lax
from jax.experimental import pallas as pl
from jax.experimental.pallas import tpu as pltpu
from jax.sharding import PartitionSpec as P

ORDER = 4
CHUNK = 128
BOXES = 8
FEATS = 48
ROWS = 48
F32 = jnp.float32
BF16 = jnp.bfloat16
NODES = [math.cos((2.0 * a + 1.0) * math.pi / (2.0 * ORDER)) for a in range(ORDER)]


def box_id(axis, at, first, second):
    place = [0, 0, 0]
    rest = [d for d in range(3) if d != axis]
    place[axis] = at
    place[rest[0]] = first
    place[rest[1]] = second
    return (place[0] * 2 + place[1]) * 2 + place[2]


def face_boxes(axis, at):
    return [box_id(axis, at, i, j) for i in range(2) for j in range(2)]


def split3(value):
    high = value.astype(BF16).astype(F32)
    rest = value - high
    mid = rest.astype(BF16).astype(F32)
    return high, mid, rest - mid


def row_ids(points):
    return lax.broadcasted_iota(jnp.int32, (8, points), 0)


def source_rows(pos, row):
    p1, p2, p3 = split3(pos)
    n1, n2, n3 = split3(1.0 + jnp.sum(pos * pos, axis=0, keepdims=True))
    s1 = jnp.where(row < 3, p1, jnp.where(row == 3, n1, jnp.where(row == 4, n2, jnp.where(row == 5, n3, 1.0))))
    s2 = p2 + pltpu.roll(p3, 3, 0)
    return jnp.concatenate([s1, s1, s2, s2, s1, jnp.zeros_like(s1)], axis=0).astype(BF16)


def target_rows(pos, row):
    p1, p2, p3 = split3(-2.0 * pos)
    m1, m2, m3 = split3(jnp.sum(pos * pos, axis=0, keepdims=True))
    qa = jnp.where(row < 3, p1, jnp.where(row < 6, 1.0, jnp.where(row == 6, m1, m2)))
    qb = jnp.where(row < 3, p2, jnp.where(row == 6, m3, 0.0))
    qc = p1 + pltpu.roll(p1, 3, 0)
    return jnp.concatenate([qa, qb, qc, p2, p3, jnp.zeros_like(qa)], axis=0).astype(BF16)


def prep_kernel(counts, offs, probes, pay, fa, fb, tab, mom, momf, f0, f1, f2, pad):
    points = offs.shape[-1]
    row = row_ids(points)
    lane = lax.broadcasted_iota(jnp.int32, (1, points), 1)
    faces = (f0, f1, f2)
    pay[BOXES] = jnp.zeros_like(pay[BOXES])
    for k in range(BOXES):
        place = (k // 4, k // 2 % 2, k % 2)
        pad[...] = jnp.zeros_like(pad)
        for d in range(3):
            pad[d:d + 1, :] = offs[place[0], place[1], d, place[2]:place[2] + 1, :]
        off = pad[...]
        shift = jnp.where(row == 0, place[0] - 1.0, jnp.where(row == 1, place[1] - 1.0, jnp.where(row == 2, place[2] - 1.0, 0.0)))
        pos = off + shift
        src = source_rows(pos, row)
        fa[k] = src
        fb[k] = target_rows(pos, row)
        if k == 0:
            fa[BOXES] = src
        count = counts[place]
        chunks = ((count + CHUNK - 1) // CHUNK).astype(F32)
        p1, p2, p3 = split3(pos)
        rows_a = jnp.where(row == 6, chunks, p1 + pltpu.roll(p2, 3, 0))
        tail = jnp.concatenate([rows_a, p3], axis=0).astype(BF16)
        vec = jnp.where(lane < count, probes[place].astype(F32), 0.0).astype(BF16)
        pay[k, 0:32, :] = vec
        pay[k, 32:48, :] = tail
        for axis in range(3):
            if place[axis] == 0:
                other = [d for d in range(3) if d != axis]
                slot = place[other[0]] * 2 + place[other[1]]
                faces[axis][slot, 0:32, :] = vec
                faces[axis][slot, 32:48, :] = tail
        unit = 2.0 * off - 1.0
        t2 = 2.0 * unit * unit - 1.0
        t3 = 2.0 * unit * t2 - unit
        weights = []
        for c in NODES:
            e2 = 2.0 * c * c - 1.0
            e3 = 2.0 * c * e2 - c
            weights.append(0.25 + 0.5 * (c * unit + e2 * t2 + e3 * t3))
        third = jnp.zeros_like(off)
        for d in range(ORDER):
            third = jnp.where(row % 4 == d, weights[d][2:3, :], third)
        seconds = []
        for half in range(2):
            seconds.append(jnp.where(row < 4, weights[2 * half][1:2, :], weights[2 * half + 1][1:2, :]))
        parts = []
        for a in range(ORDER):
            for half in range(2):
                parts.append(weights[a][0:1, :] * seconds[half] * third)
        table = jnp.concatenate(parts, axis=0).astype(BF16)
        tab[k] = table
        moment = lax.dot_general(table, vec, (((1,), (1,)), ((), ())), preferred_element_type=F32)
        momf[:, k * 32:(k + 1) * 32] = moment
    mom[...] = momf[...].astype(BF16)


WIDTHS = (768, 1024)
REGION = 160


def run_steps(targets, sources_of, chunks_of, width_of, dummy, fa, vec, fb, own, out, back, tiles, flips, steps, owner, filled):
    for c in range(len(WIDTHS)):
        filled[c] = 0
    for b in targets:
        count_b = width_of(b)
        kind = jnp.int32(0)
        for width in WIDTHS[:-1]:
            kind = kind + (count_b > width).astype(jnp.int32)
        base = kind * REGION
        at = base + filled[kind]
        for s in sources_of(b):
            for c in range(8):
                steps[at + c] = s * 8 + c
            for c in range(5):
                owner[(at >> 1) + c] = b
            at = at + chunks_of(s)
        steps[at] = dummy * 8
        at = at + (at & 1)
        filled[kind] = at - base
    for c in range(len(WIDTHS)):
        end = c * REGION + filled[c]
        for extra in range(8):
            steps[end + extra] = dummy * 8
            owner[(end + extra) >> 1] = targets[0]

    def columns(index):
        return pl.ds(pl.multiple_of((index & 7) * CHUNK, CHUNK), CHUNK)

    def flip(t, slot):
        for h in range(2):
            index = steps[2 * t + h]
            flips[slot, h * CHUNK:(h + 1) * CHUNK, :] = fa[index >> 3, :, columns(index)].T

    def make(t, slot, width):
        target = fb[owner[t], :, 0:width]
        squares = jnp.dot(flips[slot], target, preferred_element_type=F32)
        tiles[slot, :, 0:width] = lax.rsqrt(squares).astype(BF16)

    def use(t, slot, width):
        b = owner[t]
        first = steps[2 * t]
        second = steps[2 * t + 1]
        tile = tiles[slot, :, 0:width]
        both = jnp.concatenate([vec[first >> 3, 0:32, columns(first)], vec[second >> 3, 0:32, columns(second)]], axis=1)
        out[b, :, 0:width] += jnp.dot(both, tile, preferred_element_type=F32)
        if back is not None:
            sent = lax.dot_general(own[b, 0:32, 0:width], tile, (((1,), (1,)), ((), ())), preferred_element_type=F32)
            back[first >> 3, :, columns(first)] += sent[:, 0:CHUNK]
            back[second >> 3, :, columns(second)] += sent[:, CHUNK:]

    def begin(c):
        if c < len(WIDTHS):
            flip(c * (REGION // 2), 2 * c)
            flip(c * (REGION // 2) + 1, 2 * c + 1)
            make(c * (REGION // 2), 2 * c, WIDTHS[c])

    begin(0)
    for c, width in enumerate(WIDTHS):
        first_step = c * (REGION // 2)
        total = filled[c] >> 1
        even, odd = 2 * c, 2 * c + 1

        def body(k, carry, first_step=first_step, width=width, even=even, odd=odd):
            t = first_step + 2 * k
            make(t + 1, odd, width)
            flip(t + 2, even)
            use(t, even, width)
            make(t + 2, even, width)
            flip(t + 3, odd)
            use(t + 1, odd, width)
            return carry

        whole = jnp.maximum(total - 1, 0) >> 1
        lax.fori_loop(0, whole, body, 0)
        last = first_step + 2 * whole
        left = total - 2 * whole

        if c + 1 < len(WIDTHS):
            @pl.when(left == 0)
            def _(c=c):
                begin(c + 1)

        @pl.when(left == 1)
        def _(c=c, last=last, width=width, even=even):
            use(last, even, width)
            begin(c + 1)

        @pl.when(left == 2)
        def _(c=c, last=last, width=width, even=even, odd=odd):
            make(last + 1, odd, width)
            use(last, even, width)
            begin(c + 1)
            use(last + 1, odd, width)


INNER = {4: (0,), 2: (0,), 1: (0,), 6: (2, 4), 5: (1, 4), 3: (1, 2), 7: (3, 5, 6)}


def count_of(counts, k):
    return counts[k // 4, k // 2 % 2, k % 2]


def inner_kernel(targets, sources_of, two_way, counts, fa, pay, fb, acc_in, after, out, done, tiles, flips, steps, owner, filled):
    if acc_in is None:
        out[...] = jnp.zeros_like(out)
    else:
        out[...] = acc_in[...]
    run_steps(
        targets, sources_of, lambda s: (count_of(counts, s) + CHUNK - 1) >> 7, lambda b: count_of(counts, b), BOXES,
        fa, pay, fb, pay, out, out if two_way else None, tiles, flips, steps, owner, filled,
    )
    done[...] = jnp.zeros_like(done)


def outer_kernel(counts, fb, pay, acc_self, acc_in, after, halo0, halo1, halo2, near, b0, b1, b2, probe_sums,
                 fa, vec, plus, back, tiles, flips, steps, owner, filled, chunk_no):
    halos = (halo0, halo1, halo2)
    points = fb.shape[-1]
    row = row_ids(points)
    plus[...] = jnp.zeros_like(plus)
    back[...] = jnp.zeros_like(back)
    sources = {b: [] for b in range(BOXES)}
    spare = 12
    for axis in range(3):
        halo = halos[axis]
        name = ("gx", "gy", "gz")[axis]
        at_edge = lax.axis_index(name) == lax.axis_size(name) - 1
        targets = face_boxes(axis, 1)
        for i in range(4):
            s = axis * 4 + i
            sources[targets[i]].append(s)
            tail = halo[i, 32:48, :].astype(F32)
            rows_a = tail[0:8]
            pos = rows_a + pltpu.roll(rows_a, 5, 0) + tail[8:16]
            pos = jnp.where(row < 3, pos + jnp.where(row == axis, 2.0, 0.0), 0.0)
            feats = source_rows(pos, row)
            fa[s] = feats
            if s == 0:
                fa[spare] = feats
            vec[s] = halo[i, 0:32, :]
            chunk_no[s] = jnp.where(at_edge, 0, jnp.max(rows_a[6:7, 0:128]).astype(jnp.int32))
    vec[spare] = jnp.zeros_like(vec[spare])
    order = [b for b in range(BOXES) if sources[b]]
    run_steps(
        order, lambda b: sources[b], lambda s: chunk_no[s], lambda b: count_of(counts, b), spare,
        fa, vec, fb, pay, plus, back, tiles, flips, steps, owner, filled,
    )
    total = jnp.zeros((32, 128), F32)
    for b in range(BOXES):
        extra = plus[b]
        base = acc_self[b] + acc_in[b]
        near[b] = base + extra
        weighted = pay[b, 0:32, :].astype(F32) * (base + 2.0 * extra)
        for j in range(points // 128):
            total = total + weighted[:, j * 128:(j + 1) * 128]
    probe_sums[...] = total
    for axis, ref in enumerate((b0, b1, b2)):
        ref[...] = back[4 * axis:4 * axis + 4]


def local_kernel(counts, req_box, req_tgt, here, there, momf, probe_sums, loc, sums, far_acc, live):
    my_y = lax.axis_index("gy")
    my_z = lax.axis_index("gz")
    far_acc[...] = jnp.zeros_like(far_acc)

    def keep(i, n):
        live[n] = i
        return n + (req_box[i >> 6, i & 63] >= 0).astype(jnp.int32)

    used = lax.fori_loop(0, 128, keep, jnp.int32(0), unroll=16)
    shape = (64, 64)
    source_q = lax.broadcasted_iota(jnp.int32, shape, 1)
    target_q = lax.broadcasted_iota(jnp.int32, shape, 0)

    def node(index):
        value = jnp.full(shape, 0.5 + 0.5 * NODES[0], F32)
        for a in range(1, ORDER):
            value = jnp.where(index == a, 0.5 + 0.5 * NODES[a], value)
        return value

    gaps = [node((source_q >> s) & 3) - node((target_q >> s) & 3) for s in (4, 2, 0)]
    group = lax.broadcasted_iota(jnp.int32, (64, 256), 1) >> 5

    def step(g, carry):
        for u in range(8):
            k = g * 8 + u
            i = live[jnp.minimum(k, used - 1)]
            peer = i & 63
            box = req_box[i >> 6, peer]
            tgt = req_tgt[i >> 6, peer]
            peer_y = peer >> 4
            peer_z = peer & 15
            dx = (box >> 2) - (tgt >> 2)
            dy = (peer_y - my_y) * 2 + ((box >> 1) & 1) - ((tgt >> 1) & 1)
            dz = (peer_z - my_z) * 2 + (box & 1) - (tgt & 1)
            ex = gaps[0] + dx.astype(F32)
            ey = gaps[1] + dy.astype(F32)
            ez = gaps[2] + dz.astype(F32)
            coupling = lax.rsqrt(1.0 + ex * ex + ey * ey + ez * ez).astype(BF16)
            rel_y = peer_y ^ my_y
            rel_z = peer_z ^ my_z
            at = ((rel_z >> 1) & 3) * 8 + rel_y * 2 + (rel_z >> 3)
            block = jnp.where((rel_z & 1) == 0, here[at], there[at])
            term = jnp.dot(coupling, block, preferred_element_type=F32)
            wanted = jnp.where(k < used, box, -1)
            far_acc[tgt] += jnp.where(group == wanted, term, 0.0)
        return carry

    lax.fori_loop(0, (used + 7) >> 3, step, 0)
    lane = lax.broadcasted_iota(jnp.int32, (64, 128), 1)
    far_sums = jnp.zeros((64, 128), F32)
    live_points = jnp.int32(0)
    for b in range(BOXES):
        wide = far_acc[b]
        half = wide[:, 0:128] + wide[:, 128:256]
        half = half + pltpu.roll(half, 64, 1)
        half = half + pltpu.roll(half, 32, 1)
        rounded = half.astype(BF16)
        loc[b] = rounded
        moment = momf[:, (b // 4) * 128:(b // 4 + 1) * 128]
        far_sums = far_sums + jnp.where((lane >> 5) == b % 4, rounded.astype(F32) * moment, 0.0)
        live_points = live_points + count_of(counts, b)
    folded = jnp.sum(far_sums, axis=0, keepdims=True)
    folded = folded + pltpu.roll(folded, 64, 1)
    folded = folded + pltpu.roll(folded, 32, 1)
    lane32 = lax.broadcasted_iota(jnp.int32, (32, 128), 1)
    row32 = lax.broadcasted_iota(jnp.int32, (32, 128), 0)
    per_probe = jnp.sum(probe_sums[...], axis=1, keepdims=True)
    flat = jnp.sum(jnp.where(lane32 == row32, per_probe, 0.0), axis=0, keepdims=True)
    row_sums = jnp.where(lane32[0:1] < 32, flat + folded, jnp.where(lane32[0:1] == 32, live_points.astype(F32), 0.0))
    sums[...] = jnp.broadcast_to(row_sums.reshape(1, 1, 128), sums.shape)


def total_kernel(counts, near, r2, r0, r1, loc, tab, kv, done):
    points = tab.shape[-1]
    lane = lax.broadcasted_iota(jnp.int32, (1, points), 1)
    for b in range(BOXES):
        place = (b // 4, b // 2 % 2, b % 2)
        far = lax.dot_general(loc[b][:, 0:32], tab[b], (((0,), (0,)), ((), ())), preferred_element_type=F32)
        total = near[b] + far
        for axis, ref in enumerate((r0, r1, r2)):
            if place[axis] == 0:
                other = [d for d in range(3) if d != axis]
                total = total + ref[place[other[0]] * 2 + place[other[1]]]
        if b == 0:
            done[...] = jnp.zeros_like(done)
        kv[b] = jnp.where(lane < count_of(counts, b), total * (1.0 / math.sqrt(7.0 * points)), 0.0).astype(BF16)


def quad_kernel(gathered, after, quad):
    lane = lax.broadcasted_iota(jnp.int32, (1, 128), 1)
    whole = jnp.sum(gathered[...], axis=0)
    live_points = jnp.sum(jnp.where(lane == 32, whole, 0.0), axis=1, keepdims=True)
    scaled = whole * (1.0 / math.sqrt(7.0 * 1024)) / live_points
    quad[...] = scaled[0, 0:32]


VMEM = pl.BlockSpec(memory_space=pltpu.VMEM)
SMEM = pl.BlockSpec(memory_space=pltpu.SMEM)
ANY = pl.BlockSpec(memory_space=pl.ANY)
PARAMS = pltpu.CompilerParams(vmem_limit_bytes=20 * 2**20)


COST = pl.CostEstimate(flops=12 * 10**9, bytes_accessed=4 * 2**20, transcendentals=10**7)


def join(name, *arrays):
    return pl.pallas_call(
        lambda *refs: None,
        out_shape=[jax.ShapeDtypeStruct(a.shape, a.dtype) for a in arrays],
        in_specs=[ANY] * len(arrays),
        out_specs=[ANY] * len(arrays),
        input_output_aliases={i: i for i in range(len(arrays))},
        compiler_params=pltpu.CompilerParams(vmem_limit_bytes=2**20),
        name=name,
    )(*arrays)


def xor_permute(value, axis, bits):
    count = lax.axis_size(axis)
    return lax.ppermute(value, axis, [(i, i ^ bits) for i in range(count)])


def shards(offsets, probes, counts, req_box, req_tgt):
    points = offsets.shape[-1]
    shape = jax.ShapeDtypeStruct
    face = shape((4, ROWS, points), BF16)
    pay, fa, fb, tab, mom, momf, *faces = pl.pallas_call(
        prep_kernel,
        out_shape=[
            shape((BOXES + 1, ROWS, points), BF16),
            shape((BOXES + 1, FEATS, points), BF16),
            shape((BOXES, FEATS, points), BF16),
            shape((BOXES, 64, points), BF16),
            shape((64, 256), BF16),
            shape((64, 256), F32),
        ] + [face] * 3,
        in_specs=[SMEM, VMEM, VMEM],
        out_specs=[VMEM] * 9,
        scratch_shapes=[
            pltpu.VMEM((8, points), F32),
        ],
        compiler_params=PARAMS,
        name="prep",
    )(counts, jnp.swapaxes(offsets, 2, 3), probes)

    acc_shape = shape((BOXES, 32, points), F32)
    lists = [
        pltpu.VMEM((2 * len(WIDTHS), 2 * CHUNK, points), BF16),
        pltpu.VMEM((2 * len(WIDTHS), 2 * CHUNK, FEATS), BF16),
        pltpu.SMEM((len(WIDTHS) * REGION,), jnp.int32),
        pltpu.SMEM((len(WIDTHS) * REGION // 2,), jnp.int32),
        pltpu.SMEM((8,), jnp.int32),
    ]

    def inner(name, targets, sources_of, two_way, acc, after):
        has_acc = acc is not None

        def kernel(*refs):
            refs = list(refs)
            head = refs[:4]
            rest = refs[4:]
            acc_ref = rest.pop(0) if has_acc else None
            inner_kernel(targets, sources_of, two_way, *head, acc_ref, *rest)

        args = [counts, fa, pay, fb] + ([acc] if has_acc else []) + [after]
        return pl.pallas_call(
            kernel,
            out_shape=[shape((BOXES + 1, 32, points), F32), shape((8, 128), F32)],
            in_specs=[SMEM, VMEM, VMEM, VMEM] + [VMEM] * has_acc + [ANY],
            out_specs=[VMEM, VMEM],
            scratch_shapes=lists,
            compiler_params=PARAMS,
            cost_estimate=COST,
            name=name,
        )(*args)

    def along(axis, value, step):
        name = ("gx", "gy", "gz")[axis]
        size = lax.axis_size(name)
        return lax.ppermute(value, name, [(i, (i + step) % size) for i in range(size)])

    block = mom.reshape(1, 64, 256)
    twin = xor_permute(block, "gz", 8)
    got = [None] * 3
    got[2] = along(2, faces[2], -1)
    acc_self, tick = inner("self_tiles", list(range(BOXES)), lambda b: [b], False, None, mom)
    tick, twin, face_x = join("join_first", tick, twin, faces[0])
    block = jnp.concatenate([block, twin], axis=0)
    more = [xor_permute(block, "gy", k) for k in (1, 2, 3)]
    got[0] = along(0, face_x, -1)
    acc, tick = inner("pairs_low", [1, 2, 4, 3], lambda b: INNER[b], True, None, tick)
    tick, got[2], face_y, *more = join("join_second", tick, got[2], faces[1], *more)
    block = jnp.concatenate([block] + more, axis=0)
    more = [xor_permute(block, "gz", 2 * k) for k in (1, 2, 3)]
    got[1] = along(1, face_y, -1)
    acc, tick = inner("pairs_high", [5, 6, 7], lambda b: INNER[b], True, acc, tick)
    tick, got[0], got[1], *more = join("join_third", tick, got[0], got[1], *more)
    block = jnp.concatenate([block] + more, axis=0)
    other = xor_permute(block, "gz", 1)
    near, *backs, probe_sums = pl.pallas_call(
        outer_kernel,
        out_shape=[acc_shape] + [shape((4, 32, points), F32)] * 3 + [shape((32, 128), F32)],
        in_specs=[SMEM, VMEM, VMEM, VMEM, VMEM, ANY, VMEM, VMEM, VMEM],
        out_specs=[VMEM] * 5,
        scratch_shapes=[
            pltpu.VMEM((13, FEATS, points), BF16),
            pltpu.VMEM((13, 32, points), BF16),
            pltpu.VMEM((BOXES, 32, points), F32),
            pltpu.VMEM((13, 32, points), F32),
        ] + lists + [pltpu.SMEM((16,), jnp.int32)],
        compiler_params=PARAMS,
        cost_estimate=COST,
        name="face_tiles",
    )(counts, fb, pay, acc_self, acc, tick, *got)
    returned = [None] * 3
    for axis in (2, 0, 1):
        returned[axis] = along(axis, backs[axis], 1)
    devices = lax.axis_size("gx") * lax.axis_size("gy") * lax.axis_size("gz")
    loc, sums = pl.pallas_call(
        local_kernel,
        out_shape=[shape((BOXES, 64, 128), BF16), shape((devices, 1, 128), F32)],
        in_specs=[SMEM, SMEM, SMEM, VMEM, VMEM, VMEM, VMEM],
        out_specs=[VMEM, VMEM],
        scratch_shapes=[
            pltpu.VMEM((BOXES, 64, 256), F32),
            pltpu.SMEM((136,), jnp.int32),
        ],
        compiler_params=PARAMS,
        name="locals",
    )(counts, *[jnp.swapaxes(r, 3, 4).reshape(2, 64) for r in (req_box, req_tgt)], block, other, momf, probe_sums)
    gathered = lax.all_to_all(sums, ("gx", "gy", "gz"), 0, 0, tiled=True)
    kv, total_tick = pl.pallas_call(
        total_kernel,
        out_shape=[shape((BOXES, 32, points), BF16), shape((8, 128), F32)],
        in_specs=[SMEM] + [VMEM] * 6,
        out_specs=[VMEM, VMEM],
        compiler_params=PARAMS,
        cost_estimate=COST,
        name="total",
    )(counts, near, returned[2], returned[0], returned[1], loc, tab)
    quad = pl.pallas_call(
        quad_kernel,
        out_shape=shape((32,), F32),
        in_specs=[VMEM, ANY],
        out_specs=VMEM,
        compiler_params=pltpu.CompilerParams(vmem_limit_bytes=2**21),
        name="quad",
    )(gathered, total_tick)
    return kv.reshape(probes.shape), quad


def solution(mesh):
    placed = (
        P("gx", "gy", "gz", None, None),
        P("gx", "gy", "gz", None, None),
        P("gx", "gy", "gz"),
        P("gx", "gy", "gz", None, None),
        P("gx", "gy", "gz", None, None),
    )
    return jax.shard_map(
        shards,
        mesh=mesh,
        in_specs=placed,
        out_specs=(P("gx", "gy", "gz", None, None), P()),
        check_vma=False,
    )
```

```python
import functools
import math

import jax
import jax.numpy as jnp
from jax import lax
from jax.experimental import pallas as pl
from jax.experimental.pallas import tpu as pltpu
from jax.sharding import PartitionSpec as P

ORDER = 4
CHUNK = 128
BOXES = 8
FEATS = 48
ROWS = 48
F32 = jnp.float32
BF16 = jnp.bfloat16
NODES = [math.cos((2.0 * a + 1.0) * math.pi / (2.0 * ORDER)) for a in range(ORDER)]


def box_id(axis, at, first, second):
    place = [0, 0, 0]
    rest = [d for d in range(3) if d != axis]
    place[axis] = at
    place[rest[0]] = first
    place[rest[1]] = second
    return (place[0] * 2 + place[1]) * 2 + place[2]


def face_boxes(axis, at):
    return [box_id(axis, at, i, j) for i in range(2) for j in range(2)]


def split3(value):
    high = value.astype(BF16).astype(F32)
    rest = value - high
    mid = rest.astype(BF16).astype(F32)
    return high, mid, rest - mid


def row_ids(points):
    return lax.broadcasted_iota(jnp.int32, (8, points), 0)


def source_rows(pos, row):
    p1, p2, p3 = split3(pos)
    n1, n2, n3 = split3(1.0 + jnp.sum(pos * pos, axis=0, keepdims=True))
    s1 = jnp.where(row < 3, p1, jnp.where(row == 3, n1, jnp.where(row == 4, n2, jnp.where(row == 5, n3, 1.0))))
    s2 = p2 + pltpu.roll(p3, 3, 0)
    return jnp.concatenate([s1, s1, s2, s2, s1, jnp.zeros_like(s1)], axis=0).astype(BF16)


def target_rows(pos, row):
    p1, p2, p3 = split3(-2.0 * pos)
    m1, m2, m3 = split3(jnp.sum(pos * pos, axis=0, keepdims=True))
    qa = jnp.where(row < 3, p1, jnp.where(row < 6, 1.0, jnp.where(row == 6, m1, m2)))
    qb = jnp.where(row < 3, p2, jnp.where(row == 6, m3, 0.0))
    qc = p1 + pltpu.roll(p1, 3, 0)
    return jnp.concatenate([qa, qb, qc, p2, p3, jnp.zeros_like(qa)], axis=0).astype(BF16)


def prep_kernel(counts, offs, probes, pay, fa, fb, tab, mom, momf, f0, f1, f2, pad):
    points = offs.shape[-1]
    row = row_ids(points)
    lane = lax.broadcasted_iota(jnp.int32, (1, points), 1)
    faces = (f0, f1, f2)
    pay[BOXES] = jnp.zeros_like(pay[BOXES])
    for k in range(BOXES):
        place = (k // 4, k // 2 % 2, k % 2)
        pad[...] = jnp.zeros_like(pad)
        for d in range(3):
            pad[d:d + 1, :] = offs[place[0], place[1], d, place[2]:place[2] + 1, :]
        off = pad[...]
        shift = jnp.where(row == 0, place[0] - 1.0, jnp.where(row == 1, place[1] - 1.0, jnp.where(row == 2, place[2] - 1.0, 0.0)))
        pos = off + shift
        src = source_rows(pos, row)
        fa[k] = src
        fb[k] = target_rows(pos, row)
        if k == 0:
            fa[BOXES] = src
        count = counts[place]
        chunks = ((count + CHUNK - 1) // CHUNK).astype(F32)
        p1, p2, p3 = split3(pos)
        rows_a = jnp.where(row == 6, chunks, p1 + pltpu.roll(p2, 3, 0))
        tail = jnp.concatenate([rows_a, p3], axis=0).astype(BF16)
        vec = jnp.where(lane < count, probes[place].astype(F32), 0.0).astype(BF16)
        pay[k, 0:32, :] = vec
        pay[k, 32:48, :] = tail
        for axis in range(3):
            if place[axis] == 0:
                other = [d for d in range(3) if d != axis]
                slot = place[other[0]] * 2 + place[other[1]]
                faces[axis][slot, 0:32, :] = vec
                faces[axis][slot, 32:48, :] = tail
        unit = 2.0 * off - 1.0
        t2 = 2.0 * unit * unit - 1.0
        t3 = 2.0 * unit * t2 - unit
        weights = []
        for c in NODES:
            e2 = 2.0 * c * c - 1.0
            e3 = 2.0 * c * e2 - c
            weights.append(0.25 + 0.5 * (c * unit + e2 * t2 + e3 * t3))
        third = jnp.zeros_like(off)
        for d in range(ORDER):
            third = jnp.where(row % 4 == d, weights[d][2:3, :], third)
        seconds = []
        for half in range(2):
            seconds.append(jnp.where(row < 4, weights[2 * half][1:2, :], weights[2 * half + 1][1:2, :]))
        parts = []
        for a in range(ORDER):
            for half in range(2):
                parts.append(weights[a][0:1, :] * seconds[half] * third)
        table = jnp.concatenate(parts, axis=0).astype(BF16)
        tab[k] = table
        moment = lax.dot_general(table, vec, (((1,), (1,)), ((), ())), preferred_element_type=F32)
        momf[:, k * 32:(k + 1) * 32] = moment
    mom[...] = momf[...].astype(BF16)


WIDTHS = (768, 1024)
REGION = 160


def run_steps(targets, sources_of, chunks_of, width_of, dummy, fa, vec, fb, own, out, back, tiles, flips, steps, owner, filled):
    for c in range(len(WIDTHS)):
        filled[c] = 0
    for b in targets:
        count_b = width_of(b)
        kind = jnp.int32(0)
        for width in WIDTHS[:-1]:
            kind = kind + (count_b > width).astype(jnp.int32)
        base = kind * REGION
        at = base + filled[kind]
        for s in sources_of(b):
            for c in range(8):
                steps[at + c] = s * 8 + c
            for c in range(5):
                owner[(at >> 1) + c] = b
            at = at + chunks_of(s)
        steps[at] = dummy * 8
        at = at + (at & 1)
        filled[kind] = at - base
    for c in range(len(WIDTHS)):
        end = c * REGION + filled[c]
        for extra in range(8):
            steps[end + extra] = dummy * 8
            owner[(end + extra) >> 1] = targets[0]

    def columns(index):
        return pl.ds(pl.multiple_of((index & 7) * CHUNK, CHUNK), CHUNK)

    def flip(t, slot):
        for h in range(2):
            index = steps[2 * t + h]
            flips[slot, h * CHUNK:(h + 1) * CHUNK, :] = fa[index >> 3, :, columns(index)].T

    def make(t, slot, width):
        target = fb[owner[t], :, 0:width]
        squares = jnp.dot(flips[slot], target, preferred_element_type=F32)
        tiles[slot, :, 0:width] = lax.rsqrt(squares).astype(BF16)

    def use(t, slot, width):
        b = owner[t]
        first = steps[2 * t]
        second = steps[2 * t + 1]
        tile = tiles[slot, :, 0:width]
        both = jnp.concatenate([vec[first >> 3, 0:32, columns(first)], vec[second >> 3, 0:32, columns(second)]], axis=1)
        out[b, :, 0:width] += jnp.dot(both, tile, preferred_element_type=F32)
        if back is not None:
            sent = lax.dot_general(own[b, 0:32, 0:width], tile, (((1,), (1,)), ((), ())), preferred_element_type=F32)
            back[first >> 3, :, columns(first)] += sent[:, 0:CHUNK]
            back[second >> 3, :, columns(second)] += sent[:, CHUNK:]

    def begin(c):
        if c < len(WIDTHS):
            flip(c * (REGION // 2), 2 * c)
            flip(c * (REGION // 2) + 1, 2 * c + 1)
            make(c * (REGION // 2), 2 * c, WIDTHS[c])

    begin(0)
    for c, width in enumerate(WIDTHS):
        first_step = c * (REGION // 2)
        total = filled[c] >> 1
        even, odd = 2 * c, 2 * c + 1

        def body(k, carry, first_step=first_step, width=width, even=even, odd=odd):
            t = first_step + 2 * k
            make(t + 1, odd, width)
            flip(t + 2, even)
            use(t, even, width)
            make(t + 2, even, width)
            flip(t + 3, odd)
            use(t + 1, odd, width)
            return carry

        whole = jnp.maximum(total - 1, 0) >> 1
        lax.fori_loop(0, whole, body, 0)
        last = first_step + 2 * whole
        left = total - 2 * whole

        if c + 1 < len(WIDTHS):
            @pl.when(left == 0)
            def _(c=c):
                begin(c + 1)

        @pl.when(left == 1)
        def _(c=c, last=last, width=width, even=even):
            use(last, even, width)
            begin(c + 1)

        @pl.when(left == 2)
        def _(c=c, last=last, width=width, even=even, odd=odd):
            make(last + 1, odd, width)
            use(last, even, width)
            begin(c + 1)
            use(last + 1, odd, width)


INNER = {4: (0,), 2: (0,), 1: (0,), 6: (2, 4), 5: (1, 4), 3: (1, 2), 7: (3, 5, 6)}


def count_of(counts, k):
    return counts[k // 4, k // 2 % 2, k % 2]


def inner_kernel(targets, sources_of, two_way, counts, fa, pay, fb, acc_in, after, out, done, tiles, flips, steps, owner, filled):
    if acc_in is None:
        out[...] = jnp.zeros_like(out)
    else:
        out[...] = acc_in[...]
    run_steps(
        targets, sources_of, lambda s: (count_of(counts, s) + CHUNK - 1) >> 7, lambda b: count_of(counts, b), BOXES,
        fa, pay, fb, pay, out, out if two_way else None, tiles, flips, steps, owner, filled,
    )
    done[...] = jnp.zeros_like(done)


def outer_kernel(counts, fb, pay, acc_self, acc_in, after, halo0, halo1, halo2, near, b0, b1, b2, probe_sums,
                 fa, vec, plus, back, tiles, flips, steps, owner, filled, chunk_no):
    halos = (halo0, halo1, halo2)
    points = fb.shape[-1]
    row = row_ids(points)
    plus[...] = jnp.zeros_like(plus)
    back[...] = jnp.zeros_like(back)
    sources = {b: [] for b in range(BOXES)}
    spare = 12
    for axis in range(3):
        halo = halos[axis]
        name = ("gx", "gy", "gz")[axis]
        at_edge = lax.axis_index(name) == lax.axis_size(name) - 1
        targets = face_boxes(axis, 1)
        for i in range(4):
            s = axis * 4 + i
            sources[targets[i]].append(s)
            tail = halo[i, 32:48, :].astype(F32)
            rows_a = tail[0:8]
            pos = rows_a + pltpu.roll(rows_a, 5, 0) + tail[8:16]
            pos = jnp.where(row < 3, pos + jnp.where(row == axis, 2.0, 0.0), 0.0)
            feats = source_rows(pos, row)
            fa[s] = feats
            if s == 0:
                fa[spare] = feats
            vec[s] = halo[i, 0:32, :]
            chunk_no[s] = jnp.where(at_edge, 0, jnp.max(rows_a[6:7, 0:128]).astype(jnp.int32))
    vec[spare] = jnp.zeros_like(vec[spare])
    order = [b for b in range(BOXES) if sources[b]]
    run_steps(
        order, lambda b: sources[b], lambda s: chunk_no[s], lambda b: count_of(counts, b), spare,
        fa, vec, fb, pay, plus, back, tiles, flips, steps, owner, filled,
    )
    total = jnp.zeros((32, 128), F32)
    for b in range(BOXES):
        extra = plus[b]
        base = acc_self[b] + acc_in[b]
        near[b] = base + extra
        weighted = pay[b, 0:32, :].astype(F32) * (base + 2.0 * extra)
        for j in range(points // 128):
            total = total + weighted[:, j * 128:(j + 1) * 128]
    probe_sums[...] = total
    for axis, ref in enumerate((b0, b1, b2)):
        ref[...] = back[4 * axis:4 * axis + 4]


def local_kernel(counts, req_box, req_tgt, here, there, momf, probe_sums, loc, sums, far_acc, live):
    my_y = lax.axis_index("gy")
    my_z = lax.axis_index("gz")
    far_acc[...] = jnp.zeros_like(far_acc)

    def keep(i, n):
        live[n] = i
        return n + (req_box[i >> 6, i & 63] >= 0).astype(jnp.int32)

    used = lax.fori_loop(0, 128, keep, jnp.int32(0), unroll=16)
    shape = (64, 64)
    source_q = lax.broadcasted_iota(jnp.int32, shape, 1)
    target_q = lax.broadcasted_iota(jnp.int32, shape, 0)

    def node(index):
        value = jnp.full(shape, 0.5 + 0.5 * NODES[0], F32)
        for a in range(1, ORDER):
            value = jnp.where(index == a, 0.5 + 0.5 * NODES[a], value)
        return value

    gaps = [node((source_q >> s) & 3) - node((target_q >> s) & 3) for s in (4, 2, 0)]
    group = lax.broadcasted_iota(jnp.int32, (64, 256), 1) >> 5

    def step(g, carry):
        for u in range(16):
            k = g * 16 + u
            i = live[jnp.minimum(k, used - 1)]
            peer = i & 63
            box = req_box[i >> 6, peer]
            tgt = req_tgt[i >> 6, peer]
            peer_y = peer >> 4
            peer_z = peer & 15
            dx = (box >> 2) - (tgt >> 2)
            dy = (peer_y - my_y) * 2 + ((box >> 1) & 1) - ((tgt >> 1) & 1)
            dz = (peer_z - my_z) * 2 + (box & 1) - (tgt & 1)
            ex = gaps[0] + dx.astype(F32)
            ey = gaps[1] + dy.astype(F32)
            ez = gaps[2] + dz.astype(F32)
            coupling = lax.rsqrt(1.0 + ex * ex + ey * ey + ez * ez).astype(BF16)
            rel_y = peer_y ^ my_y
            rel_z = peer_z ^ my_z
            at = ((rel_z >> 1) & 3) * 8 + rel_y * 2 + (rel_z >> 3)
            block = jnp.where((rel_z & 1) == 0, here[at], there[at])
            term = jnp.dot(coupling, block, preferred_element_type=F32)
            wanted = jnp.where(k < used, box, -1)
            far_acc[tgt] += jnp.where(group == wanted, term, 0.0)
        return carry

    lax.fori_loop(0, (used + 15) >> 4, step, 0)
    lane = lax.broadcasted_iota(jnp.int32, (64, 128), 1)
    far_sums = jnp.zeros((64, 128), F32)
    live_points = jnp.int32(0)
    for b in range(BOXES):
        wide = far_acc[b]
        half = wide[:, 0:128] + wide[:, 128:256]
        half = half + pltpu.roll(half, 64, 1)
        half = half + pltpu.roll(half, 32, 1)
        rounded = half.astype(BF16)
        loc[b] = rounded
        moment = momf[:, (b // 4) * 128:(b // 4 + 1) * 128]
        far_sums = far_sums + jnp.where((lane >> 5) == b % 4, rounded.astype(F32) * moment, 0.0)
        live_points = live_points + count_of(counts, b)
    folded = jnp.sum(far_sums, axis=0, keepdims=True)
    folded = folded + pltpu.roll(folded, 64, 1)
    folded = folded + pltpu.roll(folded, 32, 1)
    lane32 = lax.broadcasted_iota(jnp.int32, (32, 128), 1)
    row32 = lax.broadcasted_iota(jnp.int32, (32, 128), 0)
    per_probe = jnp.sum(probe_sums[...], axis=1, keepdims=True)
    flat = jnp.sum(jnp.where(lane32 == row32, per_probe, 0.0), axis=0, keepdims=True)
    row_sums = jnp.where(lane32[0:1] < 32, flat + folded, jnp.where(lane32[0:1] == 32, live_points.astype(F32), 0.0))
    sums[...] = jnp.broadcast_to(row_sums.reshape(1, 1, 128), sums.shape)


def total_kernel(counts, near, r2, r0, r1, loc, tab, kv, done):
    points = tab.shape[-1]
    lane = lax.broadcasted_iota(jnp.int32, (1, points), 1)
    for b in range(BOXES):
        place = (b // 4, b // 2 % 2, b % 2)
        far = lax.dot_general(loc[b][:, 0:32], tab[b], (((0,), (0,)), ((), ())), preferred_element_type=F32)
        total = near[b] + far
        for axis, ref in enumerate((r0, r1, r2)):
            if place[axis] == 0:
                other = [d for d in range(3) if d != axis]
                total = total + ref[place[other[0]] * 2 + place[other[1]]]
        if b == 0:
            done[...] = jnp.zeros_like(done)
        kv[b] = jnp.where(lane < count_of(counts, b), total * (1.0 / math.sqrt(7.0 * points)), 0.0).astype(BF16)


def quad_kernel(gathered, after, quad):
    lane = lax.broadcasted_iota(jnp.int32, (1, 128), 1)
    whole = jnp.sum(gathered[...], axis=0)
    live_points = jnp.sum(jnp.where(lane == 32, whole, 0.0), axis=1, keepdims=True)
    scaled = whole * (1.0 / math.sqrt(7.0 * 1024)) / live_points
    quad[...] = scaled[0, 0:32]


VMEM = pl.BlockSpec(memory_space=pltpu.VMEM)
SMEM = pl.BlockSpec(memory_space=pltpu.SMEM)
ANY = pl.BlockSpec(memory_space=pl.ANY)
PARAMS = pltpu.CompilerParams(vmem_limit_bytes=20 * 2**20)


COST = pl.CostEstimate(flops=12 * 10**9, bytes_accessed=4 * 2**20, transcendentals=10**7)


def join(name, *arrays):
    return pl.pallas_call(
        lambda *refs: None,
        out_shape=[jax.ShapeDtypeStruct(a.shape, a.dtype) for a in arrays],
        in_specs=[ANY] * len(arrays),
        out_specs=[ANY] * len(arrays),
        input_output_aliases={i: i for i in range(len(arrays))},
        compiler_params=pltpu.CompilerParams(vmem_limit_bytes=2**20),
        name=name,
    )(*arrays)


def xor_permute(value, axis, bits):
    count = lax.axis_size(axis)
    return lax.ppermute(value, axis, [(i, i ^ bits) for i in range(count)])


def shards(offsets, probes, counts, req_box, req_tgt):
    points = offsets.shape[-1]
    shape = jax.ShapeDtypeStruct
    face = shape((4, ROWS, points), BF16)
    pay, fa, fb, tab, mom, momf, *faces = pl.pallas_call(
        prep_kernel,
        out_shape=[
            shape((BOXES + 1, ROWS, points), BF16),
            shape((BOXES + 1, FEATS, points), BF16),
            shape((BOXES, FEATS, points), BF16),
            shape((BOXES, 64, points), BF16),
            shape((64, 256), BF16),
            shape((64, 256), F32),
        ] + [face] * 3,
        in_specs=[SMEM, VMEM, VMEM],
        out_specs=[VMEM] * 9,
        scratch_shapes=[
            pltpu.VMEM((8, points), F32),
        ],
        compiler_params=PARAMS,
        name="prep",
    )(counts, jnp.swapaxes(offsets, 2, 3), probes)

    acc_shape = shape((BOXES, 32, points), F32)
    lists = [
        pltpu.VMEM((2 * len(WIDTHS), 2 * CHUNK, points), BF16),
        pltpu.VMEM((2 * len(WIDTHS), 2 * CHUNK, FEATS), BF16),
        pltpu.SMEM((len(WIDTHS) * REGION,), jnp.int32),
        pltpu.SMEM((len(WIDTHS) * REGION // 2,), jnp.int32),
        pltpu.SMEM((8,), jnp.int32),
    ]

    def inner(name, targets, sources_of, two_way, acc, after):
        has_acc = acc is not None

        def kernel(*refs):
            refs = list(refs)
            head = refs[:4]
            rest = refs[4:]
            acc_ref = rest.pop(0) if has_acc else None
            inner_kernel(targets, sources_of, two_way, *head, acc_ref, *rest)

        args = [counts, fa, pay, fb] + ([acc] if has_acc else []) + [after]
        return pl.pallas_call(
            kernel,
            out_shape=[shape((BOXES + 1, 32, points), F32), shape((8, 128), F32)],
            in_specs=[SMEM, VMEM, VMEM, VMEM] + [VMEM] * has_acc + [ANY],
            out_specs=[VMEM, VMEM],
            scratch_shapes=lists,
            compiler_params=PARAMS,
            cost_estimate=COST,
            name=name,
        )(*args)

    def along(axis, value, step):
        name = ("gx", "gy", "gz")[axis]
        size = lax.axis_size(name)
        return lax.ppermute(value, name, [(i, (i + step) % size) for i in range(size)])

    block = mom.reshape(1, 64, 256)
    twin = xor_permute(block, "gz", 8)
    got = [None] * 3
    got[2] = along(2, faces[2], -1)
    acc_self, tick = inner("self_tiles", list(range(BOXES)), lambda b: [b], False, None, mom)
    tick, twin, face_x = join("join_first", tick, twin, faces[0])
    block = jnp.concatenate([block, twin], axis=0)
    more = [xor_permute(block, "gy", k) for k in (1, 2, 3)]
    got[0] = along(0, face_x, -1)
    acc, tick = inner("pairs_low", [1, 2, 4, 3], lambda b: INNER[b], True, None, tick)
    tick, got[2], face_y, *more = join("join_second", tick, got[2], faces[1], *more)
    block = jnp.concatenate([block] + more, axis=0)
    more = [xor_permute(block, "gz", 2 * k) for k in (1, 2, 3)]
    got[1] = along(1, face_y, -1)
    acc, tick = inner("pairs_high", [5, 6, 7], lambda b: INNER[b], True, acc, tick)
    tick, got[0], got[1], *more = join("join_third", tick, got[0], got[1], *more)
    block = jnp.concatenate([block] + more, axis=0)
    other = xor_permute(block, "gz", 1)
    near, *backs, probe_sums = pl.pallas_call(
        outer_kernel,
        out_shape=[acc_shape] + [shape((4, 32, points), F32)] * 3 + [shape((32, 128), F32)],
        in_specs=[SMEM, VMEM, VMEM, VMEM, VMEM, ANY, VMEM, VMEM, VMEM],
        out_specs=[VMEM] * 5,
        scratch_shapes=[
            pltpu.VMEM((13, FEATS, points), BF16),
            pltpu.VMEM((13, 32, points), BF16),
            pltpu.VMEM((BOXES, 32, points), F32),
            pltpu.VMEM((13, 32, points), F32),
        ] + lists + [pltpu.SMEM((16,), jnp.int32)],
        compiler_params=PARAMS,
        cost_estimate=COST,
        name="face_tiles",
    )(counts, fb, pay, acc_self, acc, tick, *got)
    returned = [None] * 3
    for axis in (2, 0, 1):
        returned[axis] = along(axis, backs[axis], 1)
    devices = lax.axis_size("gx") * lax.axis_size("gy") * lax.axis_size("gz")
    loc, sums = pl.pallas_call(
        local_kernel,
        out_shape=[shape((BOXES, 64, 128), BF16), shape((devices, 1, 128), F32)],
        in_specs=[SMEM, SMEM, SMEM, VMEM, VMEM, VMEM, VMEM],
        out_specs=[VMEM, VMEM],
        scratch_shapes=[
            pltpu.VMEM((BOXES, 64, 256), F32),
            pltpu.SMEM((136,), jnp.int32),
        ],
        compiler_params=PARAMS,
        name="locals",
    )(counts, *[jnp.swapaxes(r, 3, 4).reshape(2, 64) for r in (req_box, req_tgt)], block, other, momf, probe_sums)
    gathered = lax.all_to_all(sums, ("gx", "gy", "gz"), 0, 0, tiled=True)
    kv, total_tick = pl.pallas_call(
        total_kernel,
        out_shape=[shape((BOXES, 32, points), BF16), shape((8, 128), F32)],
        in_specs=[SMEM] + [VMEM] * 6,
        out_specs=[VMEM, VMEM],
        compiler_params=PARAMS,
        cost_estimate=COST,
        name="total",
    )(counts, near, returned[2], returned[0], returned[1], loc, tab)
    quad = pl.pallas_call(
        quad_kernel,
        out_shape=shape((32,), F32),
        in_specs=[VMEM, ANY],
        out_specs=VMEM,
        compiler_params=pltpu.CompilerParams(vmem_limit_bytes=2**21),
        name="quad",
    )(gathered, total_tick)
    return kv.reshape(probes.shape), quad


def solution(mesh):
    placed = (
        P("gx", "gy", "gz", None, None),
        P("gx", "gy", "gz", None, None),
        P("gx", "gy", "gz"),
        P("gx", "gy", "gz", None, None),
        P("gx", "gy", "gz", None, None),
    )
    return jax.shard_map(
        shards,
        mesh=mesh,
        in_specs=placed,
        out_specs=(P("gx", "gy", "gz", None, None), P()),
        check_vma=False,
    )
```
